32 devices in a mesh: dp: 4 (over y, x), mp: 8 (over z, core).
Axes of the slice: x: 2, y: 2, z: 4, core: 2. Of those that a mesh axis runs over, the one named last changes fastest.
Arguments:
- x_in: bfloat16 [16384, 2048], P(('dp', 'mp')), may hold values from -6 to 6
- seq_lengths: int32 [4, 4], P('dp'), may hold values from 1 to 3585, as said below
- norm1_gain: bfloat16 [2048], P(('dp', 'mp')), may hold values from 0.5 to 1.5
- w_query: bfloat16 [2048, 256], P(('dp', 'mp')), may hold values from -0.125 to 0.125
- w_key: bfloat16 [2048, 256], P(('dp', 'mp')), may hold values from -0.125 to 0.125
- w_value: bfloat16 [2048, 2048], P(('dp', 'mp')), may hold values from -0.125 to 0.125
- w_out: bfloat16 [2048, 2048], P(('dp', 'mp')), may hold values from -4 to 4
- norm2_gain: bfloat16 [2048], P(('dp', 'mp')), may hold values from 0.5 to 1.5
- w_gate: bfloat16 [2048, 5632], P(None, 'mp'), may hold values from -0.125 to 0.125
- w_up: bfloat16 [2048, 5632], P(None, 'mp'), may hold values from -0.125 to 0.125
- w_down: bfloat16 [5632, 2048], P('mp'), may hold values from -0.078125 to 0.078125
- cotangent: bfloat16 [16384, 2048], P(('dp', 'mp')), may hold values from -6 to 6
Outputs:
- output: bfloat16 [16384, 2048], P(('dp', 'mp'))
- input_grad: bfloat16 [16384, 2048], P(('dp', 'mp'))
- norm1_gain_grad: float32 [2048], P(('dp', 'mp'))
- w_query_grad: float32 [2048, 256], P(('dp', 'mp'))
- w_key_grad: float32 [2048, 256], P(('dp', 'mp'))
- w_value_grad: float32 [2048, 2048], P(('dp', 'mp'))
- w_out_grad: float32 [2048, 2048], P(('dp', 'mp'))
- norm2_gain_grad: float32 [2048], P(('dp', 'mp'))
- w_gate_grad: float32 [2048, 5632], P(None, 'mp')
- w_up_grad: float32 [2048, 5632], P(None, 'mp')
- w_down_grad: float32 [5632, 2048], P('mp')
The draws below stay inside these ranges and needn't reach their ends.
Inputs may be any that keep to these rules, and one draw needn't show every extreme that they name: `seq_lengths`: in every group one sequence, which one is drawn, has exactly 3585 tokens; every other sequence has at most 128; the other sequences and the padding after the last sequence together take fewer than 512 positions.
All inputs are finite; a program needn't handle non-finite values.
Results may differ from the reference program's by a relative error of at most 0.02.
Values may be sent and summed in bfloat16 or wider, within the bound.
No kernel may reach another device: no remote copies, remote signals or barrier semaphores. Data moves between devices by JAX's collectives and lax.ppermute only.
A program may use at most 768 MiB of HBM per device.

```python
import jax
import jax.numpy as jnp
from jax import lax

D = 2048
HEADS = 16
FEAT = 16
FF = 5632
FEATS = 273
HEAD_V = 128
TOK_DEV = 512
SEQS = 4
TOKENS = 16384
N_DP = 4
N_MP = 8


def draw_seq_lengths(key, part):
    key = jax.random.fold_in(key, 11)
    key_short, key_long = jax.random.split(key, 2)
    short_most = TOK_DEV // SEQS
    short_lengths = jax.random.randint(key_short, (N_DP, SEQS), 1, short_most + 1)
    longest = jax.random.randint(key_long, (N_DP, 1), 0, SEQS)
    column = jnp.arange(SEQS)[None, :]
    long_length = TOK_DEV * N_MP - SEQS * short_most + 1
    return jnp.where(column == longest, long_length, short_lengths).astype(jnp.int32)


def block_scale(rng, extent, cuts, low, largest):
    def one(axis_at, blocks):
        draws = jax.random.uniform(jax.random.fold_in(jax.random.fold_in(rng, 6), axis_at), (blocks,), jnp.float32, low / len(cuts), largest / len(cuts))
        return jnp.repeat(jnp.exp(draws), extent[axis_at] // blocks).reshape((-1,) + (1,) * (len(extent) - axis_at - 1))

    factor_of = one(*cuts[0])
    for cut in cuts[1:]:
        factor_of = factor_of * one(*cut)
    return factor_of


def centred(stream_key, shape, scale, reach, cuts=(), held_as=jnp.bfloat16):
    values = scale * jax.random.normal(stream_key, shape, jnp.float32)
    if cuts:
        values = values * block_scale(stream_key, shape, cuts, -0.22, 0.18)
    return jnp.clip(values, -reach, reach).astype(held_as)


def setup_inputs(seed: int = 0) -> dict:
    splits = jax.random.split(jax.random.key(seed), 13)
    return {
        "x_in": centred(splits[0], (TOKENS, D), 1.0, 6.0, ((0, 32),)),
        "seq_lengths": draw_seq_lengths(jax.random.fold_in(splits[12], 71), 0),
        "norm1_gain": jnp.clip(1.0 + 0.1 * jax.random.normal(splits[2], (D,), jnp.float32), 0.5, 1.5).astype(jnp.bfloat16),
        "w_query": centred(splits[3], (D, HEADS * FEAT), D ** -0.5, 0.125, ((0, 32),)),
        "w_key": centred(splits[4], (D, HEADS * FEAT), D ** -0.5, 0.125, ((0, 32),)),
        "w_value": centred(splits[5], (D, D), D ** -0.5, 0.125, ((0, 32),)),
        "w_out": centred(splits[6], (D, D), (max(1, D * 4 // (TOK_DEV * N_MP))) ** -0.5, 4.0, ((0, 32),)),
        "norm2_gain": jnp.clip(1.0 + 0.1 * jax.random.normal(splits[7], (D,), jnp.float32), 0.5, 1.5).astype(jnp.bfloat16),
        "w_gate": centred(splits[8], (D, FF), D ** -0.5, 0.125, ((1, 8),)),
        "w_up": centred(splits[9], (D, FF), D ** -0.5, 0.125, ((1, 8),)),
        "w_down": centred(splits[10], (FF, D), FF ** -0.5, 0.078125, ((0, 8),)),
        "cotangent": centred(splits[11], (TOKENS, D), 1.0, 6.0, ((0, 32),)),
    }


EPSILON = 1e-05
PRECISE = lax.Precision.HIGHEST

@jax.custom_vjp
def low(v):
    return lax.optimization_barrier(v.astype(jnp.bfloat16)).astype(jnp.float32)

@jax.custom_vjp
def low_back(v):
    return v

def low_keep(v):
    return (low(v), None)

def low_pass(kept, grad):
    return (grad,)

def back_keep(v):
    return (v, None)

def back_low(kept, grad):
    return (low(grad),)
low.defvjp(low_keep, low_pass)
low_back.defvjp(back_keep, back_low)

def matmul_high(left, right):
    return jnp.dot(left, right, precision=PRECISE, preferred_element_type=jnp.float32)

def rms_norm(inputs, gains_in):
    return inputs * lax.rsqrt(lax.optimization_barrier(jnp.mean(inputs * inputs, axis=-1, keepdims=True)) + EPSILON) * gains_in

def taylor_map(scaled):
    row_count, head_count, feat_count = scaled.shape
    square = (scaled[:, :, :, None] * scaled[:, :, None, :]).reshape(row_count, head_count, feat_count * feat_count)
    return jnp.concatenate([jnp.ones((row_count, head_count, 1), jnp.float32), scaled, square * 0.5 ** 0.5], axis=2)

def block_mix(query_heads, key_heads, value_heads, prefix_state, prefix_norm, segments, reading):
    positions = jnp.arange(segments.shape[0], dtype=jnp.int32)
    kernel_dot = jnp.einsum('ihf,jhf->hij', query_heads, key_heads, precision=PRECISE)
    same_doc = ((segments[:, None] == segments[None, :]) & (positions[None, :] <= positions[:, None])).astype(jnp.float32)
    weight = (1.0 + kernel_dot + 0.5 * kernel_dot * kernel_dot) * same_doc[None]
    feat_query = taylor_map(query_heads)
    numerator = jnp.einsum('hij,jhd->ihd', weight, value_heads, precision=PRECISE) + reading[:, None, None] * jnp.einsum('ihe,hed->ihd', feat_query, prefix_state, precision=PRECISE)
    denominator = lax.optimization_barrier(jnp.sum(weight, axis=2)).T + reading[:, None] * jnp.einsum('ihe,he->ih', feat_query, prefix_norm, precision=PRECISE)
    return numerator / denominator[:, :, None]

def block_state(key_heads, value_heads, last_doc):
    feat_key = taylor_map(key_heads) * last_doc[:, None, None]
    return (jnp.einsum('jhe,jhd->hed', feat_key, value_heads, precision=PRECISE), lax.optimization_barrier(jnp.sum(feat_key, axis=0)))

def group_mix(query_heads, key_heads, value_heads, segments):
    blocks = segments.shape[0] // TOK_DEV
    previous = jnp.concatenate([jnp.zeros((1,), jnp.int32), segments[:-1]]).reshape(blocks, TOK_DEV)[:, 0]
    starts = jnp.arange(blocks, dtype=jnp.int32) * TOK_DEV

    def split_rows(array):
        return array.reshape((blocks, TOK_DEV) + array.shape[1:])

    def block_step(carried_in, inputs):
        query_block, key_block, value_block, seg_block, seg_before, row_start = inputs
        opened = row_start > 0
        reading = ((seg_block == seg_before) & opened).astype(jnp.float32)
        mixed_rows = block_mix(query_block, key_block, value_block, carried_in[0], carried_in[1], seg_block, reading)
        last_doc = (seg_block == seg_block[-1]).astype(jnp.float32)
        keep_going = ((seg_block[-1] == seg_before) & opened).astype(jnp.float32)
        own_state, own_norm = block_state(key_block, value_block, last_doc)
        return ((own_state + keep_going * carried_in[0], own_norm + keep_going * carried_in[1]), mixed_rows)
    initial = (jnp.zeros((HEADS, FEATS, HEAD_V), jnp.float32), jnp.zeros((HEADS, FEATS), jnp.float32))
    unused, mixed_rows = lax.scan(jax.checkpoint(block_step), initial, (split_rows(query_heads), split_rows(key_heads), split_rows(value_heads), split_rows(segments), previous, starts))
    return mixed_rows.reshape(query_heads.shape[0], HEADS, HEAD_V)

def group_forward(inputs, segments, weights):
    gain_one, query_w, key_w, value_w, out_w, gain_two, gate_w, up_w, down_w = weights
    feat_scale = FEAT ** (-0.25)
    row_count = inputs.shape[0]
    normed_one = low(rms_norm(inputs, gain_one))
    queries = low_back(low(matmul_high(normed_one, query_w)))
    keys_out = low_back(low(matmul_high(normed_one, key_w)))
    values_out = low_back(low(matmul_high(normed_one, value_w)))
    mixed_rows = group_mix(queries.reshape(row_count, HEADS, FEAT) * feat_scale, keys_out.reshape(row_count, HEADS, FEAT) * feat_scale, values_out.reshape(row_count, HEADS, HEAD_V), segments)
    attended = low_back(low(mixed_rows.reshape(row_count, D)))
    hidden_in = inputs + low_back(matmul_high(attended, out_w))
    normed_two = low(rms_norm(hidden_in, gain_two))
    gate_rows = low_back(matmul_high(normed_two, gate_w))
    up_rows = low_back(matmul_high(normed_two, up_w))
    hidden = low_back(low(jax.nn.silu(gate_rows) * up_rows))
    return hidden_in + low_back(matmul_high(hidden, down_w))

def reference(x_in, seq_lengths, norm1_gain, w_query, w_key, w_value, w_out, norm2_gain, w_gate, w_up, w_down, cotangent):
    group_rows = TOK_DEV * N_MP
    positions = jnp.arange(group_rows, dtype=jnp.int32)
    seq_ends = jnp.cumsum(seq_lengths, axis=1, dtype=jnp.int32)
    segments = lax.optimization_barrier(jnp.sum((positions[None, :, None] >= seq_ends[:, None, :]).astype(jnp.int32), axis=2, dtype=jnp.int32))
    floats = tuple((array.astype(jnp.float32) for array in (x_in, norm1_gain, w_query, w_key, w_value, w_out, norm2_gain, w_gate, w_up, w_down)))

    def forward(inputs, gain_one, query_w, key_w, value_w, out_w, gain_two, gate_w, up_w, down_w):
        weights = (gain_one, query_w, key_w, value_w, out_w, gain_two, gate_w, up_w, down_w)

        def one_group(group_pair):
            return group_forward(group_pair[0], group_pair[1], weights)
        result = lax.map(jax.checkpoint(one_group), (inputs.reshape(N_DP, group_rows, D), segments))
        return result.reshape(N_DP * group_rows, D)
    outputs, pullback = jax.vjp(forward, *floats)
    gradients = pullback(cotangent.astype(jnp.float32))
    return (outputs.astype(jnp.bfloat16), gradients[0].astype(jnp.bfloat16), gradients[1], gradients[2], gradients[3], gradients[4], gradients[5], gradients[6], gradients[7], gradients[8], gradients[9])
```

```python
import functools
import numpy as np
import jax
import jax.numpy as jnp
from jax import lax
from jax.experimental import pallas as pl
from jax.experimental.pallas import tpu as pltpu

HEADS = 16
FEAT = 16
HEAD_V = 128
WIDE = 256
STATE = 160
SQUARES = FEAT * (FEAT + 1) // 2
LINEAR = SQUARES + FEAT
HALF_HEADS = 128 // FEAT
STEP_HEADS = 8


def feature_tables():
    pairs = [(a, b) for a in range(FEAT) for b in range(a, FEAT)]
    pick = np.zeros((3, WIDE, WIDE), np.float32)
    for row in range(128):
        for entry, (a, b) in enumerate(pairs):
            if row % FEAT == a:
                pick[0, row, entry] = 1.0
                pick[1, row, entry] = 0.5 if a == b else 1.0
            if row % FEAT == b:
                pick[2, row, entry] = 1.0
        pick[0:2, row, SQUARES + row % FEAT] = 1.0
    pick[0:2, 128, LINEAR] = 1.0
    pick[2, 128, SQUARES : LINEAR + 1] = 1.0
    back = np.stack([np.concatenate([pick[n, :128], pick[2, :128]], axis=1) for n in (0, 1)])
    return jnp.asarray(pick, jnp.bfloat16), jnp.asarray(back, jnp.bfloat16)


def mul(left, right, kind="nn"):
    dims = {"nn": ((1,), (0,)), "nt": ((1,), (1,)), "tn": ((0,), (0,))}[kind]
    return lax.dot_general(left, right, (dims, ((), ())), preferred_element_type=jnp.float32)


def head_lanes(head, rows):
    lane = lax.broadcasted_iota(jnp.int32, (rows, 128), 1)
    return lane // FEAT == lax.rem(head, HALF_HEADS)


def own_lanes(block, head):
    scaled = block * jnp.asarray(FEAT**-0.25, jnp.bfloat16)
    return jnp.where(head_lanes(head, block.shape[0]), scaled, jnp.zeros_like(scaled))


def first_lanes(*columns):
    lane = lax.broadcasted_iota(jnp.int32, (columns[0].shape[0], 128), 1)
    out = jnp.zeros(lane.shape, jnp.float32)
    for n, column in enumerate(columns):
        out = jnp.where(lane == n, column, out)
    return out.astype(jnp.bfloat16)


def factors(own, pick_ref, which, kept):
    ones = first_lanes(jnp.ones_like(kept))
    plain = jnp.concatenate([own, ones], axis=1)
    masked = jnp.concatenate(
        [own * kept.astype(jnp.bfloat16), ones * kept.astype(jnp.bfloat16)], axis=1
    )
    first = mul(masked, pick_ref[which]).astype(jnp.bfloat16)
    second = mul(plain, pick_ref[2]).astype(jnp.bfloat16)
    return first, second


def pack_state(state, norm_rows):
    row = lax.broadcasted_iota(jnp.int32, (STATE, HEAD_V), 0)
    out = jnp.where(row == LINEAR + 1, norm_rows[0:1, :HEAD_V], state[:STATE])
    return jnp.where(row == LINEAR + 2, norm_rows[0:1, HEAD_V:], out)


def widen(packed):
    padded = jnp.concatenate([packed, jnp.zeros((WIDE - STATE, HEAD_V), packed.dtype)], axis=0)
    norm = jnp.concatenate(
        [packed[LINEAR + 1 : LINEAR + 2, :], packed[LINEAR + 2 : LINEAR + 3, :]], axis=1
    )
    return padded, norm


def step_heads():
    first = pl.program_id(0) * STEP_HEADS
    return [
        (first + n, n, slice(n * HEAD_V, (n + 1) * HEAD_V)) for n in range(STEP_HEADS)
    ]


def state_kernel(k_ref, v_ref, pick_ref, last_ref, out_ref):
    keys, last = k_ref[...], last_ref[...]
    ones = jnp.ones((16, keys.shape[0]), jnp.bfloat16)
    for head, n, lanes in step_heads():
        first, second = factors(own_lanes(keys, head), pick_ref, 0, last)
        phi = first * second
        state = mul(phi, v_ref[:, lanes], "tn")
        out_ref[n] = pack_state(state, mul(ones, phi)).astype(out_ref.dtype)


def causal_mask(seg_col_ref, seg_row_ref, mask_ref):
    rows = mask_ref.shape[0]
    i = lax.broadcasted_iota(jnp.int32, (rows, rows), 0)
    j = lax.broadcasted_iota(jnp.int32, (rows, rows), 1)
    keep = (seg_col_ref[...] == seg_row_ref[0:1, :]) & (j <= i)
    mask_ref[...] = keep.astype(jnp.float32).astype(jnp.bfloat16)


def triangle(rows):
    half = rows // 2
    return ((slice(0, half), slice(0, half)), (slice(half, rows), slice(0, rows)))


def local_kernel(q_ref, k_ref, v_ref, seg_col_ref, seg_row_ref, num_ref, den_ref, mask_ref):
    @pl.when(pl.program_id(0) == 0)
    def _():
        causal_mask(seg_col_ref, seg_row_ref, mask_ref)

    queries = q_ref[...]
    scaled = k_ref[...] * jnp.asarray(FEAT**-0.25, jnp.bfloat16)
    for head, _, lanes in step_heads():
        own_q = own_lanes(queries, head)
        value = v_ref[:, lanes]
        wide = jnp.concatenate([value, jnp.ones_like(value)], axis=1)
        for at, upto in triangle(own_q.shape[0]):
            up = 1.0 + mul(own_q[at], scaled[upto], "nt")
            kappa = (0.5 * up * up + 0.5).astype(jnp.bfloat16) * mask_ref[at, upto]
            both = mul(kappa, wide[upto])
            num_ref[at, lanes] = both[:, :HEAD_V]
            den_ref[at, lanes] = both[:, HEAD_V:]


def prefix_kernel(
    q_ref, num_ref, den_ref, state_ref, pick_ref, reading_ref, out_ref, inverse_ref
):
    queries, reading = q_ref[...], reading_ref[...]
    for head, n, lanes in step_heads():
        first, second = factors(own_lanes(queries, head), pick_ref, 1, reading)
        phi = first * second
        state, norm = widen(state_ref[n])
        num = num_ref[:, lanes] + mul(phi, state)
        norm = mul(phi, jnp.broadcast_to(norm, (HEAD_V, WIDE)), "nt")
        inverse = 1.0 / (den_ref[:, lanes] + norm)
        out_ref[:, lanes] = (num * inverse).astype(jnp.bfloat16)
        inverse_ref[:, lanes] = inverse


def scaled_grad(g_ref, att_ref, inverse_ref, lanes):
    gn = (g_ref[:, lanes].astype(jnp.float32) * inverse_ref[:, lanes]).astype(jnp.bfloat16)
    mixed = att_ref[:, lanes].astype(jnp.float32)
    gd = -jnp.sum(gn.astype(jnp.float32) * mixed, axis=1, keepdims=True)
    return gn, gd


def state_grad_kernel(q_ref, g_ref, att_ref, inverse_ref, pick_ref, reading_ref, out_ref):
    queries, reading = q_ref[...], reading_ref[...]
    for head, n, lanes in step_heads():
        gn, gd = scaled_grad(g_ref, att_ref, inverse_ref, lanes)
        first, second = factors(own_lanes(queries, head), pick_ref, 1, reading)
        phi = first * second
        state = mul(phi, gn, "tn")
        wide = jnp.broadcast_to(gd, gn.shape).astype(jnp.bfloat16)
        out_ref[n] = pack_state(state, mul(wide, phi, "tn")).astype(out_ref.dtype)


def chain(grad_phi, first, second, back_ref, which, head):
    both = jnp.concatenate([grad_phi * second, grad_phi * first], axis=1)
    grad = mul(both, back_ref[which], "nt")
    return jnp.where(head_lanes(head, grad_phi.shape[0]), grad, 0.0)


def local_grad_kernel(
    q_ref, k_ref, v_ref, g_ref, att_ref, inverse_ref, state_ref, pick_ref, back_ref,
    reading_ref, seg_col_ref, seg_row_ref, gq_ref, gk_ref, gv_ref, mask_ref, acc_ref,
):
    start = pl.program_id(0) * STEP_HEADS

    @pl.when(start == 0)
    def _():
        causal_mask(seg_col_ref, seg_row_ref, mask_ref)

    @pl.when(lax.rem(start, HALF_HEADS) == 0)
    def _():
        acc_ref[...] = jnp.zeros_like(acc_ref)
        gk_ref[...] = jnp.zeros_like(gk_ref)

    queries, keys, reading = q_ref[...], k_ref[...], reading_ref[...]
    half = queries.shape[0] // 2
    query_sums = jnp.zeros_like(acc_ref)
    key_sums = jnp.zeros_like(gk_ref)
    for head, n, lanes in step_heads():
        gn, gd = scaled_grad(g_ref, att_ref, inverse_ref, lanes)
        high = gd.astype(jnp.bfloat16).astype(jnp.float32)
        gn_wide = jnp.concatenate([gn, first_lanes(high, gd - high)], axis=1)
        ones = jnp.ones_like(gd)
        v_wide = jnp.concatenate([v_ref[:, lanes], first_lanes(ones, ones)], axis=1)
        own_q = own_lanes(queries, head)
        own_k = own_lanes(keys, head)
        parts, query_parts, key_parts = [], [], []
        for at, upto in triangle(own_q.shape[0]):
            keep = mask_ref[at, upto]
            up = 1.0 + mul(own_q[at], own_k[upto], "nt")
            kappa = (0.5 * up * up + 0.5).astype(jnp.bfloat16) * keep
            grad_t = mul(gn_wide[at], v_wide[upto], "nt").astype(jnp.bfloat16)
            grad_t = grad_t * up.astype(jnp.bfloat16) * keep
            query_parts.append(mul(grad_t, own_k[upto]))
            key_parts.append(mul(grad_t, own_q[at], "tn"))
            parts.append(mul(kappa, gn[at], "tn"))
        gv_ref[:half, lanes] = parts[0] + parts[1][:half]
        gv_ref[half:, lanes] = parts[1][half:]
        key_sums += key_parts[1] + jnp.concatenate(
            [key_parts[0], jnp.zeros_like(key_parts[0])], axis=0
        )
        first, second = factors(own_q, pick_ref, 1, reading)
        state, norm = widen(state_ref[n])
        grad_phi = mul(gn, state, "nt") + gd * norm.astype(jnp.float32)
        grad_phi = (grad_phi * reading).astype(jnp.bfloat16)
        query_sums += jnp.concatenate(query_parts, axis=0)
        query_sums += chain(grad_phi, first, second, back_ref, 1, head)
    acc_ref[...] += query_sums
    gk_ref[...] += key_sums

    @pl.when(lax.rem(start + STEP_HEADS, HALF_HEADS) == 0)
    def _():
        gq_ref[...] = (acc_ref[...] * FEAT**-0.25).astype(jnp.bfloat16)


def later_grad_kernel(
    k_ref, v_ref, gk_in_ref, gv_in_ref, state_ref, pick_ref, back_ref, last_ref,
    gk_ref, gv_ref, acc_ref,
):
    start = pl.program_id(0) * STEP_HEADS

    @pl.when(lax.rem(start, HALF_HEADS) == 0)
    def _():
        acc_ref[...] = gk_in_ref[...]

    keys, last = k_ref[...], last_ref[...]
    total = jnp.zeros_like(acc_ref)
    for head, n, lanes in step_heads():
        first, second = factors(own_lanes(keys, head), pick_ref, 0, last)
        state, norm = widen(state_ref[n])
        values = gv_in_ref[:, lanes] + mul(first * second, state)
        gv_ref[:, lanes] = values.astype(jnp.bfloat16)
        grad_phi = mul(v_ref[:, lanes], state, "nt") + norm.astype(jnp.float32)
        grad_phi = (grad_phi * last).astype(jnp.bfloat16)
        total = total + chain(grad_phi, first, second, back_ref, 0, head)
    acc_ref[...] += total

    @pl.when(lax.rem(start + STEP_HEADS, HALF_HEADS) == 0)
    def _():
        gk_ref[...] = (acc_ref[...] * FEAT**-0.25).astype(jnp.bfloat16)


def specs(rows):
    return dict(
        pair=pl.BlockSpec((rows, 128), lambda h: (0, h * STEP_HEADS // HALF_HEADS)),
        head=pl.BlockSpec((rows, STEP_HEADS * HEAD_V), lambda h: (0, h)),
        state=pl.BlockSpec((STEP_HEADS, STATE, HEAD_V), lambda h: (h, 0, 0)),
        pick=pl.BlockSpec((3, WIDE, WIDE), lambda h: (0, 0, 0)),
        back=pl.BlockSpec((2, 128, 2 * WIDE), lambda h: (0, 0, 0)),
        column=pl.BlockSpec((rows, 1), lambda h: (0, 0)),
        row=pl.BlockSpec((8, rows), lambda h: (0, 0)),
    )


def heads_call(kernel, rows, ins, outs, scratch=(), name=None):
    table = specs(rows)
    shapes = {
        "pair": (rows, HEADS * FEAT),
        "head": (rows, HEADS * HEAD_V),
        "state": (HEADS, STATE, HEAD_V),
    }
    return pl.pallas_call(
        kernel,
        grid=(HEADS // STEP_HEADS,),
        in_specs=[table[kind] for kind in ins],
        out_specs=[table[kind] for kind, _ in outs],
        out_shape=[jax.ShapeDtypeStruct(shapes[kind], kept) for kind, kept in outs],
        scratch_shapes=list(scratch),
        compiler_params=pltpu.CompilerParams(
            dimension_semantics=("arbitrary",), vmem_limit_bytes=32 * 2**20
        ),
        cost_estimate=pl.CostEstimate(flops=2**20, bytes_accessed=2**16, transcendentals=0),
        name=name,
    )


f32, bf = jnp.float32, jnp.bfloat16


def mix_state(k, v, tables, last):
    rows = k.shape[0]
    return heads_call(state_kernel, rows, ["pair", "head", "pick", "column"],
        [("state", bf)], name="mix_state")(k, v, tables[0], last)[0]


def mix_local(q, k, v, seg_col, seg_row):
    rows = k.shape[0]
    return heads_call(local_kernel, rows, ["pair", "pair", "head", "column", "row"],
        [("head", f32), ("head", f32)], [pltpu.VMEM((rows, rows), bf)], name="mix_local")(q, k, v, seg_col, seg_row)


def mix_prefix(q, num, den, state, tables, reading):
    rows = q.shape[0]
    return heads_call(prefix_kernel, rows, ["pair", "head", "head", "state", "pick", "column"],
        [("head", bf), ("head", f32)], name="mix_prefix")(q, num, den, state, tables[0], reading)


def mix_state_grad(q, g, att, inverse, tables, reading):
    rows = q.shape[0]
    return heads_call(state_grad_kernel, rows, ["pair", "head", "head", "head", "pick", "column"],
        [("state", bf)], name="mix_state_grad")(q, g, att, inverse, tables[0], reading)[0]


def mix_local_grad(q, k, v, g, att, inverse, state, tables, reading, seg_col, seg_row):
    rows = q.shape[0]
    return heads_call(local_grad_kernel, rows,
        ["pair", "pair", "head", "head", "head", "head", "state", "pick", "back", "column", "column", "row"],
        [("pair", bf), ("pair", f32), ("head", f32)],
        [pltpu.VMEM((rows, rows), bf), pltpu.VMEM((rows, 128), f32)], name="mix_local_grad")(
        q, k, v, g, att, inverse, state, *tables, reading, seg_col, seg_row)


def mix_later_grad(k, v, gk, gv, state, tables, last):
    rows = k.shape[0]
    return heads_call(later_grad_kernel, rows,
        ["pair", "head", "pair", "head", "state", "pick", "back", "column"],
        [("pair", bf), ("head", bf)], [pltpu.VMEM((rows, 128), f32)], name="mix_later_grad")(
        k, v, gk, gv, state, *tables, last)


from jax.sharding import PartitionSpec as P

D = 2048
EPSILON = 1e-05
LIMIT = 36 * 2**20
TILE = 352


def cost(flops, moved):
    return pl.CostEstimate(flops=flops, bytes_accessed=moved, transcendentals=0)


def whole(*shape):
    return pl.BlockSpec(shape, lambda *_: (0,) * len(shape), pipeline_mode=pl.Buffered(1))


def tiling(parts, rows):
    if parts == 1:
        taken = TILE if rows % TILE == 0 else rows
        return 1, taken, rows // taken
    taken = max(1, TILE // rows)
    taken = taken if parts % taken == 0 else parts
    return taken, rows, parts // taken


def gate_kernel(x_ref, c_ref, *refs):
    count = len(refs) // 3
    half = x_ref.shape[0] // 2
    for n in range(count):
        both_ref, down_ref, out_ref = refs[2 * n], refs[2 * n + 1], refs[2 * count + n]
        parts, _, rows, _ = both_ref.shape
        gate_w, up_w = [both_ref[:, k].reshape(parts * rows, D) for k in range(2)]
        down_w = down_ref[:, 0].reshape(parts * rows, D)
        for at in (slice(0, half), slice(half, 2 * half)):
            x, c = x_ref[at, :], c_ref[at, :]
            gate = mul(gate_w, x, "nt")
            up = mul(up_w, x, "nt")
            grad = mul(down_w, c, "nt").astype(bf).astype(f32)
            sig = 1.0 / (1.0 + jnp.exp(-gate))
            act = gate * sig
            out_ref[0, :, at] = (grad * up * sig * (1.0 + gate * (1.0 - sig))).astype(bf)
            out_ref[1, :, at] = (grad * act).astype(bf)
            out_ref[2, :, at] = (act * up).astype(bf)


def ffn_gates(x, c, weights):
    rows, count = x.shape[0], len(weights)
    hidden = weights[0][1].shape[0] * weights[0][1].shape[2]
    ins, outs = [whole(rows, D)] * 2, []
    for pair in weights:
        for w in pair:
            taken, height, steps = tiling(w.shape[0], w.shape[2])
            at = (lambda i: (0, 0, i, 0)) if w.shape[0] == 1 else (lambda i: (i, 0, 0, 0))
            ins.append(pl.BlockSpec((taken, w.shape[1], height, D), at))
        outs.append(pl.BlockSpec((3, taken * height, rows), lambda i: (0, i, 0)))
    return pl.pallas_call(
        gate_kernel,
        grid=(steps,),
        in_specs=ins,
        out_specs=outs,
        out_shape=[jax.ShapeDtypeStruct((3, hidden, rows), bf)] * count,
        compiler_params=pltpu.CompilerParams(vmem_limit_bytes=LIMIT),
        cost_estimate=cost(
            6 * rows * D * hidden * count,
            2 * (2 * rows * D + 3 * count * hidden * (D + rows)),
        ),
        name="ffn_gates",
    )(x, c, *[w for pair in weights for w in pair])


def back_kernel(count, *refs):
    made, weights, out_ref, turned = (
        refs[:count], refs[count : 2 * count], refs[-count - 1], refs[-count:]
    )
    added = refs[2 * count : -count - 1]

    @pl.when(pl.program_id(0) == 0)
    def _():
        for block, kept in zip(made, turned):
            kinds, hidden, rows = block.shape
            kept[...] = block[...].reshape(kinds * hidden, rows).T

    total = None
    for kept, w_ref in zip(turned, weights):
        parts, kinds, rows, columns = w_ref.shape
        right = jnp.concatenate(
            [w_ref[:, k].reshape(parts * rows, columns) for k in range(kinds)], axis=0
        )
        part = mul(kept[...], right)
        total = part if total is None else total + part
    for more in added:
        total = total + more[...].astype(f32)
    out_ref[...] = total.astype(out_ref.dtype)


def ffn_back(made, weights, which, added=(), columns=512):
    count = len(weights)
    weights = [pair[which] for pair in weights]
    kinds = weights[0].shape[1]
    _, hidden, rows = made[0].shape
    out = pl.BlockSpec((rows, columns), lambda j: (0, j))
    ins = [
        pl.BlockSpec(
            (kinds, hidden, rows), lambda j: (2 * which // kinds, 0, 0), pipeline_mode=pl.Buffered(1)
        )
    ] * count
    for w in weights:
        ins.append(pl.BlockSpec((w.shape[0], kinds, w.shape[2], columns), lambda j: (0, 0, 0, j)))
    ins += [out] * len(added)
    return pl.pallas_call(
        functools.partial(back_kernel, count),
        grid=(D // columns,),
        in_specs=ins,
        out_specs=out,
        out_shape=jax.ShapeDtypeStruct((rows, D), bf),
        scratch_shapes=[pltpu.VMEM((rows, kinds * hidden), bf)] * count,
        compiler_params=pltpu.CompilerParams(vmem_limit_bytes=LIMIT),
        cost_estimate=cost(
            2 * rows * D * hidden * kinds * count,
            2 * (count * kinds * hidden * (D + rows) + rows * D),
        ),
        name="ffn_back",
    )(*made, *weights, *added)


def grad_kernel(blocks, *refs):
    made, xs, cs = refs[:blocks], refs[blocks : 2 * blocks], refs[2 * blocks : 3 * blocks]
    added, out_ref = refs[3 * blocks : -1], refs[-1]
    parts, _, rows, _ = out_ref.shape

    def write(rights):
        total = None
        for left, right in zip(made, rights):
            part = mul(left[0], right[...])
            total = part if total is None else total + part
        for more in added:
            total = total + more[...].reshape(parts * rows, D).astype(f32)
        out_ref[...] = total.astype(bf).reshape(parts, 1, rows, D)

    kind = pl.program_id(0)

    @pl.when(kind < 2)
    def _():
        write(xs)

    @pl.when(kind == 2)
    def _():
        write(cs)


def ffn_grad(made, xs, cs, parts, height, added=None):
    blocks = len(made)
    rows = xs[0].shape[0]
    hidden = made[0].shape[1]
    taken, rise, steps = tiling(parts, height)
    left = pl.BlockSpec((1, taken * rise, rows), lambda k, i: (k, i, 0))
    at = (lambda k, i: (0, k, i, 0)) if parts == 1 else (lambda k, i: (i, k, 0, 0))
    out = pl.BlockSpec((taken, 1, rise, D), at)
    more = [] if added is None else [added]
    return pl.pallas_call(
        functools.partial(grad_kernel, blocks),
        grid=(3, steps),
        in_specs=[left] * blocks + [whole(rows, D)] * (2 * blocks) + [out] * len(more),
        out_specs=out,
        out_shape=jax.ShapeDtypeStruct((parts, 3, height, D), bf),
        compiler_params=pltpu.CompilerParams(vmem_limit_bytes=LIMIT),
        cost_estimate=cost(
            6 * rows * D * hidden * blocks,
            2 * (2 * blocks * rows * D + 3 * hidden * (rows * blocks + D * (1 + len(more)))),
        ),
        name="ffn_grad",
    )(*made, *xs, *cs, *more)


def widen_kernel(sum_ref, *out_refs):
    for kind, out_ref in enumerate(out_refs):
        out_ref[...] = sum_ref[0, kind].astype(f32)


def widened(sums):
    parts, _, height, _ = sums.shape
    return pl.pallas_call(
        widen_kernel,
        grid=(parts,),
        in_specs=[pl.BlockSpec((1, 3, height, D), lambda i: (i, 0, 0, 0))],
        out_specs=[pl.BlockSpec((height, D), lambda i: (i, 0))] * 3,
        out_shape=[jax.ShapeDtypeStruct((parts * height, D), f32)] * 3,
        compiler_params=pltpu.CompilerParams(vmem_limit_bytes=LIMIT),
        cost_estimate=cost(0, 6 * parts * 3 * height * D),
        name="widened",
    )(sums)


def qkv_grad_kernel(n_ref, gq_ref, gk_ref, gv_ref, out_ref):
    turned = n_ref[...].T
    qk = gq_ref.shape[1]
    out_ref[:, :qk] = mul(turned, gq_ref[...]).astype(bf)
    out_ref[:, qk : 2 * qk] = mul(turned, gk_ref[...]).astype(bf)
    out_ref[:, 2 * qk :] = mul(turned, gv_ref[...]).astype(bf)


def qkv_grad(normed, gq, gk, gv):
    rows, qk = gq.shape
    columns = 2 * qk + D
    tile = 256
    return pl.pallas_call(
        qkv_grad_kernel,
        grid=(D // tile,),
        in_specs=[
            pl.BlockSpec((rows, tile), lambda i: (0, i)), whole(rows, qk), whole(rows, qk), whole(rows, D)
        ],
        out_specs=pl.BlockSpec((tile, columns), lambda i: (i, 0)),
        out_shape=jax.ShapeDtypeStruct((D, columns), bf),
        compiler_params=pltpu.CompilerParams(vmem_limit_bytes=LIMIT),
        cost_estimate=cost(2 * rows * D * columns, 2 * (rows * (D + columns) + D * columns)),
        name="qkv_grad",
    )(normed, gq, gk, gv)


def norm_forward(inputs):
    inverse = lax.rsqrt(jnp.mean(inputs * inputs, axis=-1, keepdims=True) + EPSILON)
    return (inputs * inverse, inverse)


def norm_backward(grad_normed, unit_rows, inverse, gain_vec):
    gain_grad = jnp.sum(grad_normed * unit_rows, axis=0)
    grad_unit = grad_normed * gain_vec
    return (
        inverse * (grad_unit - unit_rows * jnp.mean(grad_unit * unit_rows, axis=-1, keepdims=True)),
        gain_grad,
    )


def move(array, target, axis="mp"):
    size = lax.axis_size(axis)
    pairs = [(m, target(m)) for m in range(size)]
    return lax.ppermute(array, axis, [(m, t) for m, t in pairs if t is not None])


def then(value, *before):
    return lax.optimization_barrier((value, before))[0]


def beside(array, mover, *works):
    ends = [array.shape[0] * n // len(works) // 16 * 16 for n in range(len(works))] + [array.shape[0]]
    moved, made = [], []
    for n, work in enumerate(works):
        share = array[ends[n] : ends[n + 1]]
        if made:
            share = then(share, made[-1])
        result = work(share, made)
        arrived, result = lax.optimization_barrier((mover(share), result))
        moved.append(arrived)
        made.append(result)
    return jnp.concatenate(moved, axis=0), made


def to_mate(array):
    return move(array, lambda m: m ^ 1)


def to_half(array):
    size = lax.axis_size("mp")
    return move(array, lambda m: (m + size // 2) % size)


def to_peer(array, step):
    half = lax.axis_size("mp") // 2

    def target(m):
        low = m % half
        return m - low + (low + 2 * step) % half

    return move(array, target)


def to_chip(array, step):
    size = lax.axis_size("mp")
    return move(array, lambda m: m + 2 * step if 0 <= m + 2 * step < size else None)


def sums_before(own, sign, *beside, made=None):
    core = lax.axis_index("mp") % 2
    chips = lax.axis_size("mp") // 2
    wire = own.astype(bf)
    mate = to_mate(wire).astype(f32)
    half = own.shape[0] // 2
    both = wire.astype(f32) + mate
    running = lax.dynamic_slice_in_dim(both, core * half, half, 0)
    before = jnp.zeros_like(running)
    step, beside, made = 1, list(beside), [] if made is None else made
    while step < chips:
        came = to_chip(running.astype(bf), sign * step)
        if beside:
            came, result = lax.optimization_barrier((came, beside.pop(0)(running)))
            made.append(result)
        came = came.astype(f32)
        before = before + came
        running = running + came
        step *= 2
    before = before.astype(bf)
    other = to_mate(before)
    first = jnp.where(core == 0, before, other)
    second = jnp.where(core == 0, other, before)
    total = jnp.concatenate([first, second], axis=0).astype(f32)
    inner = core == (1 if sign > 0 else 0)
    return (total + jnp.where(inner, mate, 0.0)).astype(bf), made


def pick(array, index, dim=0):
    return lax.dynamic_index_in_dim(array, index, dim, keepdims=False)


def chip_halves(array):
    groups, size = lax.axis_size("dp"), lax.axis_size("mp")
    core = lax.axis_index("mp") % 2
    rows, columns = array.shape[0] // (groups * size), array.shape[1]
    blocks = array.reshape(groups, size // 2, 2, rows, columns)
    return pick(blocks, core, 2), pick(blocks, 1 - core, 2)


def add(first, *more, kept=bf):
    total = first.astype(f32)
    for array in more:
        total = total + array.astype(f32)
    return total.astype(kept)


def placed(shares, places):
    out = jnp.zeros((len(shares),) + shares[0].shape, shares[0].dtype)
    for share, at in zip(shares, places):
        out = lax.dynamic_update_index_in_dim(out, share, at, 0)
    return out


def chip_shares(array):
    steps = range(1, lax.axis_size("mp") // 2)
    return [move(array, lambda m: m ^ (2 * step)) for step in steps]


def by_chip(array, shares):
    chip = lax.axis_index("mp") // 2
    return placed([array] + shares, [chip ^ step for step in range(len(shares) + 1)])


def first_groups(array):
    return [move(array, lambda m: m ^ step, "dp") for step in (1, 2)]


def third_group(first, second):
    half = first.shape[0] // 2
    return [
        move(second[:half], lambda m: m ^ 1, "dp"),
        move(first[half:], lambda m: m ^ 2, "dp"),
    ]


def assembled(pieces, groups, chips, out=None):
    group, core = lax.axis_index("dp"), lax.axis_index("mp") % 2
    shape = pieces[0][2].shape[1:]
    if out is None:
        out = jnp.zeros((groups, chips, 2) + shape, bf)
    for step, at, own, other in pieces:
        both = jnp.where(core == 0, jnp.stack([own, other], 1), jnp.stack([other, own], 1))
        start = (group ^ step, at) + (0,) * (len(shape) + 1)
        out = lax.dynamic_update_slice(out, both[None], start)
    return out


def group_move(array, step):
    return move(pick(array, lax.axis_index("dp") ^ step), lambda m: m ^ step, "dp")


def chip_moves(array):
    chip = lax.axis_index("mp") // 2
    return [
        move(pick(array, chip ^ step), lambda m: m ^ (2 * step))
        for step in range(1, lax.axis_size("mp") // 2)
    ]


def sum_everywhere(array):
    for axis in ("mp", "dp"):
        step = 1
        while step < lax.axis_size(axis):
            array = array + move(array, lambda m: m ^ step, axis)
            step *= 2
    return array


def body(
    x_in,
    seq_lengths,
    norm1_gain,
    w_query,
    w_key,
    w_value,
    w_out,
    norm2_gain,
    w_gate,
    w_up,
    w_down,
    cotangent,
):
    rows = x_in.shape[0]
    groups = lax.axis_size("dp")
    size = lax.axis_size("mp")
    peers = size // 4
    hidden = w_gate.shape[1]
    piece = hidden // groups
    place = lax.axis_index("mp")
    group = lax.axis_index("dp")
    everywhere = ("dp", "mp")
    qk = w_query.shape[1]
    aligned = piece % 16 == 0

    own_rows = w_query.shape[0]
    gain_block = jnp.concatenate(
        [norm1_gain[:, None], norm2_gain[:, None], jnp.zeros((own_rows, 126), bf)], axis=1
    )
    packed = jnp.concatenate([w_query, w_key, w_value, gain_block], axis=1)
    in_chips, packed = lax.optimization_barrier((chip_shares(packed), packed))
    in_chips = by_chip(packed, in_chips)

    full_out = lax.all_gather(w_out, everywhere, axis=0, tiled=True)
    half_chips = size // 4
    mine_both = jnp.concatenate(then([w_gate.T, w_up.T], in_chips), axis=0)
    mine = (mine_both.reshape(1, 2, hidden, D), then(w_down, in_chips).reshape(1, 1, hidden, D))
    far_down = lax.dynamic_slice_in_dim(mine[1][0, 0], group * piece, piece, 0)
    far_both = lax.dynamic_slice_in_dim(mine[0][0], group * piece, piece, 1).reshape(2 * piece, D)
    cot_ends = [rows * n // 16 for n in (0, 6, 10, 13, 16)]
    cot_shares = [cotangent[a:b] for a, b in zip(cot_ends, cot_ends[1:])]

    def peers_of(array):
        return [to_peer(array, step) for step in range(1, peers)]

    def beside_one(array, mover, work):
        return lax.optimization_barrier((mover(array), work(array)))

    both_cut, down_cut = 2 * piece * 8 // 11, piece * 7 // 11
    in_near, in_mate, cot_first, both_first = lax.optimization_barrier(
        (
            first_groups(in_chips),
            to_mate(in_chips),
            peers_of(then(cot_shares[0], in_chips)),
            to_half(then(far_both[:both_cut], in_chips)),
        )
    )
    in_third, in_mates, both_second = lax.optimization_barrier(
        (
            third_group(*in_near),
            [to_mate(share) for share in in_near],
            to_half(then(far_both[both_cut:], in_near)),
        )
    )
    in_mates = [in_mate, *in_mates] + [to_mate(share) for share in in_third]
    far_both = jnp.concatenate([both_first, both_second], axis=0)
    far_both = lax.all_gather(far_both, "dp", axis=0, tiled=True).reshape(groups, 2, piece, D)
    down_first = to_half(then(far_down[:down_cut], in_third))
    mate_down = to_mate(then(mine[1], in_third))
    cot_second = peers_of(then(cot_shares[1], in_third))
    in_pieces = [
        (step, at, own, other)
        for (step, at, own), other in zip(
            (
                (0, 0, in_chips),
                (1, 0, in_near[0]),
                (2, 0, in_near[1]),
                (3, 0, in_third[0]),
                (3, half_chips, in_third[1]),
            ),
            in_mates,
        )
    ]
    full_in = assembled(in_pieces, groups, size // 2).reshape(D, packed.shape[1])

    row_start = place * rows
    seq_ends = jnp.cumsum(seq_lengths[0], dtype=jnp.int32)
    positions = row_start + jnp.arange(rows, dtype=jnp.int32)
    segments = jnp.sum((positions[:, None] >= seq_ends[None, :]).astype(jnp.int32), axis=1)
    seg_before = jnp.sum((row_start - 1 >= seq_ends).astype(jnp.int32))
    reading = ((segments == seg_before) & (row_start > 0)).astype(f32)[:, None]
    last_doc = (segments == segments[-1]).astype(f32)[:, None]
    seg_col = segments[:, None]
    seg_row = jnp.broadcast_to(segments[None, :], (8, rows))
    tables = feature_tables()

    inputs = x_in.astype(f32)
    inverse_one = norm_forward(inputs)[1]
    early = (full_out, mine, down_first, mate_down, cot_second, inverse_one, reading, last_doc, seg_col, seg_row)
    full_in, early = lax.optimization_barrier((full_in, early))
    full_out, mine, down_first, mate_down, cot_second, inverse_one, reading, last_doc, seg_col, seg_row = early
    gain_one = full_in[:, 2 * qk + D].astype(f32)
    gain_two = full_in[:, 2 * qk + D + 1].astype(f32)
    full_qkv = full_in[:, : 2 * qk + D]
    unit_one = inputs * inverse_one
    normed_one = (unit_one * gain_one).astype(bf)
    (got, mate_gate, down_second), qkv = beside_one(
        then(cot_shares[2], full_in),
        lambda ready: (
            peers_of(ready),
            to_mate(then(mine[0][:, :1], ready)),
            to_half(then(far_down[down_cut:], ready)),
        ),
        lambda ready: mul(then(normed_one, ready), full_qkv).astype(bf),
    )
    cot_got = [cot_first, cot_second, got]
    queries, keys, values = qkv[:, :qk], qkv[:, qk : 2 * qk], qkv[:, 2 * qk :]
    far_down = jnp.concatenate([down_first, down_second], axis=0)
    far_down = lax.all_gather(far_down, "dp", axis=0, tiled=True).reshape(groups, 1, piece, D)
    (got, mate_up), own_state = beside_one(
        then(cot_shares[3], qkv),
        lambda ready: (peers_of(ready), to_mate(then(mine[0][:, 1:], ready))),
        lambda ready: mix_state(then(keys, ready), values, tables, last_doc),
    )
    cot_got.append(got)

    def local_work(ready):
        local = mix_local(then(queries, ready), keys, values, seg_col, seg_row)
        return local

    def pack_work(ready):
        gate, up = then((mate_gate, mate_up), ready)
        return jnp.concatenate([gate, up], axis=1)

    prefix, [(num, den), mate_both] = sums_before(own_state, 1, local_work, pack_work)
    attended, inverse_den = mix_prefix(queries, num, den, prefix, tables, reading)
    mate = (mate_both, mate_down)
    near = [mine, mate]
    hidden_in = inputs + mul(attended, full_out)
    unit_two, inverse_two = norm_forward(hidden_in)
    normed_two = (unit_two * gain_two).astype(bf)
    came = [to_peer(normed_two, step) for step in range(1, peers)]

    near_own = ffn_gates(normed_two, cotangent, near)
    far_mine = then((far_both, far_down), normed_two)
    if not aligned:
        far_mine = tuple(jnp.swapaxes(w, 0, 1).reshape(1, -1, hidden, D) for w in far_mine)
    far_mate = then(tuple(to_mate(w) for w in far_mine), near_own)
    far = [tuple(far_mine), far_mate]
    weights = near + far
    shape = (groups, piece) if aligned else (1, hidden)
    far_own = ffn_gates(normed_two, cotangent, far)
    made_own = list(near_own) + list(far_own)
    grad_own = ffn_back(made_own, weights, 0)
    out_own = ffn_back(then(made_own, grad_own), weights, 1)
    normed = [normed_two] + then(came, out_own)
    cot_got = then(cot_got, near_own)
    cots = [cotangent] + [jnp.concatenate(parts, axis=0) for parts in zip(*cot_got)]
    near_made = [near_own] + [ffn_gates(x, c, near) for x, c in zip(normed[1:], cots[1:])]
    far_made = [far_own] + [
        ffn_gates(x, c, then(far, near_made)) for x, c in zip(normed[1:], cots[1:])
    ]
    made = [list(a) + list(b) for a, b in zip(near_made, far_made)]

    def weight_grads(made, ready, added=None):
        return ffn_grad(then(made, ready), normed, cots, *shape, added)

    def over_groups(grad):
        if not aligned:
            grad = jnp.swapaxes(grad.reshape(3, groups, piece, D), 0, 1)
        return lax.psum_scatter(
            grad.reshape(groups * 3 * piece, D), "dp", scatter_dimension=0, tiled=True
        )

    def back(block, which, ready):
        return ffn_back(then(block, ready), weights, which)

    far_given = weight_grads([block[1] for block in far_made], far_made)
    far_sent = to_mate(far_given)
    grad_parts = [back(block, 0, far_given) for block in made[1:]]

    def owners(parts):
        return [to_peer(part, peers - step) for step, part in enumerate(parts, 1)]

    def stacked(parts):
        return jnp.concatenate([part[:, None] for part in parts], axis=1)

    def to_owners(parts):
        return stacked(owners([parts[:, n] for n in range(peers - 1)]))

    def near_work(ready, _):
        given = weight_grads([block[1] for block in near_made], ready)
        return given

    def far_work(ready, done):
        kept = weight_grads([block[0] for block in far_made], ready, far_sent)
        return kept, to_mate(then(done[0], ready))

    def last_work(ready, done):
        return weight_grads([block[0] for block in near_made], ready, done[1][1])

    grad_sent, (_, (far_kept, _), near_kept) = beside(
        stacked(grad_parts), to_owners, near_work, far_work, last_work
    )
    far_part = over_groups(far_kept)
    near_part = over_groups(near_kept)
    grad_normed_two = jnp.sum(grad_sent.astype(f32), axis=1) + grad_own.astype(f32)

    grad_two, gain_two_grad = norm_backward(grad_normed_two, unit_two, inverse_two, gain_two)
    grad_hidden_in = cotangent.astype(f32) + grad_two
    grad_branch = grad_hidden_in.astype(bf)
    grad_attended = mul(grad_branch, full_out, "nt").astype(bf)
    state_grad = mix_state_grad(queries, grad_attended, attended, inverse_den, tables, reading)

    def local_grads(ready):
        local = mix_local_grad(
            then(queries, ready), keys, values, grad_attended, attended, inverse_den, prefix, tables,
            reading, seg_col, seg_row,
        )
        return local, to_mate(then(out_halves[1], ready))

    out_halves = []

    def out_work(ready):
        halves = chip_halves(mul(then(attended, ready), grad_branch, "tn").astype(bf))
        out_halves.extend(halves)
        return halves

    later, [_, (local, out_came)] = sums_before(state_grad, -1, out_work, local_grads)
    grad_queries, part_keys, part_values = local
    out_kept = add(out_halves[0], out_came)
    out_kept, far_part = then((out_kept, far_part), later)
    ends = [far_part.shape[0] * n // 33 for n in (0, 3, 7, 12, 33)]
    far_shares = [far_part[a:b] for a, b in zip(ends, ends[1:])]
    out_first, out_second, out_diag = [pick(out_kept, group ^ step) for step in range(1, groups)]
    low, high = slice(None, half_chips), slice(half_chips, None)

    def by_first(block):
        return move(block, lambda m: m ^ 1, "dp")

    def by_second(block):
        return move(block, lambda m: m ^ 2, "dp")

    (far_first, for_second, for_first), (grad_keys, grad_values) = beside_one(
        then(far_shares[0], out_kept),
        lambda ready: (
            to_half(ready), by_first(then(out_diag[low], ready)), by_second(then(out_diag[high], ready))
        ),
        lambda ready: mix_later_grad(
            then(keys, ready), values, part_keys, part_values, later, tables, last_doc
        ),
    )
    out_second = [add(out_second[low], for_second), out_second[high]]
    out_first = [out_first[low], add(out_first[high], for_first)]
    (far_second, out_low), in_grad = beside_one(
        then(far_shares[1], grad_keys),
        lambda ready: (
            to_half(ready), [by_first(then(out_first[0], ready)), by_second(then(out_second[0], ready))]
        ),
        lambda ready: qkv_grad(then(normed_one, ready), grad_queries, grad_keys, grad_values),
    )
    in_keep, in_give = chip_halves(in_grad)
    in_came = to_mate(in_give)
    far_third = to_half(then(far_shares[2], in_grad))
    out_high = [by_first(then(out_first[1], in_grad)), by_second(then(out_second[1], in_grad))]
    far_third, in_came, out_high = lax.optimization_barrier((far_third, in_came, out_high))
    in_shares = [
        add(pick(in_keep, group ^ step), pick(in_came, group ^ step)) for step in range(1, groups)
    ]
    out_parts = [back(block, 1, in_shares) for block in made[1:]]
    in_moved = [
        move(share, lambda m: m ^ step, "dp") for step, share in enumerate(in_shares, 1)
    ]
    far_last = to_half(then(far_shares[3], in_came))
    grad_queries, grad_keys, grad_values = then(
        (grad_queries, grad_keys, grad_values), in_shares
    )
    grad_normed_one = (
        mul(grad_queries, full_qkv[:, :qk], "nt")
        + mul(grad_keys, full_qkv[:, qk : 2 * qk], "nt")
        + mul(grad_values, full_qkv[:, 2 * qk :], "nt")
    )
    grad_one, gain_one_grad = norm_backward(grad_normed_one, unit_one, inverse_one, gain_one)
    input_grad = (grad_hidden_in + grad_one).astype(bf)
    out_parts, input_grad, gain_one_grad, in_moved, far_last = lax.optimization_barrier(
        (out_parts, input_grad, gain_one_grad, in_moved, far_last)
    )
    far_sum = jnp.concatenate([far_first, far_second, far_third, far_last], axis=0)
    ffn_sum = lax.all_gather(add(near_part, far_sum), "dp", axis=0, tiled=True)
    ffn_sum = ffn_sum.reshape(groups, 3, piece, D)
    out_sent = to_owners(stacked(out_parts))
    output = (hidden_in + jnp.sum(out_sent.astype(f32), axis=1) + out_own.astype(f32)).astype(bf)
    chip = place // 2

    def over_chips(blocks, kept):
        shares = [
            add(*[pick(block, chip ^ step) for block in blocks]) for step in range(1, size // 2)
        ]
        moved = [move(share, lambda m: m ^ (2 * step)) for step, share in enumerate(shares, 1)]
        return add(*[pick(block, chip) for block in blocks], *moved, kept=kept)

    in_sum = over_chips([pick(in_keep, group), pick(in_came, group), *in_moved], f32)
    out_blocks = [jnp.concatenate(pair, axis=0) for pair in zip(out_low, out_high)]
    out_blocks = then([pick(out_kept, group), *out_blocks], in_moved)
    out_sum = over_chips(out_blocks, f32)
    if not aligned:
        ffn_sum = jnp.swapaxes(ffn_sum, 0, 1).reshape(1, 3, hidden, D)
    gate_grad, up_grad, down_grad = widened(ffn_sum)
    gain_sums = sum_everywhere(jnp.stack([gain_one_grad, gain_two_grad]))
    gain_sums = lax.dynamic_slice_in_dim(
        gain_sums, (group * size + place) * own_rows, own_rows, 1
    )
    return (
        output,
        input_grad,
        gain_sums[0],
        in_sum[:, :qk],
        in_sum[:, qk : 2 * qk],
        in_sum[:, 2 * qk :],
        out_sum,
        gain_sums[1],
        gate_grad.T,
        up_grad.T,
        down_grad,
    )


def solution(mesh):
    rows, vector = P(("dp", "mp"), None), P(("dp", "mp"))
    columns, down = P(None, "mp"), P("mp", None)
    return jax.shard_map(
        body,
        mesh=mesh,
        in_specs=(rows, P("dp", None), vector, rows, rows, rows, rows, vector, columns, columns, down, rows),
        out_specs=(rows, rows, vector, rows, rows, rows, rows, vector, columns, columns, down),
        check_vma=False,
    )
```

```python
import functools
import numpy as np
import jax
import jax.numpy as jnp
from jax import lax
from jax.experimental import pallas as pl
from jax.experimental.pallas import tpu as pltpu

HEADS = 16
FEAT = 16
HEAD_V = 128
WIDE = 256
STATE = 160
SQUARES = FEAT * (FEAT + 1) // 2
LINEAR = SQUARES + FEAT
HALF_HEADS = 128 // FEAT
STEP_HEADS = 8


def feature_tables():
    pairs = [(a, b) for a in range(FEAT) for b in range(a, FEAT)]
    pick = np.zeros((3, WIDE, WIDE), np.float32)
    for row in range(128):
        for entry, (a, b) in enumerate(pairs):
            if row % FEAT == a:
                pick[0, row, entry] = 1.0
                pick[1, row, entry] = 0.5 if a == b else 1.0
            if row % FEAT == b:
                pick[2, row, entry] = 1.0
        pick[0:2, row, SQUARES + row % FEAT] = 1.0
    pick[0:2, 128, LINEAR] = 1.0
    pick[2, 128, SQUARES : LINEAR + 1] = 1.0
    back = np.stack([np.concatenate([pick[n, :128], pick[2, :128]], axis=1) for n in (0, 1)])
    return jnp.asarray(pick, jnp.bfloat16), jnp.asarray(back, jnp.bfloat16)


def mul(left, right, kind="nn"):
    dims = {"nn": ((1,), (0,)), "nt": ((1,), (1,)), "tn": ((0,), (0,))}[kind]
    return lax.dot_general(left, right, (dims, ((), ())), preferred_element_type=jnp.float32)


def head_lanes(head, rows):
    lane = lax.broadcasted_iota(jnp.int32, (rows, 128), 1)
    return lane // FEAT == lax.rem(head, HALF_HEADS)


def own_lanes(block, head):
    scaled = block * jnp.asarray(FEAT**-0.25, jnp.bfloat16)
    return jnp.where(head_lanes(head, block.shape[0]), scaled, jnp.zeros_like(scaled))


def first_lanes(*columns):
    lane = lax.broadcasted_iota(jnp.int32, (columns[0].shape[0], 128), 1)
    out = jnp.zeros(lane.shape, jnp.float32)
    for n, column in enumerate(columns):
        out = jnp.where(lane == n, column, out)
    return out.astype(jnp.bfloat16)


def factors(own, pick_ref, which, kept):
    ones = first_lanes(jnp.ones_like(kept))
    plain = jnp.concatenate([own, ones], axis=1)
    masked = jnp.concatenate(
        [own * kept.astype(jnp.bfloat16), ones * kept.astype(jnp.bfloat16)], axis=1
    )
    first = mul(masked, pick_ref[which]).astype(jnp.bfloat16)
    second = mul(plain, pick_ref[2]).astype(jnp.bfloat16)
    return first, second


def pack_state(state, norm_rows):
    row = lax.broadcasted_iota(jnp.int32, (STATE, HEAD_V), 0)
    out = jnp.where(row == LINEAR + 1, norm_rows[0:1, :HEAD_V], state[:STATE])
    return jnp.where(row == LINEAR + 2, norm_rows[0:1, HEAD_V:], out)


def widen(packed):
    padded = jnp.concatenate([packed, jnp.zeros((WIDE - STATE, HEAD_V), packed.dtype)], axis=0)
    norm = jnp.concatenate(
        [packed[LINEAR + 1 : LINEAR + 2, :], packed[LINEAR + 2 : LINEAR + 3, :]], axis=1
    )
    return padded, norm


def step_heads():
    first = pl.program_id(0) * STEP_HEADS
    return [
        (first + n, n, slice(n * HEAD_V, (n + 1) * HEAD_V)) for n in range(STEP_HEADS)
    ]


def state_kernel(k_ref, v_ref, pick_ref, last_ref, out_ref):
    keys, last = k_ref[...], last_ref[...]
    ones = jnp.ones((16, keys.shape[0]), jnp.bfloat16)
    for head, n, lanes in step_heads():
        first, second = factors(own_lanes(keys, head), pick_ref, 0, last)
        phi = first * second
        state = mul(phi, v_ref[:, lanes], "tn")
        out_ref[n] = pack_state(state, mul(ones, phi)).astype(out_ref.dtype)


def causal_mask(seg_col_ref, seg_row_ref, mask_ref):
    rows = mask_ref.shape[0]
    i = lax.broadcasted_iota(jnp.int32, (rows, rows), 0)
    j = lax.broadcasted_iota(jnp.int32, (rows, rows), 1)
    keep = (seg_col_ref[...] == seg_row_ref[0:1, :]) & (j <= i)
    mask_ref[...] = keep.astype(jnp.float32).astype(jnp.bfloat16)


def triangle(rows):
    half = rows // 2
    return ((slice(0, half), slice(0, half)), (slice(half, rows), slice(0, rows)))


def local_kernel(q_ref, k_ref, v_ref, seg_col_ref, seg_row_ref, num_ref, den_ref, mask_ref):
    @pl.when(pl.program_id(0) == 0)
    def _():
        causal_mask(seg_col_ref, seg_row_ref, mask_ref)

    queries = q_ref[...]
    scaled = k_ref[...] * jnp.asarray(FEAT**-0.25, jnp.bfloat16)
    for head, _, lanes in step_heads():
        own_q = own_lanes(queries, head)
        value = v_ref[:, lanes]
        wide = jnp.concatenate([value, jnp.ones_like(value)], axis=1)
        for at, upto in triangle(own_q.shape[0]):
            up = 1.0 + mul(own_q[at], scaled[upto], "nt")
            kappa = (0.5 * up * up + 0.5).astype(jnp.bfloat16) * mask_ref[at, upto]
            both = mul(kappa, wide[upto])
            num_ref[at, lanes] = both[:, :HEAD_V]
            den_ref[at, lanes] = both[:, HEAD_V:]


def prefix_kernel(
    q_ref, num_ref, den_ref, state_ref, pick_ref, reading_ref, out_ref, inverse_ref
):
    queries, reading = q_ref[...], reading_ref[...]
    for head, n, lanes in step_heads():
        first, second = factors(own_lanes(queries, head), pick_ref, 1, reading)
        phi = first * second
        state, norm = widen(state_ref[n])
        num = num_ref[:, lanes] + mul(phi, state)
        norm = mul(phi, jnp.broadcast_to(norm, (HEAD_V, WIDE)), "nt")
        inverse = 1.0 / (den_ref[:, lanes] + norm)
        out_ref[:, lanes] = (num * inverse).astype(jnp.bfloat16)
        inverse_ref[:, lanes] = inverse


def scaled_grad(g_ref, att_ref, inverse_ref, lanes):
    gn = (g_ref[:, lanes].astype(jnp.float32) * inverse_ref[:, lanes]).astype(jnp.bfloat16)
    mixed = att_ref[:, lanes].astype(jnp.float32)
    gd = -jnp.sum(gn.astype(jnp.float32) * mixed, axis=1, keepdims=True)
    return gn, gd


def state_grad_kernel(q_ref, g_ref, att_ref, inverse_ref, pick_ref, reading_ref, out_ref):
    queries, reading = q_ref[...], reading_ref[...]
    for head, n, lanes in step_heads():
        gn, gd = scaled_grad(g_ref, att_ref, inverse_ref, lanes)
        first, second = factors(own_lanes(queries, head), pick_ref, 1, reading)
        phi = first * second
        state = mul(phi, gn, "tn")
        wide = jnp.broadcast_to(gd, gn.shape).astype(jnp.bfloat16)
        out_ref[n] = pack_state(state, mul(wide, phi, "tn")).astype(out_ref.dtype)


def chain(grad_phi, first, second, back_ref, which, head):
    both = jnp.concatenate([grad_phi * second, grad_phi * first], axis=1)
    grad = mul(both, back_ref[which], "nt")
    return jnp.where(head_lanes(head, grad_phi.shape[0]), grad, 0.0)


def local_grad_kernel(
    q_ref, k_ref, v_ref, g_ref, att_ref, inverse_ref, state_ref, pick_ref, back_ref,
    reading_ref, seg_col_ref, seg_row_ref, gq_ref, gk_ref, gv_ref, mask_ref, acc_ref,
):
    start = pl.program_id(0) * STEP_HEADS

    @pl.when(start == 0)
    def _():
        causal_mask(seg_col_ref, seg_row_ref, mask_ref)

    @pl.when(lax.rem(start, HALF_HEADS) == 0)
    def _():
        acc_ref[...] = jnp.zeros_like(acc_ref)
        gk_ref[...] = jnp.zeros_like(gk_ref)

    queries, keys, reading = q_ref[...], k_ref[...], reading_ref[...]
    half = queries.shape[0] // 2
    query_sums = jnp.zeros_like(acc_ref)
    key_sums = jnp.zeros_like(gk_ref)
    for head, n, lanes in step_heads():
        gn, gd = scaled_grad(g_ref, att_ref, inverse_ref, lanes)
        high = gd.astype(jnp.bfloat16).astype(jnp.float32)
        gn_wide = jnp.concatenate([gn, first_lanes(high, gd - high)], axis=1)
        ones = jnp.ones_like(gd)
        v_wide = jnp.concatenate([v_ref[:, lanes], first_lanes(ones, ones)], axis=1)
        own_q = own_lanes(queries, head)
        own_k = own_lanes(keys, head)
        parts, query_parts, key_parts = [], [], []
        for at, upto in triangle(own_q.shape[0]):
            keep = mask_ref[at, upto]
            up = 1.0 + mul(own_q[at], own_k[upto], "nt")
            kappa = (0.5 * up * up + 0.5).astype(jnp.bfloat16) * keep
            grad_t = mul(gn_wide[at], v_wide[upto], "nt").astype(jnp.bfloat16)
            grad_t = grad_t * up.astype(jnp.bfloat16) * keep
            query_parts.append(mul(grad_t, own_k[upto]))
            key_parts.append(mul(grad_t, own_q[at], "tn"))
            parts.append(mul(kappa, gn[at], "tn"))
        gv_ref[:half, lanes] = parts[0] + parts[1][:half]
        gv_ref[half:, lanes] = parts[1][half:]
        key_sums += key_parts[1] + jnp.concatenate(
            [key_parts[0], jnp.zeros_like(key_parts[0])], axis=0
        )
        first, second = factors(own_q, pick_ref, 1, reading)
        state, norm = widen(state_ref[n])
        grad_phi = mul(gn, state, "nt") + gd * norm.astype(jnp.float32)
        grad_phi = (grad_phi * reading).astype(jnp.bfloat16)
        query_sums += jnp.concatenate(query_parts, axis=0)
        query_sums += chain(grad_phi, first, second, back_ref, 1, head)
    acc_ref[...] += query_sums
    gk_ref[...] += key_sums

    @pl.when(lax.rem(start + STEP_HEADS, HALF_HEADS) == 0)
    def _():
        gq_ref[...] = (acc_ref[...] * FEAT**-0.25).astype(jnp.bfloat16)


def later_grad_kernel(
    k_ref, v_ref, gk_in_ref, gv_in_ref, state_ref, pick_ref, back_ref, last_ref,
    gk_ref, gv_ref, acc_ref,
):
    start = pl.program_id(0) * STEP_HEADS

    @pl.when(lax.rem(start, HALF_HEADS) == 0)
    def _():
        acc_ref[...] = gk_in_ref[...]

    keys, last = k_ref[...], last_ref[...]
    total = jnp.zeros_like(acc_ref)
    for head, n, lanes in step_heads():
        first, second = factors(own_lanes(keys, head), pick_ref, 0, last)
        state, norm = widen(state_ref[n])
        values = gv_in_ref[:, lanes] + mul(first * second, state)
        gv_ref[:, lanes] = values.astype(jnp.bfloat16)
        grad_phi = mul(v_ref[:, lanes], state, "nt") + norm.astype(jnp.float32)
        grad_phi = (grad_phi * last).astype(jnp.bfloat16)
        total = total + chain(grad_phi, first, second, back_ref, 0, head)
    acc_ref[...] += total

    @pl.when(lax.rem(start + STEP_HEADS, HALF_HEADS) == 0)
    def _():
        gk_ref[...] = (acc_ref[...] * FEAT**-0.25).astype(jnp.bfloat16)


def specs(rows):
    return dict(
        pair=pl.BlockSpec((rows, 128), lambda h: (0, h * STEP_HEADS // HALF_HEADS)),
        head=pl.BlockSpec((rows, STEP_HEADS * HEAD_V), lambda h: (0, h)),
        state=pl.BlockSpec((STEP_HEADS, STATE, HEAD_V), lambda h: (h, 0, 0)),
        pick=pl.BlockSpec((3, WIDE, WIDE), lambda h: (0, 0, 0)),
        back=pl.BlockSpec((2, 128, 2 * WIDE), lambda h: (0, 0, 0)),
        column=pl.BlockSpec((rows, 1), lambda h: (0, 0)),
        row=pl.BlockSpec((8, rows), lambda h: (0, 0)),
    )


def heads_call(kernel, rows, ins, outs, scratch=(), name=None):
    table = specs(rows)
    shapes = {
        "pair": (rows, HEADS * FEAT),
        "head": (rows, HEADS * HEAD_V),
        "state": (HEADS, STATE, HEAD_V),
    }
    return pl.pallas_call(
        kernel,
        grid=(HEADS // STEP_HEADS,),
        in_specs=[table[kind] for kind in ins],
        out_specs=[table[kind] for kind, _ in outs],
        out_shape=[jax.ShapeDtypeStruct(shapes[kind], kept) for kind, kept in outs],
        scratch_shapes=list(scratch),
        compiler_params=pltpu.CompilerParams(
            dimension_semantics=("arbitrary",), vmem_limit_bytes=48 * 2**20
        ),
        cost_estimate=pl.CostEstimate(flops=2**20, bytes_accessed=2**16, transcendentals=0),
        name=name,
    )


f32, bf = jnp.float32, jnp.bfloat16


def mix_state(k, v, tables, last):
    rows = k.shape[0]
    return heads_call(state_kernel, rows, ["pair", "head", "pick", "column"],
        [("state", bf)], name="mix_state")(k, v, tables[0], last)[0]


def mix_local(q, k, v, seg_col, seg_row):
    rows = k.shape[0]
    return heads_call(local_kernel, rows, ["pair", "pair", "head", "column", "row"],
        [("head", f32), ("head", f32)], [pltpu.VMEM((rows, rows), bf)], name="mix_local")(q, k, v, seg_col, seg_row)


def mix_prefix(q, num, den, state, tables, reading):
    rows = q.shape[0]
    return heads_call(prefix_kernel, rows, ["pair", "head", "head", "state", "pick", "column"],
        [("head", bf), ("head", f32)], name="mix_prefix")(q, num, den, state, tables[0], reading)


def mix_state_grad(q, g, att, inverse, tables, reading):
    rows = q.shape[0]
    return heads_call(state_grad_kernel, rows, ["pair", "head", "head", "head", "pick", "column"],
        [("state", bf)], name="mix_state_grad")(q, g, att, inverse, tables[0], reading)[0]


def mix_local_grad(q, k, v, g, att, inverse, state, tables, reading, seg_col, seg_row):
    rows = q.shape[0]
    return heads_call(local_grad_kernel, rows,
        ["pair", "pair", "head", "head", "head", "head", "state", "pick", "back", "column", "column", "row"],
        [("pair", bf), ("pair", f32), ("head", f32)],
        [pltpu.VMEM((rows, rows), bf), pltpu.VMEM((rows, 128), f32)], name="mix_local_grad")(
        q, k, v, g, att, inverse, state, *tables, reading, seg_col, seg_row)


def mix_later_grad(k, v, gk, gv, state, tables, last):
    rows = k.shape[0]
    return heads_call(later_grad_kernel, rows,
        ["pair", "head", "pair", "head", "state", "pick", "back", "column"],
        [("pair", bf), ("head", bf)], [pltpu.VMEM((rows, 128), f32)], name="mix_later_grad")(
        k, v, gk, gv, state, *tables, last)


from jax.sharding import PartitionSpec as P

D = 2048
EPSILON = 1e-05
LIMIT = 58 * 2**20
TILE = 352


def cost(flops, moved):
    return pl.CostEstimate(flops=flops, bytes_accessed=moved, transcendentals=0)


def whole(*shape):
    return pl.BlockSpec(shape, lambda *_: (0,) * len(shape), pipeline_mode=pl.Buffered(1))


def tiling(parts, rows):
    if parts == 1:
        taken = TILE if rows % TILE == 0 else rows
        return 1, taken, rows // taken
    taken = max(1, TILE // rows)
    taken = taken if parts % taken == 0 else parts
    return taken, rows, parts // taken


def gate_kernel(x_ref, c_ref, *refs):
    count = len(refs) // 3
    half = x_ref.shape[0] // 2
    for n in range(count):
        both_ref, down_ref, out_ref = refs[2 * n], refs[2 * n + 1], refs[2 * count + n]
        parts, _, rows, _ = both_ref.shape
        gate_w, up_w = [both_ref[:, k].reshape(parts * rows, D) for k in range(2)]
        down_w = down_ref[:, 0].reshape(parts * rows, D)
        for at in (slice(0, half), slice(half, 2 * half)):
            x, c = x_ref[at, :], c_ref[at, :]
            gate = mul(gate_w, x, "nt")
            up = mul(up_w, x, "nt")
            grad = mul(down_w, c, "nt").astype(bf).astype(f32)
            sig = 1.0 / (1.0 + jnp.exp(-gate))
            act = gate * sig
            out_ref[0, :, at] = (grad * up * sig * (1.0 + gate * (1.0 - sig))).astype(bf)
            out_ref[1, :, at] = (grad * act).astype(bf)
            out_ref[2, :, at] = (act * up).astype(bf)


def ffn_gates(x, c, weights):
    rows, count = x.shape[0], len(weights)
    hidden = weights[0][1].shape[0] * weights[0][1].shape[2]
    ins, outs = [whole(rows, D)] * 2, []
    for pair in weights:
        for w in pair:
            taken, height, steps = tiling(w.shape[0], w.shape[2])
            at = (lambda i: (0, 0, i, 0)) if w.shape[0] == 1 else (lambda i: (i, 0, 0, 0))
            ins.append(pl.BlockSpec((taken, w.shape[1], height, D), at))
        outs.append(pl.BlockSpec((3, taken * height, rows), lambda i: (0, i, 0)))
    return pl.pallas_call(
        gate_kernel,
        grid=(steps,),
        in_specs=ins,
        out_specs=outs,
        out_shape=[jax.ShapeDtypeStruct((3, hidden, rows), bf)] * count,
        compiler_params=pltpu.CompilerParams(vmem_limit_bytes=LIMIT),
        cost_estimate=cost(
            6 * rows * D * hidden * count,
            2 * (2 * rows * D + 3 * count * hidden * (D + rows)),
        ),
        name="ffn_gates",
    )(x, c, *[w for pair in weights for w in pair])


def back_kernel(count, *refs):
    made, weights, out_ref, turned = (
        refs[:count], refs[count : 2 * count], refs[-count - 1], refs[-count:]
    )
    added = refs[2 * count : -count - 1]

    @pl.when(pl.program_id(0) == 0)
    def _():
        for block, kept in zip(made, turned):
            kinds, hidden, rows = block.shape
            kept[...] = block[...].reshape(kinds * hidden, rows).T

    total = None
    for kept, w_ref in zip(turned, weights):
        parts, kinds, rows, columns = w_ref.shape
        right = jnp.concatenate(
            [w_ref[:, k].reshape(parts * rows, columns) for k in range(kinds)], axis=0
        )
        part = mul(kept[...], right)
        total = part if total is None else total + part
    for more in added:
        total = total + more[...].astype(f32)
    out_ref[...] = total.astype(out_ref.dtype)


def ffn_back(made, weights, which, added=(), columns=512):
    count = len(weights)
    weights = [pair[which] for pair in weights]
    kinds = weights[0].shape[1]
    _, hidden, rows = made[0].shape
    out = pl.BlockSpec((rows, columns), lambda j: (0, j))
    ins = [
        pl.BlockSpec(
            (kinds, hidden, rows), lambda j: (2 * which // kinds, 0, 0), pipeline_mode=pl.Buffered(1)
        )
    ] * count
    for w in weights:
        ins.append(pl.BlockSpec((w.shape[0], kinds, w.shape[2], columns), lambda j: (0, 0, 0, j)))
    ins += [out] * len(added)
    return pl.pallas_call(
        functools.partial(back_kernel, count),
        grid=(D // columns,),
        in_specs=ins,
        out_specs=out,
        out_shape=jax.ShapeDtypeStruct((rows, D), bf),
        scratch_shapes=[pltpu.VMEM((rows, kinds * hidden), bf)] * count,
        compiler_params=pltpu.CompilerParams(vmem_limit_bytes=LIMIT),
        cost_estimate=cost(
            2 * rows * D * hidden * kinds * count,
            2 * (count * kinds * hidden * (D + rows) + rows * D),
        ),
        name="ffn_back",
    )(*made, *weights, *added)


def grad_kernel(blocks, *refs):
    made, xs, cs = refs[:blocks], refs[blocks : 2 * blocks], refs[2 * blocks : 3 * blocks]
    added, out_ref = refs[3 * blocks : -1], refs[-1]
    parts, _, rows, _ = out_ref.shape

    def write(rights):
        total = None
        for left, right in zip(made, rights):
            part = mul(left[0], right[...])
            total = part if total is None else total + part
        for more in added:
            total = total + more[...].reshape(parts * rows, D).astype(f32)
        out_ref[...] = total.astype(bf).reshape(parts, 1, rows, D)

    kind = pl.program_id(0)

    @pl.when(kind < 2)
    def _():
        write(xs)

    @pl.when(kind == 2)
    def _():
        write(cs)


def ffn_grad(made, xs, cs, parts, height, added=None):
    blocks = len(made)
    rows = xs[0].shape[0]
    hidden = made[0].shape[1]
    taken, rise, steps = tiling(parts, height)
    left = pl.BlockSpec((1, taken * rise, rows), lambda k, i: (k, i, 0))
    at = (lambda k, i: (0, k, i, 0)) if parts == 1 else (lambda k, i: (i, k, 0, 0))
    out = pl.BlockSpec((taken, 1, rise, D), at)
    more = [] if added is None else [added]
    return pl.pallas_call(
        functools.partial(grad_kernel, blocks),
        grid=(3, steps),
        in_specs=[left] * blocks + [whole(rows, D)] * (2 * blocks) + [out] * len(more),
        out_specs=out,
        out_shape=jax.ShapeDtypeStruct((parts, 3, height, D), bf),
        compiler_params=pltpu.CompilerParams(vmem_limit_bytes=LIMIT),
        cost_estimate=cost(
            6 * rows * D * hidden * blocks,
            2 * (2 * blocks * rows * D + 3 * hidden * (rows * blocks + D * (1 + len(more)))),
        ),
        name="ffn_grad",
    )(*made, *xs, *cs, *more)


def widen_kernel(sum_ref, *out_refs):
    for kind, out_ref in enumerate(out_refs):
        out_ref[...] = sum_ref[0, kind].astype(f32)


def widened(sums):
    parts, _, height, _ = sums.shape
    return pl.pallas_call(
        widen_kernel,
        grid=(parts,),
        in_specs=[pl.BlockSpec((1, 3, height, D), lambda i: (i, 0, 0, 0))],
        out_specs=[pl.BlockSpec((height, D), lambda i: (i, 0))] * 3,
        out_shape=[jax.ShapeDtypeStruct((parts * height, D), f32)] * 3,
        compiler_params=pltpu.CompilerParams(vmem_limit_bytes=LIMIT),
        cost_estimate=cost(0, 6 * parts * 3 * height * D),
        name="widened",
    )(sums)


def qkv_grad_kernel(n_ref, gq_ref, gk_ref, gv_ref, out_ref):
    turned = n_ref[...].T
    qk = gq_ref.shape[1]
    out_ref[:, :qk] = mul(turned, gq_ref[...]).astype(bf)
    out_ref[:, qk : 2 * qk] = mul(turned, gk_ref[...]).astype(bf)
    out_ref[:, 2 * qk :] = mul(turned, gv_ref[...]).astype(bf)


def qkv_grad(normed, gq, gk, gv):
    rows, qk = gq.shape
    columns = 2 * qk + D
    tile = 256
    return pl.pallas_call(
        qkv_grad_kernel,
        grid=(D // tile,),
        in_specs=[
            pl.BlockSpec((rows, tile), lambda i: (0, i)), whole(rows, qk), whole(rows, qk), whole(rows, D)
        ],
        out_specs=pl.BlockSpec((tile, columns), lambda i: (i, 0)),
        out_shape=jax.ShapeDtypeStruct((D, columns), bf),
        compiler_params=pltpu.CompilerParams(vmem_limit_bytes=LIMIT),
        cost_estimate=cost(2 * rows * D * columns, 2 * (rows * (D + columns) + D * columns)),
        name="qkv_grad",
    )(normed, gq, gk, gv)


def norm_forward(inputs):
    inverse = lax.rsqrt(jnp.mean(inputs * inputs, axis=-1, keepdims=True) + EPSILON)
    return (inputs * inverse, inverse)


def norm_backward(grad_normed, unit_rows, inverse, gain_vec):
    gain_grad = jnp.sum(grad_normed * unit_rows, axis=0)
    grad_unit = grad_normed * gain_vec
    return (
        inverse * (grad_unit - unit_rows * jnp.mean(grad_unit * unit_rows, axis=-1, keepdims=True)),
        gain_grad,
    )


def move(array, target, axis="mp"):
    size = lax.axis_size(axis)
    pairs = [(m, target(m)) for m in range(size)]
    return lax.ppermute(array, axis, [(m, t) for m, t in pairs if t is not None])


def then(value, *before):
    return lax.optimization_barrier((value, before))[0]


def beside(array, mover, *works):
    ends = [array.shape[0] * n // len(works) // 16 * 16 for n in range(len(works))] + [array.shape[0]]
    moved, made = [], []
    for n, work in enumerate(works):
        share = array[ends[n] : ends[n + 1]]
        if made:
            share = then(share, made[-1])
        result = work(share, made)
        arrived, result = lax.optimization_barrier((mover(share), result))
        moved.append(arrived)
        made.append(result)
    return jnp.concatenate(moved, axis=0), made


def to_mate(array):
    return move(array, lambda m: m ^ 1)


def to_half(array):
    size = lax.axis_size("mp")
    return move(array, lambda m: (m + size // 2) % size)


def to_peer(array, step):
    half = lax.axis_size("mp") // 2

    def target(m):
        low = m % half
        return m - low + (low + 2 * step) % half

    return move(array, target)


def to_chip(array, step):
    size = lax.axis_size("mp")
    return move(array, lambda m: m + 2 * step if 0 <= m + 2 * step < size else None)


def sums_before(own, sign, *beside, made=None):
    core = lax.axis_index("mp") % 2
    chips = lax.axis_size("mp") // 2
    wire = own.astype(bf)
    mate = to_mate(wire).astype(f32)
    half = own.shape[0] // 2
    both = wire.astype(f32) + mate
    running = lax.dynamic_slice_in_dim(both, core * half, half, 0)
    before = jnp.zeros_like(running)
    step, beside, made = 1, list(beside), [] if made is None else made
    while step < chips:
        came = to_chip(running.astype(bf), sign * step)
        if beside:
            came, result = lax.optimization_barrier((came, beside.pop(0)(running)))
            made.append(result)
        came = came.astype(f32)
        before = before + came
        running = running + came
        step *= 2
    before = before.astype(bf)
    other = to_mate(before)
    first = jnp.where(core == 0, before, other)
    second = jnp.where(core == 0, other, before)
    total = jnp.concatenate([first, second], axis=0).astype(f32)
    inner = core == (1 if sign > 0 else 0)
    return (total + jnp.where(inner, mate, 0.0)).astype(bf), made


def pick(array, index, dim=0):
    return lax.dynamic_index_in_dim(array, index, dim, keepdims=False)


def chip_halves(array):
    groups, size = lax.axis_size("dp"), lax.axis_size("mp")
    core = lax.axis_index("mp") % 2
    rows, columns = array.shape[0] // (groups * size), array.shape[1]
    blocks = array.reshape(groups, size // 2, 2, rows, columns)
    return pick(blocks, core, 2), pick(blocks, 1 - core, 2)


def add(first, *more, kept=bf):
    total = first.astype(f32)
    for array in more:
        total = total + array.astype(f32)
    return total.astype(kept)


def placed(shares, places):
    out = jnp.zeros((len(shares),) + shares[0].shape, shares[0].dtype)
    for share, at in zip(shares, places):
        out = lax.dynamic_update_index_in_dim(out, share, at, 0)
    return out


def chip_shares(array):
    steps = range(1, lax.axis_size("mp") // 2)
    return [move(array, lambda m: m ^ (2 * step)) for step in steps]


def by_chip(array, shares):
    chip = lax.axis_index("mp") // 2
    return placed([array] + shares, [chip ^ step for step in range(len(shares) + 1)])


def first_groups(array):
    return [move(array, lambda m: m ^ step, "dp") for step in (1, 2)]


def third_group(first, second):
    half = first.shape[0] // 2
    return [
        move(second[:half], lambda m: m ^ 1, "dp"),
        move(first[half:], lambda m: m ^ 2, "dp"),
    ]


def assembled(pieces, groups, chips, out=None):
    group, core = lax.axis_index("dp"), lax.axis_index("mp") % 2
    shape = pieces[0][2].shape[1:]
    if out is None:
        out = jnp.zeros((groups, chips, 2) + shape, bf)
    for step, at, own, other in pieces:
        both = jnp.where(core == 0, jnp.stack([own, other], 1), jnp.stack([other, own], 1))
        start = (group ^ step, at) + (0,) * (len(shape) + 1)
        out = lax.dynamic_update_slice(out, both[None], start)
    return out


def group_move(array, step):
    return move(pick(array, lax.axis_index("dp") ^ step), lambda m: m ^ step, "dp")


def chip_moves(array):
    chip = lax.axis_index("mp") // 2
    return [
        move(pick(array, chip ^ step), lambda m: m ^ (2 * step))
        for step in range(1, lax.axis_size("mp") // 2)
    ]


def sum_everywhere(array):
    for axis in ("mp", "dp"):
        step = 1
        while step < lax.axis_size(axis):
            array = array + move(array, lambda m: m ^ step, axis)
            step *= 2
    return array


def body(
    x_in,
    seq_lengths,
    norm1_gain,
    w_query,
    w_key,
    w_value,
    w_out,
    norm2_gain,
    w_gate,
    w_up,
    w_down,
    cotangent,
):
    rows = x_in.shape[0]
    groups = lax.axis_size("dp")
    size = lax.axis_size("mp")
    peers = size // 4
    hidden = w_gate.shape[1]
    piece = hidden // groups
    place = lax.axis_index("mp")
    group = lax.axis_index("dp")
    everywhere = ("dp", "mp")
    qk = w_query.shape[1]
    aligned = piece % 16 == 0

    own_rows = w_query.shape[0]
    gain_block = jnp.concatenate(
        [norm1_gain[:, None], norm2_gain[:, None], jnp.zeros((own_rows, 126), bf)], axis=1
    )
    packed = jnp.concatenate([w_query, w_key, w_value, gain_block], axis=1)
    in_chips, packed = lax.optimization_barrier((chip_shares(packed), packed))
    in_chips = by_chip(packed, in_chips)

    full_out = lax.all_gather(w_out, everywhere, axis=0, tiled=True)
    half_chips = size // 4
    mine_both = jnp.concatenate(then([w_gate.T, w_up.T], in_chips), axis=0)
    mine = (mine_both.reshape(1, 2, hidden, D), then(w_down, in_chips).reshape(1, 1, hidden, D))
    far_down = lax.dynamic_slice_in_dim(mine[1][0, 0], group * piece, piece, 0)
    far_both = lax.dynamic_slice_in_dim(mine[0][0], group * piece, piece, 1).reshape(2 * piece, D)
    cot_ends = [rows * n // 16 for n in (0, 3, 6, 10, 13, 16)]
    cot_shares = [cotangent[a:b] for a, b in zip(cot_ends, cot_ends[1:])]

    def peers_of(array):
        return [to_peer(array, step) for step in range(1, peers)]

    def beside_one(array, mover, work):
        return lax.optimization_barrier((mover(array), work(array)))

    both_cut, down_cut = 2 * piece * 8 // 11, piece * 7 // 11
    in_near, in_mate, both_first = lax.optimization_barrier(
        (
            first_groups(in_chips),
            to_mate(in_chips),
            to_half(then(far_both[:both_cut], in_chips)),
        )
    )
    in_third, in_mates, both_second = lax.optimization_barrier(
        (
            third_group(*in_near),
            [to_mate(share) for share in in_near],
            to_half(then(far_both[both_cut:], in_near)),
        )
    )
    in_mates = [in_mate, *in_mates] + [to_mate(share) for share in in_third]
    far_both = jnp.concatenate([both_first, both_second], axis=0)
    far_both = lax.all_gather(far_both, "dp", axis=0, tiled=True).reshape(groups, 2, piece, D)
    down_first = to_half(then(far_down[:down_cut], in_third))
    mate_down = to_mate(then(mine[1], in_third))
    cot_third = peers_of(then(cot_shares[2], in_third))
    in_pieces = [
        (step, at, own, other)
        for (step, at, own), other in zip(
            (
                (0, 0, in_chips),
                (1, 0, in_near[0]),
                (2, 0, in_near[1]),
                (3, 0, in_third[0]),
                (3, half_chips, in_third[1]),
            ),
            in_mates,
        )
    ]
    full_in = assembled(in_pieces, groups, size // 2).reshape(D, packed.shape[1])

    row_start = place * rows
    seq_ends = jnp.cumsum(seq_lengths[0], dtype=jnp.int32)
    positions = row_start + jnp.arange(rows, dtype=jnp.int32)
    segments = jnp.sum((positions[:, None] >= seq_ends[None, :]).astype(jnp.int32), axis=1)
    seg_before = jnp.sum((row_start - 1 >= seq_ends).astype(jnp.int32))
    reading = ((segments == seg_before) & (row_start > 0)).astype(f32)[:, None]
    last_doc = (segments == segments[-1]).astype(f32)[:, None]
    seg_col = segments[:, None]
    seg_row = jnp.broadcast_to(segments[None, :], (8, rows))
    tables = feature_tables()

    inputs = x_in.astype(f32)
    inverse_one = norm_forward(inputs)[1]
    early = (full_out, mine, down_first, mate_down, cot_third, inverse_one, reading, last_doc, seg_col, seg_row)
    full_in, early = lax.optimization_barrier((full_in, early))
    full_out, mine, down_first, mate_down, cot_third, inverse_one, reading, last_doc, seg_col, seg_row = early
    gain_one = full_in[:, 2 * qk + D].astype(f32)
    gain_two = full_in[:, 2 * qk + D + 1].astype(f32)
    full_qkv = full_in[:, : 2 * qk + D]
    unit_one = inputs * inverse_one
    normed_one = (unit_one * gain_one).astype(bf)
    (got, mate_gate, down_second), qkv = beside_one(
        then(cot_shares[3], full_in),
        lambda ready: (
            peers_of(ready),
            to_mate(then(mine[0][:, :1], ready)),
            to_half(then(far_down[down_cut:], ready)),
        ),
        lambda ready: mul(then(normed_one, ready), full_qkv).astype(bf),
    )
    cot_got = [cot_third, got]
    queries, keys, values = qkv[:, :qk], qkv[:, qk : 2 * qk], qkv[:, 2 * qk :]
    far_down = jnp.concatenate([down_first, down_second], axis=0)
    far_down = lax.all_gather(far_down, "dp", axis=0, tiled=True).reshape(groups, 1, piece, D)
    (got, mate_up), own_state = beside_one(
        then(cot_shares[4], qkv),
        lambda ready: (peers_of(ready), to_mate(then(mine[0][:, 1:], ready))),
        lambda ready: mix_state(then(keys, ready), values, tables, last_doc),
    )
    cot_got.append(got)

    def local_work(ready):
        local = mix_local(then(queries, ready), keys, values, seg_col, seg_row)
        return local

    def pack_work(ready):
        gate, up = then((mate_gate, mate_up), ready)
        return jnp.concatenate([gate, up], axis=1)

    prefix, [(num, den), mate_both] = sums_before(own_state, 1, local_work, pack_work)
    cot_first, (attended, inverse_den) = beside_one(
        then(cot_shares[0], prefix),
        peers_of,
        lambda ready: mix_prefix(then(queries, ready), num, den, prefix, tables, reading),
    )
    mate = (mate_both, mate_down)
    near = [mine, mate]
    cot_second, hidden_in = beside_one(
        then(cot_shares[1], attended),
        peers_of,
        lambda ready: inputs + mul(then(attended, ready), full_out),
    )
    cot_got = [cot_first, cot_second] + cot_got
    unit_two, inverse_two = norm_forward(hidden_in)
    normed_two = (unit_two * gain_two).astype(bf)
    came = [to_peer(normed_two, step) for step in range(1, peers)]

    near_own = ffn_gates(normed_two, cotangent, near)
    far_mine = then((far_both, far_down), normed_two)
    if not aligned:
        far_mine = tuple(jnp.swapaxes(w, 0, 1).reshape(1, -1, hidden, D) for w in far_mine)
    far_mate = then(tuple(to_mate(w) for w in far_mine), near_own)
    far = [tuple(far_mine), far_mate]
    weights = near + far
    shape = (groups, piece) if aligned else (1, hidden)
    far_own = ffn_gates(normed_two, cotangent, far)
    made_own = list(near_own) + list(far_own)
    grad_own = ffn_back(made_own, weights, 0)
    normed = [normed_two] + then(came, grad_own)
    cot_got = then(cot_got, near_own)
    cots = [cotangent] + [jnp.concatenate(parts, axis=0) for parts in zip(*cot_got)]
    near_made = [near_own] + [ffn_gates(x, c, near) for x, c in zip(normed[1:], cots[1:])]
    far_made = [far_own] + [
        ffn_gates(x, c, then(far, near_made)) for x, c in zip(normed[1:], cots[1:])
    ]
    made = [list(a) + list(b) for a, b in zip(near_made, far_made)]

    def weight_grads(made, ready, added=None):
        return ffn_grad(then(made, ready), normed, cots, *shape, added)

    def over_groups(grad):
        if not aligned:
            grad = jnp.swapaxes(grad.reshape(3, groups, piece, D), 0, 1)
        return lax.psum_scatter(
            grad.reshape(groups * 3 * piece, D), "dp", scatter_dimension=0, tiled=True
        )

    def back(block, which, ready):
        return ffn_back(then(block, ready), weights, which)

    far_given = weight_grads([block[1] for block in far_made], far_made)
    far_sent = to_mate(far_given)
    grad_parts = [back(block, 0, far_given) for block in made[1:]]

    def owners(parts):
        return [to_peer(part, peers - step) for step, part in enumerate(parts, 1)]

    def stacked(parts):
        return jnp.concatenate([part[:, None] for part in parts], axis=1)

    def to_owners(parts):
        return stacked(owners([parts[:, n] for n in range(peers - 1)]))

    def near_work(ready, _):
        given = weight_grads([block[1] for block in near_made], ready)
        return given

    def far_work(ready, done):
        kept = weight_grads([block[0] for block in far_made], ready, far_sent)
        return kept, to_mate(then(done[0], ready))

    def last_work(ready, done):
        return weight_grads([block[0] for block in near_made], ready, done[1][1])

    grad_sent, (_, (far_kept, _), near_kept) = beside(
        stacked(grad_parts), to_owners, near_work, far_work, last_work
    )
    far_part = over_groups(far_kept)
    near_part = over_groups(near_kept)
    grad_normed_two = jnp.sum(grad_sent.astype(f32), axis=1) + grad_own.astype(f32)

    grad_two, gain_two_grad = norm_backward(grad_normed_two, unit_two, inverse_two, gain_two)
    grad_hidden_in = cotangent.astype(f32) + grad_two
    grad_branch = grad_hidden_in.astype(bf)
    grad_attended = mul(grad_branch, full_out, "nt").astype(bf)
    state_grad = mix_state_grad(queries, grad_attended, attended, inverse_den, tables, reading)

    def local_grads(ready):
        local = mix_local_grad(
            then(queries, ready), keys, values, grad_attended, attended, inverse_den, prefix, tables,
            reading, seg_col, seg_row,
        )
        return local, to_mate(then(out_halves[1], ready))

    out_halves = []

    def out_work(ready):
        halves = chip_halves(mul(then(attended, ready), grad_branch, "tn").astype(bf))
        out_halves.extend(halves)
        return halves

    later, [_, (local, out_came)] = sums_before(state_grad, -1, out_work, local_grads)
    grad_queries, part_keys, part_values = local
    out_kept = add(out_halves[0], out_came)
    out_kept, far_part = then((out_kept, far_part), later)
    ends = [far_part.shape[0] * n // 33 for n in (0, 3, 9, 16, 22, 33)]
    far_shares = [far_part[a:b] for a, b in zip(ends, ends[1:])]
    out_first, out_second, out_diag = [pick(out_kept, group ^ step) for step in range(1, groups)]
    low, high = slice(None, half_chips), slice(half_chips, None)

    def by_first(block):
        return move(block, lambda m: m ^ 1, "dp")

    def by_second(block):
        return move(block, lambda m: m ^ 2, "dp")

    (far_first, for_second, for_first), (grad_keys, grad_values) = beside_one(
        then(far_shares[0], out_kept),
        lambda ready: (
            to_half(ready), by_first(then(out_diag[low], ready)), by_second(then(out_diag[high], ready))
        ),
        lambda ready: mix_later_grad(
            then(keys, ready), values, part_keys, part_values, later, tables, last_doc
        ),
    )
    out_second = [add(out_second[low], for_second), out_second[high]]
    out_first = [out_first[low], add(out_first[high], for_first)]
    (out_low, far_slot), in_grad = beside_one(
        then((out_first[0], out_second[0]), grad_keys),
        lambda ready: (
            [by_first(ready[0]), by_second(ready[1])], to_half(then(far_shares[1], ready))
        ),
        lambda ready: qkv_grad(then(normed_one, ready), grad_queries, grad_keys, grad_values),
    )
    in_keep, in_give = chip_halves(in_grad)
    in_came, out_high, far_second = lax.optimization_barrier(
        (
            to_mate(in_give),
            [by_first(then(out_first[1], in_grad)), by_second(then(out_second[1], in_grad))],
            to_half(then(far_shares[2], in_grad)),
        )
    )
    in_diag = add(pick(in_keep, group ^ 3), pick(in_came, group ^ 3))
    in_first, in_second = [
        add(pick(in_keep, group ^ step), pick(in_came, group ^ step)) for step in (1, 2)
    ]
    grad_queries, grad_keys, grad_values = then(
        (grad_queries, grad_keys, grad_values), (in_diag, in_first, in_second)
    )
    grad_normed_one = (
        mul(grad_queries, full_qkv[:, :qk], "nt")
        + mul(grad_keys, full_qkv[:, qk : 2 * qk], "nt")
        + mul(grad_values, full_qkv[:, 2 * qk :], "nt")
    )
    for_second, for_first, far_third, grad_normed_one, in_first, in_second = (
        lax.optimization_barrier(
            (
                by_first(in_diag[low]),
                by_second(in_diag[high]),
                to_half(then(far_shares[3], in_diag)),
                grad_normed_one,
                in_first,
                in_second,
            )
        )
    )
    in_first = jnp.concatenate([in_first[low], add(in_first[high], for_first)], axis=0)
    in_second = jnp.concatenate([add(in_second[low], for_second), in_second[high]], axis=0)
    in_moved = [by_first(in_first), by_second(in_second)]
    far_last = to_half(then(far_shares[4], in_first))
    grad_normed_one = then(grad_normed_one, (in_first, in_second))
    grad_one, gain_one_grad = norm_backward(grad_normed_one, unit_one, inverse_one, gain_one)
    input_grad = (grad_hidden_in + grad_one).astype(bf)
    out_parts = [back(block, 1, (in_first, in_second)) for block in made[1:]]
    out_parts, input_grad, gain_one_grad, in_moved, far_last = lax.optimization_barrier(
        (out_parts, input_grad, gain_one_grad, in_moved, far_last)
    )
    out_own = back(made[0], 1, in_moved)
    far_sum = jnp.concatenate([far_first, far_slot, far_second, far_third, far_last], axis=0)
    ffn_sum = lax.all_gather(add(near_part, far_sum), "dp", axis=0, tiled=True)
    ffn_sum = ffn_sum.reshape(groups, 3, piece, D)
    chip = place // 2

    def over_chips(blocks, kept):
        shares = [
            add(*[pick(block, chip ^ step) for block in blocks]) for step in range(1, size // 2)
        ]
        moved = [move(share, lambda m: m ^ (2 * step)) for step, share in enumerate(shares, 1)]
        return add(*[pick(block, chip) for block in blocks], *moved, kept=kept)

    in_sum = over_chips([pick(in_keep, group), pick(in_came, group), *in_moved], f32)
    out_blocks = [jnp.concatenate(pair, axis=0) for pair in zip(out_low, out_high)]
    out_blocks = then([pick(out_kept, group), *out_blocks], in_moved)
    out_sum = over_chips(out_blocks, f32)
    if not aligned:
        ffn_sum = jnp.swapaxes(ffn_sum, 0, 1).reshape(1, 3, hidden, D)
    gate_grad, up_grad, down_grad = widened(ffn_sum)
    gain_sums = sum_everywhere(jnp.stack([gain_one_grad, gain_two_grad]))
    gain_sums = lax.dynamic_slice_in_dim(
        gain_sums, (group * size + place) * own_rows, own_rows, 1
    )
    out_sent = to_owners(then(stacked(out_parts), in_sum, gain_sums))
    output = (hidden_in + jnp.sum(out_sent.astype(f32), axis=1) + out_own.astype(f32)).astype(bf)
    return (
        output,
        input_grad,
        gain_sums[0],
        in_sum[:, :qk],
        in_sum[:, qk : 2 * qk],
        in_sum[:, 2 * qk :],
        out_sum,
        gain_sums[1],
        gate_grad.T,
        up_grad.T,
        down_grad,
    )


def solution(mesh):
    rows, vector = P(("dp", "mp"), None), P(("dp", "mp"))
    columns, down = P(None, "mp"), P("mp", None)
    return jax.shard_map(
        body,
        mesh=mesh,
        in_specs=(rows, P("dp", None), vector, rows, rows, rows, rows, vector, columns, columns, down, rows),
        out_specs=(rows, rows, vector, rows, rows, rows, rows, vector, columns, columns, down),
        check_vma=False,
    )
```

```python
import functools
import numpy as np
import jax
import jax.numpy as jnp
from jax import lax
from jax.experimental import pallas as pl
from jax.experimental.pallas import tpu as pltpu

HEADS = 16
FEAT = 16
HEAD_V = 128
WIDE = 256
STATE = 160
SQUARES = FEAT * (FEAT + 1) // 2
LINEAR = SQUARES + FEAT
HALF_HEADS = 128 // FEAT
STEP_HEADS = 8


def feature_tables():
    pairs = [(a, b) for a in range(FEAT) for b in range(a, FEAT)]
    pick = np.zeros((3, WIDE, WIDE), np.float32)
    for row in range(128):
        for entry, (a, b) in enumerate(pairs):
            if row % FEAT == a:
                pick[0, row, entry] = 1.0
                pick[1, row, entry] = 0.5 if a == b else 1.0
            if row % FEAT == b:
                pick[2, row, entry] = 1.0
        pick[0:2, row, SQUARES + row % FEAT] = 1.0
    pick[0:2, 128, LINEAR] = 1.0
    pick[2, 128, SQUARES : LINEAR + 1] = 1.0
    back = np.stack([np.concatenate([pick[n, :128], pick[2, :128]], axis=1) for n in (0, 1)])
    return jnp.asarray(pick, jnp.bfloat16), jnp.asarray(back, jnp.bfloat16)


def mul(left, right, kind="nn"):
    dims = {"nn": ((1,), (0,)), "nt": ((1,), (1,)), "tn": ((0,), (0,))}[kind]
    return lax.dot_general(left, right, (dims, ((), ())), preferred_element_type=jnp.float32)


def head_lanes(head, rows):
    lane = lax.broadcasted_iota(jnp.int32, (rows, 128), 1)
    return lane // FEAT == lax.rem(head, HALF_HEADS)


def own_lanes(block, head):
    scaled = block * jnp.asarray(FEAT**-0.25, jnp.bfloat16)
    return jnp.where(head_lanes(head, block.shape[0]), scaled, jnp.zeros_like(scaled))


def first_lanes(*columns):
    lane = lax.broadcasted_iota(jnp.int32, (columns[0].shape[0], 128), 1)
    out = jnp.zeros(lane.shape, jnp.float32)
    for n, column in enumerate(columns):
        out = jnp.where(lane == n, column, out)
    return out.astype(jnp.bfloat16)


def factors(own, pick_ref, which, kept):
    ones = first_lanes(jnp.ones_like(kept))
    plain = jnp.concatenate([own, ones], axis=1)
    masked = jnp.concatenate(
        [own * kept.astype(jnp.bfloat16), ones * kept.astype(jnp.bfloat16)], axis=1
    )
    first = mul(masked, pick_ref[which]).astype(jnp.bfloat16)
    second = mul(plain, pick_ref[2]).astype(jnp.bfloat16)
    return first, second


def pack_state(state, norm_rows):
    row = lax.broadcasted_iota(jnp.int32, (STATE, HEAD_V), 0)
    out = jnp.where(row == LINEAR + 1, norm_rows[0:1, :HEAD_V], state[:STATE])
    return jnp.where(row == LINEAR + 2, norm_rows[0:1, HEAD_V:], out)


def widen(packed):
    padded = jnp.concatenate([packed, jnp.zeros((WIDE - STATE, HEAD_V), packed.dtype)], axis=0)
    norm = jnp.concatenate(
        [packed[LINEAR + 1 : LINEAR + 2, :], packed[LINEAR + 2 : LINEAR + 3, :]], axis=1
    )
    return padded, norm


def step_heads():
    first = pl.program_id(0) * STEP_HEADS
    return [
        (first + n, n, slice(n * HEAD_V, (n + 1) * HEAD_V)) for n in range(STEP_HEADS)
    ]


def state_kernel(k_ref, v_ref, pick_ref, last_ref, out_ref):
    keys, last = k_ref[...], last_ref[...]
    ones = jnp.ones((16, keys.shape[0]), jnp.bfloat16)
    for head, n, lanes in step_heads():
        first, second = factors(own_lanes(keys, head), pick_ref, 0, last)
        phi = first * second
        state = mul(phi, v_ref[:, lanes], "tn")
        out_ref[n] = pack_state(state, mul(ones, phi)).astype(out_ref.dtype)


def causal_mask(seg_col_ref, seg_row_ref, mask_ref):
    rows = mask_ref.shape[0]
    i = lax.broadcasted_iota(jnp.int32, (rows, rows), 0)
    j = lax.broadcasted_iota(jnp.int32, (rows, rows), 1)
    keep = (seg_col_ref[...] == seg_row_ref[0:1, :]) & (j <= i)
    mask_ref[...] = keep.astype(jnp.float32).astype(jnp.bfloat16)


def triangle(rows):
    half = rows // 2
    return ((slice(0, half), slice(0, half)), (slice(half, rows), slice(0, rows)))


def local_kernel(q_ref, k_ref, v_ref, seg_col_ref, seg_row_ref, num_ref, den_ref, mask_ref):
    @pl.when(pl.program_id(0) == 0)
    def _():
        causal_mask(seg_col_ref, seg_row_ref, mask_ref)

    queries = q_ref[...]
    scaled = k_ref[...] * jnp.asarray(FEAT**-0.25, jnp.bfloat16)
    for head, _, lanes in step_heads():
        own_q = own_lanes(queries, head)
        value = v_ref[:, lanes]
        wide = jnp.concatenate([value, jnp.ones_like(value)], axis=1)
        for at, upto in triangle(own_q.shape[0]):
            up = 1.0 + mul(own_q[at], scaled[upto], "nt")
            kappa = (0.5 * up * up + 0.5).astype(jnp.bfloat16) * mask_ref[at, upto]
            both = mul(kappa, wide[upto])
            num_ref[at, lanes] = both[:, :HEAD_V]
            den_ref[at, lanes] = both[:, HEAD_V:]


def prefix_kernel(
    q_ref, num_ref, den_ref, state_ref, pick_ref, reading_ref, out_ref, inverse_ref
):
    queries, reading = q_ref[...], reading_ref[...]
    for head, n, lanes in step_heads():
        first, second = factors(own_lanes(queries, head), pick_ref, 1, reading)
        phi = first * second
        state, norm = widen(state_ref[n])
        num = num_ref[:, lanes] + mul(phi, state)
        norm = mul(phi, jnp.broadcast_to(norm, (HEAD_V, WIDE)), "nt")
        inverse = 1.0 / (den_ref[:, lanes] + norm)
        out_ref[:, lanes] = (num * inverse).astype(jnp.bfloat16)
        inverse_ref[:, lanes] = inverse


def scaled_grad(g_ref, att_ref, inverse_ref, lanes):
    gn = (g_ref[:, lanes].astype(jnp.float32) * inverse_ref[:, lanes]).astype(jnp.bfloat16)
    mixed = att_ref[:, lanes].astype(jnp.float32)
    gd = -jnp.sum(gn.astype(jnp.float32) * mixed, axis=1, keepdims=True)
    return gn, gd


def state_grad_kernel(q_ref, g_ref, att_ref, inverse_ref, pick_ref, reading_ref, out_ref):
    queries, reading = q_ref[...], reading_ref[...]
    for head, n, lanes in step_heads():
        gn, gd = scaled_grad(g_ref, att_ref, inverse_ref, lanes)
        first, second = factors(own_lanes(queries, head), pick_ref, 1, reading)
        phi = first * second
        state = mul(phi, gn, "tn")
        wide = jnp.broadcast_to(gd, gn.shape).astype(jnp.bfloat16)
        out_ref[n] = pack_state(state, mul(wide, phi, "tn")).astype(out_ref.dtype)


def chain(grad_phi, first, second, back_ref, which, head):
    both = jnp.concatenate([grad_phi * second, grad_phi * first], axis=1)
    grad = mul(both, back_ref[which], "nt")
    return jnp.where(head_lanes(head, grad_phi.shape[0]), grad, 0.0)


def local_grad_kernel(
    q_ref, k_ref, v_ref, g_ref, att_ref, inverse_ref, state_ref, pick_ref, back_ref,
    reading_ref, seg_col_ref, seg_row_ref, gq_ref, gk_ref, gv_ref, mask_ref, acc_ref,
):
    start = pl.program_id(0) * STEP_HEADS

    @pl.when(start == 0)
    def _():
        causal_mask(seg_col_ref, seg_row_ref, mask_ref)

    @pl.when(lax.rem(start, HALF_HEADS) == 0)
    def _():
        acc_ref[...] = jnp.zeros_like(acc_ref)
        gk_ref[...] = jnp.zeros_like(gk_ref)

    queries, keys, reading = q_ref[...], k_ref[...], reading_ref[...]
    half = queries.shape[0] // 2
    query_sums = jnp.zeros_like(acc_ref)
    key_sums = jnp.zeros_like(gk_ref)
    for head, n, lanes in step_heads():
        gn, gd = scaled_grad(g_ref, att_ref, inverse_ref, lanes)
        high = gd.astype(jnp.bfloat16).astype(jnp.float32)
        gn_wide = jnp.concatenate([gn, first_lanes(high, gd - high)], axis=1)
        ones = jnp.ones_like(gd)
        v_wide = jnp.concatenate([v_ref[:, lanes], first_lanes(ones, ones)], axis=1)
        own_q = own_lanes(queries, head)
        own_k = own_lanes(keys, head)
        parts, query_parts, key_parts = [], [], []
        for at, upto in triangle(own_q.shape[0]):
            keep = mask_ref[at, upto]
            up = 1.0 + mul(own_q[at], own_k[upto], "nt")
            kappa = (0.5 * up * up + 0.5).astype(jnp.bfloat16) * keep
            grad_t = mul(gn_wide[at], v_wide[upto], "nt").astype(jnp.bfloat16)
            grad_t = grad_t * up.astype(jnp.bfloat16) * keep
            query_parts.append(mul(grad_t, own_k[upto]))
            key_parts.append(mul(grad_t, own_q[at], "tn"))
            parts.append(mul(kappa, gn[at], "tn"))
        gv_ref[:half, lanes] = parts[0] + parts[1][:half]
        gv_ref[half:, lanes] = parts[1][half:]
        key_sums += key_parts[1] + jnp.concatenate(
            [key_parts[0], jnp.zeros_like(key_parts[0])], axis=0
        )
        first, second = factors(own_q, pick_ref, 1, reading)
        state, norm = widen(state_ref[n])
        grad_phi = mul(gn, state, "nt") + gd * norm.astype(jnp.float32)
        grad_phi = (grad_phi * reading).astype(jnp.bfloat16)
        query_sums += jnp.concatenate(query_parts, axis=0)
        query_sums += chain(grad_phi, first, second, back_ref, 1, head)
    acc_ref[...] += query_sums
    gk_ref[...] += key_sums

    @pl.when(lax.rem(start + STEP_HEADS, HALF_HEADS) == 0)
    def _():
        gq_ref[...] = (acc_ref[...] * FEAT**-0.25).astype(jnp.bfloat16)


def later_grad_kernel(
    k_ref, v_ref, gk_in_ref, gv_in_ref, state_ref, pick_ref, back_ref, last_ref,
    gk_ref, gv_ref, acc_ref,
):
    start = pl.program_id(0) * STEP_HEADS

    @pl.when(lax.rem(start, HALF_HEADS) == 0)
    def _():
        acc_ref[...] = gk_in_ref[...]

    keys, last = k_ref[...], last_ref[...]
    total = jnp.zeros_like(acc_ref)
    for head, n, lanes in step_heads():
        first, second = factors(own_lanes(keys, head), pick_ref, 0, last)
        state, norm = widen(state_ref[n])
        values = gv_in_ref[:, lanes] + mul(first * second, state)
        gv_ref[:, lanes] = values.astype(jnp.bfloat16)
        grad_phi = mul(v_ref[:, lanes], state, "nt") + norm.astype(jnp.float32)
        grad_phi = (grad_phi * last).astype(jnp.bfloat16)
        total = total + chain(grad_phi, first, second, back_ref, 0, head)
    acc_ref[...] += total

    @pl.when(lax.rem(start + STEP_HEADS, HALF_HEADS) == 0)
    def _():
        gk_ref[...] = (acc_ref[...] * FEAT**-0.25).astype(jnp.bfloat16)


def specs(rows):
    return dict(
        pair=pl.BlockSpec((rows, 128), lambda h: (0, h * STEP_HEADS // HALF_HEADS)),
        head=pl.BlockSpec((rows, STEP_HEADS * HEAD_V), lambda h: (0, h)),
        state=pl.BlockSpec((STEP_HEADS, STATE, HEAD_V), lambda h: (h, 0, 0)),
        pick=pl.BlockSpec((3, WIDE, WIDE), lambda h: (0, 0, 0)),
        back=pl.BlockSpec((2, 128, 2 * WIDE), lambda h: (0, 0, 0)),
        column=pl.BlockSpec((rows, 1), lambda h: (0, 0)),
        row=pl.BlockSpec((8, rows), lambda h: (0, 0)),
    )


def heads_call(kernel, rows, ins, outs, scratch=(), name=None):
    table = specs(rows)
    shapes = {
        "pair": (rows, HEADS * FEAT),
        "head": (rows, HEADS * HEAD_V),
        "state": (HEADS, STATE, HEAD_V),
    }
    return pl.pallas_call(
        kernel,
        grid=(HEADS // STEP_HEADS,),
        in_specs=[table[kind] for kind in ins],
        out_specs=[table[kind] for kind, _ in outs],
        out_shape=[jax.ShapeDtypeStruct(shapes[kind], kept) for kind, kept in outs],
        scratch_shapes=list(scratch),
        compiler_params=pltpu.CompilerParams(
            dimension_semantics=("arbitrary",), vmem_limit_bytes=48 * 2**20
        ),
        cost_estimate=pl.CostEstimate(flops=2**20, bytes_accessed=2**16, transcendentals=0),
        name=name,
    )


f32, bf = jnp.float32, jnp.bfloat16


def mix_state(k, v, tables, last):
    rows = k.shape[0]
    return heads_call(state_kernel, rows, ["pair", "head", "pick", "column"],
        [("state", bf)], name="mix_state")(k, v, tables[0], last)[0]


def mix_local(q, k, v, seg_col, seg_row):
    rows = k.shape[0]
    return heads_call(local_kernel, rows, ["pair", "pair", "head", "column", "row"],
        [("head", f32), ("head", f32)], [pltpu.VMEM((rows, rows), bf)], name="mix_local")(q, k, v, seg_col, seg_row)


def mix_prefix(q, num, den, state, tables, reading):
    rows = q.shape[0]
    return heads_call(prefix_kernel, rows, ["pair", "head", "head", "state", "pick", "column"],
        [("head", bf), ("head", f32)], name="mix_prefix")(q, num, den, state, tables[0], reading)


def mix_state_grad(q, g, att, inverse, tables, reading):
    rows = q.shape[0]
    return heads_call(state_grad_kernel, rows, ["pair", "head", "head", "head", "pick", "column"],
        [("state", bf)], name="mix_state_grad")(q, g, att, inverse, tables[0], reading)[0]


def mix_local_grad(q, k, v, g, att, inverse, state, tables, reading, seg_col, seg_row):
    rows = q.shape[0]
    return heads_call(local_grad_kernel, rows,
        ["pair", "pair", "head", "head", "head", "head", "state", "pick", "back", "column", "column", "row"],
        [("pair", bf), ("pair", f32), ("head", f32)],
        [pltpu.VMEM((rows, rows), bf), pltpu.VMEM((rows, 128), f32)], name="mix_local_grad")(
        q, k, v, g, att, inverse, state, *tables, reading, seg_col, seg_row)


def mix_later_grad(k, v, gk, gv, state, tables, last):
    rows = k.shape[0]
    return heads_call(later_grad_kernel, rows,
        ["pair", "head", "pair", "head", "state", "pick", "back", "column"],
        [("pair", bf), ("head", bf)], [pltpu.VMEM((rows, 128), f32)], name="mix_later_grad")(
        k, v, gk, gv, state, *tables, last)


from jax.sharding import PartitionSpec as P

D = 2048
EPSILON = 1e-05
LIMIT = 58 * 2**20
TILE = 352


def cost(flops, moved):
    return pl.CostEstimate(flops=flops, bytes_accessed=moved, transcendentals=0)


def whole(*shape):
    return pl.BlockSpec(shape, lambda *_: (0,) * len(shape), pipeline_mode=pl.Buffered(1))


def tiling(parts, rows):
    if parts == 1:
        taken = TILE if rows % TILE == 0 else rows
        return 1, taken, rows // taken
    taken = max(1, TILE // rows)
    taken = taken if parts % taken == 0 else parts
    return taken, rows, parts // taken


def gate_kernel(x_ref, c_ref, *refs):
    count = len(refs) // 3
    half = x_ref.shape[0] // 2
    for n in range(count):
        both_ref, down_ref, out_ref = refs[2 * n], refs[2 * n + 1], refs[2 * count + n]
        parts, _, rows, _ = both_ref.shape
        gate_w, up_w = [both_ref[:, k].reshape(parts * rows, D) for k in range(2)]
        down_w = down_ref[:, 0].reshape(parts * rows, D)
        for at in (slice(0, half), slice(half, 2 * half)):
            x, c = x_ref[at, :], c_ref[at, :]
            gate = mul(gate_w, x, "nt")
            up = mul(up_w, x, "nt")
            grad = mul(down_w, c, "nt").astype(bf).astype(f32)
            sig = 1.0 / (1.0 + jnp.exp(-gate))
            act = gate * sig
            out_ref[0, :, at] = (grad * up * sig * (1.0 + gate * (1.0 - sig))).astype(bf)
            out_ref[1, :, at] = (grad * act).astype(bf)
            out_ref[2, :, at] = (act * up).astype(bf)


def ffn_gates(x, c, weights):
    rows, count = x.shape[0], len(weights)
    hidden = weights[0][1].shape[0] * weights[0][1].shape[2]
    ins, outs = [whole(rows, D)] * 2, []
    for pair in weights:
        for w in pair:
            taken, height, steps = tiling(w.shape[0], w.shape[2])
            at = (lambda i: (0, 0, i, 0)) if w.shape[0] == 1 else (lambda i: (i, 0, 0, 0))
            ins.append(pl.BlockSpec((taken, w.shape[1], height, D), at))
        outs.append(pl.BlockSpec((3, taken * height, rows), lambda i: (0, i, 0)))
    return pl.pallas_call(
        gate_kernel,
        grid=(steps,),
        in_specs=ins,
        out_specs=outs,
        out_shape=[jax.ShapeDtypeStruct((3, hidden, rows), bf)] * count,
        compiler_params=pltpu.CompilerParams(vmem_limit_bytes=LIMIT),
        cost_estimate=cost(
            6 * rows * D * hidden * count,
            2 * (2 * rows * D + 3 * count * hidden * (D + rows)),
        ),
        name="ffn_gates",
    )(x, c, *[w for pair in weights for w in pair])


def back_kernel(count, *refs):
    made, weights, out_ref, turned = (
        refs[:count], refs[count : 2 * count], refs[-count - 1], refs[-count:]
    )
    added = refs[2 * count : -count - 1]

    @pl.when(pl.program_id(0) == 0)
    def _():
        for block, kept in zip(made, turned):
            kinds, hidden, rows = block.shape
            kept[...] = block[...].reshape(kinds * hidden, rows).T

    total = None
    for kept, w_ref in zip(turned, weights):
        parts, kinds, rows, columns = w_ref.shape
        right = jnp.concatenate(
            [w_ref[:, k].reshape(parts * rows, columns) for k in range(kinds)], axis=0
        )
        part = mul(kept[...], right)
        total = part if total is None else total + part
    for more in added:
        total = total + more[...].astype(f32)
    out_ref[...] = total.astype(out_ref.dtype)


def ffn_back(made, weights, which, added=(), columns=512):
    count = len(weights)
    weights = [pair[which] for pair in weights]
    kinds = weights[0].shape[1]
    _, hidden, rows = made[0].shape
    out = pl.BlockSpec((rows, columns), lambda j: (0, j))
    ins = [
        pl.BlockSpec(
            (kinds, hidden, rows), lambda j: (2 * which // kinds, 0, 0), pipeline_mode=pl.Buffered(1)
        )
    ] * count
    for w in weights:
        ins.append(pl.BlockSpec((w.shape[0], kinds, w.shape[2], columns), lambda j: (0, 0, 0, j)))
    ins += [out] * len(added)
    return pl.pallas_call(
        functools.partial(back_kernel, count),
        grid=(D // columns,),
        in_specs=ins,
        out_specs=out,
        out_shape=jax.ShapeDtypeStruct((rows, D), bf),
        scratch_shapes=[pltpu.VMEM((rows, kinds * hidden), bf)] * count,
        compiler_params=pltpu.CompilerParams(vmem_limit_bytes=LIMIT),
        cost_estimate=cost(
            2 * rows * D * hidden * kinds * count,
            2 * (count * kinds * hidden * (D + rows) + rows * D),
        ),
        name="ffn_back",
    )(*made, *weights, *added)


def grad_kernel(blocks, *refs):
    made, xs, cs = refs[:blocks], refs[blocks : 2 * blocks], refs[2 * blocks : 3 * blocks]
    added, out_ref = refs[3 * blocks : -1], refs[-1]
    parts, _, rows, _ = out_ref.shape

    def write(rights):
        total = None
        for left, right in zip(made, rights):
            part = mul(left[0], right[...])
            total = part if total is None else total + part
        for more in added:
            total = total + more[...].reshape(parts * rows, D).astype(f32)
        out_ref[...] = total.astype(bf).reshape(parts, 1, rows, D)

    kind = pl.program_id(0)

    @pl.when(kind < 2)
    def _():
        write(xs)

    @pl.when(kind == 2)
    def _():
        write(cs)


def ffn_grad(made, xs, cs, parts, height, added=None):
    blocks = len(made)
    rows = xs[0].shape[0]
    hidden = made[0].shape[1]
    taken, rise, steps = tiling(parts, height)
    left = pl.BlockSpec((1, taken * rise, rows), lambda k, i: (k, i, 0))
    at = (lambda k, i: (0, k, i, 0)) if parts == 1 else (lambda k, i: (i, k, 0, 0))
    out = pl.BlockSpec((taken, 1, rise, D), at)
    more = [] if added is None else [added]
    return pl.pallas_call(
        functools.partial(grad_kernel, blocks),
        grid=(3, steps),
        in_specs=[left] * blocks + [whole(rows, D)] * (2 * blocks) + [out] * len(more),
        out_specs=out,
        out_shape=jax.ShapeDtypeStruct((parts, 3, height, D), bf),
        compiler_params=pltpu.CompilerParams(vmem_limit_bytes=LIMIT),
        cost_estimate=cost(
            6 * rows * D * hidden * blocks,
            2 * (2 * blocks * rows * D + 3 * hidden * (rows * blocks + D * (1 + len(more)))),
        ),
        name="ffn_grad",
    )(*made, *xs, *cs, *more)


def widen_kernel(sum_ref, *out_refs):
    for kind, out_ref in enumerate(out_refs):
        out_ref[...] = sum_ref[0, kind].astype(f32)


def widened(sums):
    parts, _, height, _ = sums.shape
    return pl.pallas_call(
        widen_kernel,
        grid=(parts,),
        in_specs=[pl.BlockSpec((1, 3, height, D), lambda i: (i, 0, 0, 0))],
        out_specs=[pl.BlockSpec((height, D), lambda i: (i, 0))] * 3,
        out_shape=[jax.ShapeDtypeStruct((parts * height, D), f32)] * 3,
        compiler_params=pltpu.CompilerParams(vmem_limit_bytes=LIMIT),
        cost_estimate=cost(0, 6 * parts * 3 * height * D),
        name="widened",
    )(sums)


def qkv_grad_kernel(n_ref, gq_ref, gk_ref, gv_ref, out_ref):
    turned = n_ref[...].T
    qk = gq_ref.shape[1]
    out_ref[:, :qk] = mul(turned, gq_ref[...]).astype(bf)
    out_ref[:, qk : 2 * qk] = mul(turned, gk_ref[...]).astype(bf)
    out_ref[:, 2 * qk :] = mul(turned, gv_ref[...]).astype(bf)


def qkv_grad(normed, gq, gk, gv):
    rows, qk = gq.shape
    columns = 2 * qk + D
    tile = 256
    return pl.pallas_call(
        qkv_grad_kernel,
        grid=(D // tile,),
        in_specs=[
            pl.BlockSpec((rows, tile), lambda i: (0, i)), whole(rows, qk), whole(rows, qk), whole(rows, D)
        ],
        out_specs=pl.BlockSpec((tile, columns), lambda i: (i, 0)),
        out_shape=jax.ShapeDtypeStruct((D, columns), bf),
        compiler_params=pltpu.CompilerParams(vmem_limit_bytes=LIMIT),
        cost_estimate=cost(2 * rows * D * columns, 2 * (rows * (D + columns) + D * columns)),
        name="qkv_grad",
    )(normed, gq, gk, gv)


def norm_forward(inputs):
    inverse = lax.rsqrt(jnp.mean(inputs * inputs, axis=-1, keepdims=True) + EPSILON)
    return (inputs * inverse, inverse)


def norm_backward(grad_normed, unit_rows, inverse, gain_vec):
    gain_grad = jnp.sum(grad_normed * unit_rows, axis=0)
    grad_unit = grad_normed * gain_vec
    return (
        inverse * (grad_unit - unit_rows * jnp.mean(grad_unit * unit_rows, axis=-1, keepdims=True)),
        gain_grad,
    )


def move(array, target, axis="mp"):
    size = lax.axis_size(axis)
    pairs = [(m, target(m)) for m in range(size)]
    return lax.ppermute(array, axis, [(m, t) for m, t in pairs if t is not None])


def then(value, *before):
    return lax.optimization_barrier((value, before))[0]


def beside(array, mover, *works):
    ends = [array.shape[0] * n // len(works) // 16 * 16 for n in range(len(works))] + [array.shape[0]]
    moved, made = [], []
    for n, work in enumerate(works):
        share = array[ends[n] : ends[n + 1]]
        if made:
            share = then(share, made[-1])
        result = work(share, made)
        arrived, result = lax.optimization_barrier((mover(share), result))
        moved.append(arrived)
        made.append(result)
    return jnp.concatenate(moved, axis=0), made


def to_mate(array):
    return move(array, lambda m: m ^ 1)


def to_half(array):
    size = lax.axis_size("mp")
    return move(array, lambda m: (m + size // 2) % size)


def to_peer(array, step):
    half = lax.axis_size("mp") // 2

    def target(m):
        low = m % half
        return m - low + (low + 2 * step) % half

    return move(array, target)


def to_chip(array, step):
    size = lax.axis_size("mp")
    return move(array, lambda m: m + 2 * step if 0 <= m + 2 * step < size else None)


def sums_before(own, sign, *beside, made=None):
    core = lax.axis_index("mp") % 2
    chips = lax.axis_size("mp") // 2
    wire = own.astype(bf)
    mate = to_mate(wire).astype(f32)
    half = own.shape[0] // 2
    both = wire.astype(f32) + mate
    running = lax.dynamic_slice_in_dim(both, core * half, half, 0)
    before = jnp.zeros_like(running)
    step, beside, made = 1, list(beside), [] if made is None else made
    while step < chips:
        came = to_chip(running.astype(bf), sign * step)
        if beside:
            came, result = lax.optimization_barrier((came, beside.pop(0)(running)))
            made.append(result)
        came = came.astype(f32)
        before = before + came
        running = running + came
        step *= 2
    before = before.astype(bf)
    other = to_mate(before)
    first = jnp.where(core == 0, before, other)
    second = jnp.where(core == 0, other, before)
    total = jnp.concatenate([first, second], axis=0).astype(f32)
    inner = core == (1 if sign > 0 else 0)
    return (total + jnp.where(inner, mate, 0.0)).astype(bf), made


def pick(array, index, dim=0):
    return lax.dynamic_index_in_dim(array, index, dim, keepdims=False)


def chip_halves(array):
    groups, size = lax.axis_size("dp"), lax.axis_size("mp")
    core = lax.axis_index("mp") % 2
    rows, columns = array.shape[0] // (groups * size), array.shape[1]
    blocks = array.reshape(groups, size // 2, 2, rows, columns)
    return pick(blocks, core, 2), pick(blocks, 1 - core, 2)


def add(first, *more, kept=bf):
    total = first.astype(f32)
    for array in more:
        total = total + array.astype(f32)
    return total.astype(kept)


def placed(shares, places):
    out = jnp.zeros((len(shares),) + shares[0].shape, shares[0].dtype)
    for share, at in zip(shares, places):
        out = lax.dynamic_update_index_in_dim(out, share, at, 0)
    return out


def chip_shares(array):
    steps = range(1, lax.axis_size("mp") // 2)
    return [move(array, lambda m: m ^ (2 * step)) for step in steps]


def by_chip(array, shares):
    chip = lax.axis_index("mp") // 2
    return placed([array] + shares, [chip ^ step for step in range(len(shares) + 1)])


def first_groups(array):
    return [move(array, lambda m: m ^ step, "dp") for step in (1, 2)]


def third_group(first, second):
    half = first.shape[0] // 2
    return [
        move(second[:half], lambda m: m ^ 1, "dp"),
        move(first[half:], lambda m: m ^ 2, "dp"),
    ]


def assembled(pieces, groups, chips, out=None):
    group, core = lax.axis_index("dp"), lax.axis_index("mp") % 2
    shape = pieces[0][2].shape[1:]
    if out is None:
        out = jnp.zeros((groups, chips, 2) + shape, bf)
    for step, at, own, other in pieces:
        both = jnp.where(core == 0, jnp.stack([own, other], 1), jnp.stack([other, own], 1))
        start = (group ^ step, at) + (0,) * (len(shape) + 1)
        out = lax.dynamic_update_slice(out, both[None], start)
    return out


def group_move(array, step):
    return move(pick(array, lax.axis_index("dp") ^ step), lambda m: m ^ step, "dp")


def chip_moves(array):
    chip = lax.axis_index("mp") // 2
    return [
        move(pick(array, chip ^ step), lambda m: m ^ (2 * step))
        for step in range(1, lax.axis_size("mp") // 2)
    ]


def sum_everywhere(array):
    for axis in ("mp", "dp"):
        step = 1
        while step < lax.axis_size(axis):
            array = array + move(array, lambda m: m ^ step, axis)
            step *= 2
    return array


def body(
    x_in,
    seq_lengths,
    norm1_gain,
    w_query,
    w_key,
    w_value,
    w_out,
    norm2_gain,
    w_gate,
    w_up,
    w_down,
    cotangent,
):
    rows = x_in.shape[0]
    groups = lax.axis_size("dp")
    size = lax.axis_size("mp")
    peers = size // 4
    hidden = w_gate.shape[1]
    piece = hidden // groups
    place = lax.axis_index("mp")
    group = lax.axis_index("dp")
    everywhere = ("dp", "mp")
    qk = w_query.shape[1]
    aligned = piece % 16 == 0

    own_rows = w_query.shape[0]
    gain_block = jnp.concatenate(
        [norm1_gain[:, None], norm2_gain[:, None], jnp.zeros((own_rows, 126), bf)], axis=1
    )
    packed = jnp.concatenate([w_query, w_key, w_value, gain_block], axis=1)
    in_chips, packed = lax.optimization_barrier((chip_shares(packed), packed))
    in_chips = by_chip(packed, in_chips)

    full_out = lax.all_gather(w_out, everywhere, axis=0, tiled=True)
    half_chips = size // 4
    mine_both = jnp.concatenate(then([w_gate.T, w_up.T], in_chips), axis=0)
    mine = (mine_both.reshape(1, 2, hidden, D), then(w_down, in_chips).reshape(1, 1, hidden, D))
    far_down = lax.dynamic_slice_in_dim(mine[1][0, 0], group * piece, piece, 0)
    far_both = lax.dynamic_slice_in_dim(mine[0][0], group * piece, piece, 1).reshape(2 * piece, D)
    cot_ends = [rows * n // 16 for n in (0, 3, 6, 10, 13, 16)]
    cot_shares = [cotangent[a:b] for a, b in zip(cot_ends, cot_ends[1:])]

    def peers_of(array):
        return [to_peer(array, step) for step in range(1, peers)]

    def beside_one(array, mover, work):
        return lax.optimization_barrier((mover(array), work(array)))

    both_cut, down_cut = 2 * piece * 8 // 11, piece * 7 // 11
    in_near, in_mate, both_first = lax.optimization_barrier(
        (
            first_groups(in_chips),
            to_mate(in_chips),
            to_half(then(far_both[:both_cut], in_chips)),
        )
    )
    in_third, in_mates, both_second = lax.optimization_barrier(
        (
            third_group(*in_near),
            [to_mate(share) for share in in_near],
            to_half(then(far_both[both_cut:], in_near)),
        )
    )
    in_mates = [in_mate, *in_mates] + [to_mate(share) for share in in_third]
    far_both = jnp.concatenate([both_first, both_second], axis=0)
    far_both = lax.all_gather(far_both, "dp", axis=0, tiled=True).reshape(groups, 2, piece, D)
    down_first = to_half(then(far_down[:down_cut], in_third))
    mate_down = to_mate(then(mine[1], in_third))
    cot_third = peers_of(then(cot_shares[2], in_third))
    in_pieces = [
        (step, at, own, other)
        for (step, at, own), other in zip(
            (
                (0, 0, in_chips),
                (1, 0, in_near[0]),
                (2, 0, in_near[1]),
                (3, 0, in_third[0]),
                (3, half_chips, in_third[1]),
            ),
            in_mates,
        )
    ]
    full_in = assembled(in_pieces, groups, size // 2).reshape(D, packed.shape[1])

    row_start = place * rows
    seq_ends = jnp.cumsum(seq_lengths[0], dtype=jnp.int32)
    positions = row_start + jnp.arange(rows, dtype=jnp.int32)
    segments = jnp.sum((positions[:, None] >= seq_ends[None, :]).astype(jnp.int32), axis=1)
    seg_before = jnp.sum((row_start - 1 >= seq_ends).astype(jnp.int32))
    reading = ((segments == seg_before) & (row_start > 0)).astype(f32)[:, None]
    last_doc = (segments == segments[-1]).astype(f32)[:, None]
    seg_col = segments[:, None]
    seg_row = jnp.broadcast_to(segments[None, :], (8, rows))
    tables = feature_tables()

    inputs = x_in.astype(f32)
    inverse_one = norm_forward(inputs)[1]
    early = (full_out, mine, down_first, mate_down, cot_third, inverse_one, reading, last_doc, seg_col, seg_row)
    full_in, early = lax.optimization_barrier((full_in, early))
    full_out, mine, down_first, mate_down, cot_third, inverse_one, reading, last_doc, seg_col, seg_row = early
    gain_one = full_in[:, 2 * qk + D].astype(f32)
    gain_two = full_in[:, 2 * qk + D + 1].astype(f32)
    full_qkv = full_in[:, : 2 * qk + D]
    unit_one = inputs * inverse_one
    normed_one = (unit_one * gain_one).astype(bf)
    (got, mate_gate, down_second), qkv = beside_one(
        then(cot_shares[3], full_in),
        lambda ready: (
            peers_of(ready),
            to_mate(then(mine[0][:, :1], ready)),
            to_half(then(far_down[down_cut:], ready)),
        ),
        lambda ready: mul(then(normed_one, ready), full_qkv).astype(bf),
    )
    cot_got = [cot_third, got]
    queries, keys, values = qkv[:, :qk], qkv[:, qk : 2 * qk], qkv[:, 2 * qk :]
    far_down = jnp.concatenate([down_first, down_second], axis=0)
    far_down = lax.all_gather(far_down, "dp", axis=0, tiled=True).reshape(groups, 1, piece, D)
    (got, mate_up), own_state = beside_one(
        then(cot_shares[4], qkv),
        lambda ready: (peers_of(ready), to_mate(then(mine[0][:, 1:], ready))),
        lambda ready: mix_state(then(keys, ready), values, tables, last_doc),
    )
    cot_got.append(got)

    def local_work(ready):
        local = mix_local(then(queries, ready), keys, values, seg_col, seg_row)
        return local

    def pack_work(ready):
        gate, up = then((mate_gate, mate_up), ready)
        return jnp.concatenate([gate, up], axis=1)

    prefix, [(num, den), mate_both] = sums_before(own_state, 1, local_work, pack_work)
    cot_first, (attended, inverse_den) = beside_one(
        then(cot_shares[0], prefix),
        peers_of,
        lambda ready: mix_prefix(then(queries, ready), num, den, prefix, tables, reading),
    )
    mate = (mate_both, mate_down)
    near = [mine, mate]
    cot_second, hidden_in = beside_one(
        then(cot_shares[1], attended),
        peers_of,
        lambda ready: inputs + mul(then(attended, ready), full_out),
    )
    cot_got = [cot_first, cot_second] + cot_got
    unit_two, inverse_two = norm_forward(hidden_in)
    normed_two = (unit_two * gain_two).astype(bf)
    came = [to_peer(normed_two, step) for step in range(1, peers)]

    near_own = ffn_gates(normed_two, cotangent, near)
    far_mine = then((far_both, far_down), normed_two)
    if not aligned:
        far_mine = tuple(jnp.swapaxes(w, 0, 1).reshape(1, -1, hidden, D) for w in far_mine)
    far_mate = then(tuple(to_mate(w) for w in far_mine), near_own)
    far = [tuple(far_mine), far_mate]
    weights = near + far
    shape = (groups, piece) if aligned else (1, hidden)
    far_own = ffn_gates(normed_two, cotangent, far)
    made_own = list(near_own) + list(far_own)
    grad_own = ffn_back(made_own, weights, 0)
    normed = [normed_two] + then(came, grad_own)
    cot_got = then(cot_got, near_own)
    cots = [cotangent] + [jnp.concatenate(parts, axis=0) for parts in zip(*cot_got)]
    near_made = [near_own] + [ffn_gates(x, c, near) for x, c in zip(normed[1:], cots[1:])]
    far_made = [far_own] + [
        ffn_gates(x, c, then(far, near_made)) for x, c in zip(normed[1:], cots[1:])
    ]
    made = [list(a) + list(b) for a, b in zip(near_made, far_made)]

    def weight_grads(made, ready, added=None):
        return ffn_grad(then(made, ready), normed, cots, *shape, added)

    def over_groups(grad):
        if not aligned:
            grad = jnp.swapaxes(grad.reshape(3, groups, piece, D), 0, 1)
        return lax.psum_scatter(
            grad.reshape(groups * 3 * piece, D), "dp", scatter_dimension=0, tiled=True
        )

    def back(block, which, ready):
        return ffn_back(then(block, ready), weights, which)

    far_given = weight_grads([block[1] for block in far_made], far_made)
    far_sent = to_mate(far_given)
    grad_parts = [back(block, 0, far_given) for block in made[1:]]

    def owners(parts):
        return [to_peer(part, peers - step) for step, part in enumerate(parts, 1)]

    def stacked(parts):
        return jnp.concatenate([part[:, None] for part in parts], axis=1)

    def to_owners(parts):
        return stacked(owners([parts[:, n] for n in range(peers - 1)]))

    def near_work(ready, _):
        given = weight_grads([block[1] for block in near_made], ready)
        return given

    def far_work(ready, done):
        kept = weight_grads([block[0] for block in far_made], ready, far_sent)
        return kept, to_mate(then(done[0], ready))

    def last_work(ready, done):
        return weight_grads([block[0] for block in near_made], ready, done[1][1])

    grad_sent, (_, (far_kept, _), near_kept) = beside(
        stacked(grad_parts), to_owners, near_work, far_work, last_work
    )
    far_part = over_groups(far_kept)
    near_part = over_groups(near_kept)
    grad_normed_two = jnp.sum(grad_sent.astype(f32), axis=1) + grad_own.astype(f32)

    grad_two, gain_two_grad = norm_backward(grad_normed_two, unit_two, inverse_two, gain_two)
    grad_hidden_in = cotangent.astype(f32) + grad_two
    grad_branch = grad_hidden_in.astype(bf)
    grad_attended = mul(grad_branch, full_out, "nt").astype(bf)
    state_grad = mix_state_grad(queries, grad_attended, attended, inverse_den, tables, reading)

    def local_grads(ready):
        local = mix_local_grad(
            then(queries, ready), keys, values, grad_attended, attended, inverse_den, prefix, tables,
            reading, seg_col, seg_row,
        )
        return local, to_mate(then(out_halves[1], ready))

    out_halves = []

    def out_work(ready):
        halves = chip_halves(mul(then(attended, ready), grad_branch, "tn").astype(bf))
        out_halves.extend(halves)
        return halves

    later, [_, (local, out_came)] = sums_before(state_grad, -1, out_work, local_grads)
    grad_queries, part_keys, part_values = local
    out_kept = add(out_halves[0], out_came)
    out_kept, far_part = then((out_kept, far_part), later)
    ends = [far_part.shape[0] * n // 33 for n in (0, 3, 9, 16, 22, 33)]
    far_shares = [far_part[a:b] for a, b in zip(ends, ends[1:])]
    out_first, out_second, out_diag = [pick(out_kept, group ^ step) for step in range(1, groups)]
    low, high = slice(None, half_chips), slice(half_chips, None)

    def by_first(block):
        return move(block, lambda m: m ^ 1, "dp")

    def by_second(block):
        return move(block, lambda m: m ^ 2, "dp")

    (far_first, for_second, for_first), (grad_keys, grad_values) = beside_one(
        then(far_shares[0], out_kept),
        lambda ready: (
            to_half(ready), by_first(then(out_diag[low], ready)), by_second(then(out_diag[high], ready))
        ),
        lambda ready: mix_later_grad(
            then(keys, ready), values, part_keys, part_values, later, tables, last_doc
        ),
    )
    out_second = [add(out_second[low], for_second), out_second[high]]
    out_first = [out_first[low], add(out_first[high], for_first)]
    (out_low, far_slot), in_grad = beside_one(
        then((out_first[0], out_second[0]), grad_keys),
        lambda ready: (
            [by_first(ready[0]), by_second(ready[1])], to_half(then(far_shares[1], ready))
        ),
        lambda ready: qkv_grad(then(normed_one, ready), grad_queries, grad_keys, grad_values),
    )
    in_keep, in_give = chip_halves(in_grad)
    out_parts = [back(block, 1, in_grad) for block in made[1:]]
    out_parts, in_came, out_high, far_second = lax.optimization_barrier(
        (
            out_parts,
            to_mate(in_give),
            [by_first(then(out_first[1], in_grad)), by_second(then(out_second[1], in_grad))],
            to_half(then(far_shares[2], in_grad)),
        )
    )
    in_diag = add(pick(in_keep, group ^ 3), pick(in_came, group ^ 3))
    in_first, in_second = [
        add(pick(in_keep, group ^ step), pick(in_came, group ^ step)) for step in (1, 2)
    ]
    grad_queries, grad_keys, grad_values = then(
        (grad_queries, grad_keys, grad_values), (in_diag, in_first, in_second)
    )
    grad_normed_one = (
        mul(grad_queries, full_qkv[:, :qk], "nt")
        + mul(grad_keys, full_qkv[:, qk : 2 * qk], "nt")
        + mul(grad_values, full_qkv[:, 2 * qk :], "nt")
    )
    out_split = jnp.split(stacked(out_parts), [rows * 3 // 8], axis=0)
    out_early, for_second, for_first, far_third, grad_normed_one, in_first, in_second = (
        lax.optimization_barrier(
            (
                to_owners(then(out_split[0], in_diag)),
                by_first(in_diag[low]),
                by_second(in_diag[high]),
                to_half(then(far_shares[3], in_diag)),
                grad_normed_one,
                in_first,
                in_second,
            )
        )
    )
    in_first = jnp.concatenate([in_first[low], add(in_first[high], for_first)], axis=0)
    in_second = jnp.concatenate([add(in_second[low], for_second), in_second[high]], axis=0)
    in_moved = [by_first(in_first), by_second(in_second)]
    far_last = to_half(then(far_shares[4], in_first))
    grad_normed_one = then(grad_normed_one, (in_first, in_second))
    grad_one, gain_one_grad = norm_backward(grad_normed_one, unit_one, inverse_one, gain_one)
    input_grad = (grad_hidden_in + grad_one).astype(bf)
    input_grad, gain_one_grad, in_moved, far_last = lax.optimization_barrier(
        (input_grad, gain_one_grad, in_moved, far_last)
    )
    out_own = back(made[0], 1, in_moved)
    far_sum = jnp.concatenate([far_first, far_slot, far_second, far_third, far_last], axis=0)
    ffn_sum = lax.all_gather(add(near_part, far_sum), "dp", axis=0, tiled=True)
    ffn_sum = ffn_sum.reshape(groups, 3, piece, D)
    chip = place // 2

    def over_chips(blocks, kept):
        shares = [
            add(*[pick(block, chip ^ step) for block in blocks]) for step in range(1, size // 2)
        ]
        moved = [move(share, lambda m: m ^ (2 * step)) for step, share in enumerate(shares, 1)]
        return add(*[pick(block, chip) for block in blocks], *moved, kept=kept)

    in_sum = over_chips([pick(in_keep, group), pick(in_came, group), *in_moved], f32)
    out_blocks = [jnp.concatenate(pair, axis=0) for pair in zip(out_low, out_high)]
    out_blocks = then([pick(out_kept, group), *out_blocks], in_moved)
    out_sum = over_chips(out_blocks, f32)
    if not aligned:
        ffn_sum = jnp.swapaxes(ffn_sum, 0, 1).reshape(1, 3, hidden, D)
    gate_grad, up_grad, down_grad = widened(ffn_sum)
    gain_sums = sum_everywhere(jnp.stack([gain_one_grad, gain_two_grad]))
    gain_sums = lax.dynamic_slice_in_dim(
        gain_sums, (group * size + place) * own_rows, own_rows, 1
    )
    out_last = to_owners(then(out_split[1], in_sum, gain_sums))
    out_sent = jnp.concatenate([out_early, out_last], axis=0)
    output = (hidden_in + jnp.sum(out_sent.astype(f32), axis=1) + out_own.astype(f32)).astype(bf)
    return (
        output,
        input_grad,
        gain_sums[0],
        in_sum[:, :qk],
        in_sum[:, qk : 2 * qk],
        in_sum[:, 2 * qk :],
        out_sum,
        gain_sums[1],
        gate_grad.T,
        up_grad.T,
        down_grad,
    )


def solution(mesh):
    rows, vector = P(("dp", "mp"), None), P(("dp", "mp"))
    columns, down = P(None, "mp"), P("mp", None)
    return jax.shard_map(
        body,
        mesh=mesh,
        in_specs=(rows, P("dp", None), vector, rows, rows, rows, rows, vector, columns, columns, down, rows),
        out_specs=(rows, rows, vector, rows, rows, rows, rows, vector, columns, columns, down),
        check_vma=False,
    )
```

```python
import functools
import numpy as np
import jax
import jax.numpy as jnp
from jax import lax
from jax.experimental import pallas as pl
from jax.experimental.pallas import tpu as pltpu

HEADS = 16
FEAT = 16
HEAD_V = 128
WIDE = 256
STATE = 160
SQUARES = FEAT * (FEAT + 1) // 2
LINEAR = SQUARES + FEAT
HALF_HEADS = 128 // FEAT
STEP_HEADS = 8


def feature_tables():
    pairs = [(a, b) for a in range(FEAT) for b in range(a, FEAT)]
    pick = np.zeros((3, WIDE, WIDE), np.float32)
    for row in range(128):
        for entry, (a, b) in enumerate(pairs):
            if row % FEAT == a:
                pick[0, row, entry] = 1.0
                pick[1, row, entry] = 0.5 if a == b else 1.0
            if row % FEAT == b:
                pick[2, row, entry] = 1.0
        pick[0:2, row, SQUARES + row % FEAT] = 1.0
    pick[0:2, 128, LINEAR] = 1.0
    pick[2, 128, SQUARES : LINEAR + 1] = 1.0
    back = np.stack([np.concatenate([pick[n, :128], pick[2, :128]], axis=1) for n in (0, 1)])
    return jnp.asarray(pick, jnp.bfloat16), jnp.asarray(back, jnp.bfloat16)


def mul(left, right, kind="nn"):
    dims = {"nn": ((1,), (0,)), "nt": ((1,), (1,)), "tn": ((0,), (0,))}[kind]
    return lax.dot_general(left, right, (dims, ((), ())), preferred_element_type=jnp.float32)


def head_lanes(head, rows):
    lane = lax.broadcasted_iota(jnp.int32, (rows, 128), 1)
    return lane // FEAT == lax.rem(head, HALF_HEADS)


def own_lanes(block, head):
    scaled = block * jnp.asarray(FEAT**-0.25, jnp.bfloat16)
    return jnp.where(head_lanes(head, block.shape[0]), scaled, jnp.zeros_like(scaled))


def first_lanes(*columns):
    lane = lax.broadcasted_iota(jnp.int32, (columns[0].shape[0], 128), 1)
    out = jnp.zeros(lane.shape, jnp.float32)
    for n, column in enumerate(columns):
        out = jnp.where(lane == n, column, out)
    return out.astype(jnp.bfloat16)


def factors(own, pick_ref, which, kept):
    ones = first_lanes(jnp.ones_like(kept))
    plain = jnp.concatenate([own, ones], axis=1)
    masked = jnp.concatenate(
        [own * kept.astype(jnp.bfloat16), ones * kept.astype(jnp.bfloat16)], axis=1
    )
    first = mul(masked, pick_ref[which]).astype(jnp.bfloat16)
    second = mul(plain, pick_ref[2]).astype(jnp.bfloat16)
    return first, second


def pack_state(state, norm_rows):
    row = lax.broadcasted_iota(jnp.int32, (STATE, HEAD_V), 0)
    out = jnp.where(row == LINEAR + 1, norm_rows[0:1, :HEAD_V], state[:STATE])
    return jnp.where(row == LINEAR + 2, norm_rows[0:1, HEAD_V:], out)


def widen(packed):
    padded = jnp.concatenate([packed, jnp.zeros((WIDE - STATE, HEAD_V), packed.dtype)], axis=0)
    norm = jnp.concatenate(
        [packed[LINEAR + 1 : LINEAR + 2, :], packed[LINEAR + 2 : LINEAR + 3, :]], axis=1
    )
    return padded, norm


def step_heads():
    first = pl.program_id(0) * STEP_HEADS
    return [
        (first + n, n, slice(n * HEAD_V, (n + 1) * HEAD_V)) for n in range(STEP_HEADS)
    ]


def state_kernel(k_ref, v_ref, pick_ref, last_ref, out_ref):
    keys, last = k_ref[...], last_ref[...]
    ones = jnp.ones((16, keys.shape[0]), jnp.bfloat16)
    for head, n, lanes in step_heads():
        first, second = factors(own_lanes(keys, head), pick_ref, 0, last)
        phi = first * second
        state = mul(phi, v_ref[:, lanes], "tn")
        out_ref[n] = pack_state(state, mul(ones, phi)).astype(out_ref.dtype)


def causal_mask(seg_col_ref, seg_row_ref, mask_ref):
    rows = mask_ref.shape[0]
    i = lax.broadcasted_iota(jnp.int32, (rows, rows), 0)
    j = lax.broadcasted_iota(jnp.int32, (rows, rows), 1)
    keep = (seg_col_ref[...] == seg_row_ref[0:1, :]) & (j <= i)
    mask_ref[...] = keep.astype(jnp.float32).astype(jnp.bfloat16)


def triangle(rows):
    half = rows // 2
    return ((slice(0, half), slice(0, half)), (slice(half, rows), slice(0, rows)))


def local_kernel(q_ref, k_ref, v_ref, seg_col_ref, seg_row_ref, num_ref, den_ref, mask_ref):
    @pl.when(pl.program_id(0) == 0)
    def _():
        causal_mask(seg_col_ref, seg_row_ref, mask_ref)

    queries = q_ref[...]
    scaled = k_ref[...] * jnp.asarray(FEAT**-0.25, jnp.bfloat16)
    for head, _, lanes in step_heads():
        own_q = own_lanes(queries, head)
        value = v_ref[:, lanes]
        wide = jnp.concatenate([value, jnp.ones_like(value)], axis=1)
        for at, upto in triangle(own_q.shape[0]):
            up = 1.0 + mul(own_q[at], scaled[upto], "nt")
            kappa = (0.5 * up * up + 0.5).astype(jnp.bfloat16) * mask_ref[at, upto]
            both = mul(kappa, wide[upto])
            num_ref[at, lanes] = both[:, :HEAD_V]
            den_ref[at, lanes] = both[:, HEAD_V:]


def prefix_kernel(
    q_ref, num_ref, den_ref, state_ref, pick_ref, reading_ref, out_ref, inverse_ref
):
    queries, reading = q_ref[...], reading_ref[...]
    for head, n, lanes in step_heads():
        first, second = factors(own_lanes(queries, head), pick_ref, 1, reading)
        phi = first * second
        state, norm = widen(state_ref[n])
        num = num_ref[:, lanes] + mul(phi, state)
        norm = mul(phi, jnp.broadcast_to(norm, (HEAD_V, WIDE)), "nt")
        inverse = 1.0 / (den_ref[:, lanes] + norm)
        out_ref[:, lanes] = (num * inverse).astype(jnp.bfloat16)
        inverse_ref[:, lanes] = inverse


def scaled_grad(g_ref, att_ref, inverse_ref, lanes):
    gn = (g_ref[:, lanes].astype(jnp.float32) * inverse_ref[:, lanes]).astype(jnp.bfloat16)
    mixed = att_ref[:, lanes].astype(jnp.float32)
    gd = -jnp.sum(gn.astype(jnp.float32) * mixed, axis=1, keepdims=True)
    return gn, gd


def state_grad_kernel(q_ref, g_ref, att_ref, inverse_ref, pick_ref, reading_ref, out_ref):
    queries, reading = q_ref[...], reading_ref[...]
    for head, n, lanes in step_heads():
        gn, gd = scaled_grad(g_ref, att_ref, inverse_ref, lanes)
        first, second = factors(own_lanes(queries, head), pick_ref, 1, reading)
        phi = first * second
        state = mul(phi, gn, "tn")
        wide = jnp.broadcast_to(gd, gn.shape).astype(jnp.bfloat16)
        out_ref[n] = pack_state(state, mul(wide, phi, "tn")).astype(out_ref.dtype)


def chain(grad_phi, first, second, back_ref, which, head):
    both = jnp.concatenate([grad_phi * second, grad_phi * first], axis=1)
    grad = mul(both, back_ref[which], "nt")
    return jnp.where(head_lanes(head, grad_phi.shape[0]), grad, 0.0)


def local_grad_kernel(
    q_ref, k_ref, v_ref, g_ref, att_ref, inverse_ref, state_ref, pick_ref, back_ref,
    reading_ref, seg_col_ref, seg_row_ref, gq_ref, gk_ref, gv_ref, mask_ref, acc_ref,
):
    start = pl.program_id(0) * STEP_HEADS

    @pl.when(start == 0)
    def _():
        causal_mask(seg_col_ref, seg_row_ref, mask_ref)

    @pl.when(lax.rem(start, HALF_HEADS) == 0)
    def _():
        acc_ref[...] = jnp.zeros_like(acc_ref)
        gk_ref[...] = jnp.zeros_like(gk_ref)

    queries, keys, reading = q_ref[...], k_ref[...], reading_ref[...]
    half = queries.shape[0] // 2
    query_sums = jnp.zeros_like(acc_ref)
    key_sums = jnp.zeros_like(gk_ref)
    for head, n, lanes in step_heads():
        gn, gd = scaled_grad(g_ref, att_ref, inverse_ref, lanes)
        high = gd.astype(jnp.bfloat16).astype(jnp.float32)
        gn_wide = jnp.concatenate([gn, first_lanes(high, gd - high)], axis=1)
        ones = jnp.ones_like(gd)
        v_wide = jnp.concatenate([v_ref[:, lanes], first_lanes(ones, ones)], axis=1)
        own_q = own_lanes(queries, head)
        own_k = own_lanes(keys, head)
        parts, query_parts, key_parts = [], [], []
        for at, upto in triangle(own_q.shape[0]):
            keep = mask_ref[at, upto]
            up = 1.0 + mul(own_q[at], own_k[upto], "nt")
            kappa = (0.5 * up * up + 0.5).astype(jnp.bfloat16) * keep
            grad_t = mul(gn_wide[at], v_wide[upto], "nt").astype(jnp.bfloat16)
            grad_t = grad_t * up.astype(jnp.bfloat16) * keep
            query_parts.append(mul(grad_t, own_k[upto]))
            key_parts.append(mul(grad_t, own_q[at], "tn"))
            parts.append(mul(kappa, gn[at], "tn"))
        gv_ref[:half, lanes] = parts[0] + parts[1][:half]
        gv_ref[half:, lanes] = parts[1][half:]
        key_sums += key_parts[1] + jnp.concatenate(
            [key_parts[0], jnp.zeros_like(key_parts[0])], axis=0
        )
        first, second = factors(own_q, pick_ref, 1, reading)
        state, norm = widen(state_ref[n])
        grad_phi = mul(gn, state, "nt") + gd * norm.astype(jnp.float32)
        grad_phi = (grad_phi * reading).astype(jnp.bfloat16)
        query_sums += jnp.concatenate(query_parts, axis=0)
        query_sums += chain(grad_phi, first, second, back_ref, 1, head)
    acc_ref[...] += query_sums
    gk_ref[...] += key_sums

    @pl.when(lax.rem(start + STEP_HEADS, HALF_HEADS) == 0)
    def _():
        gq_ref[...] = (acc_ref[...] * FEAT**-0.25).astype(jnp.bfloat16)


def later_grad_kernel(
    k_ref, v_ref, gk_in_ref, gv_in_ref, state_ref, pick_ref, back_ref, last_ref,
    gk_ref, gv_ref, acc_ref,
):
    start = pl.program_id(0) * STEP_HEADS

    @pl.when(lax.rem(start, HALF_HEADS) == 0)
    def _():
        acc_ref[...] = gk_in_ref[...]

    keys, last = k_ref[...], last_ref[...]
    total = jnp.zeros_like(acc_ref)
    for head, n, lanes in step_heads():
        first, second = factors(own_lanes(keys, head), pick_ref, 0, last)
        state, norm = widen(state_ref[n])
        values = gv_in_ref[:, lanes] + mul(first * second, state)
        gv_ref[:, lanes] = values.astype(jnp.bfloat16)
        grad_phi = mul(v_ref[:, lanes], state, "nt") + norm.astype(jnp.float32)
        grad_phi = (grad_phi * last).astype(jnp.bfloat16)
        total = total + chain(grad_phi, first, second, back_ref, 0, head)
    acc_ref[...] += total

    @pl.when(lax.rem(start + STEP_HEADS, HALF_HEADS) == 0)
    def _():
        gk_ref[...] = (acc_ref[...] * FEAT**-0.25).astype(jnp.bfloat16)


def specs(rows):
    return dict(
        pair=pl.BlockSpec((rows, 128), lambda h: (0, h * STEP_HEADS // HALF_HEADS)),
        head=pl.BlockSpec((rows, STEP_HEADS * HEAD_V), lambda h: (0, h)),
        state=pl.BlockSpec((STEP_HEADS, STATE, HEAD_V), lambda h: (h, 0, 0)),
        pick=pl.BlockSpec((3, WIDE, WIDE), lambda h: (0, 0, 0)),
        back=pl.BlockSpec((2, 128, 2 * WIDE), lambda h: (0, 0, 0)),
        column=pl.BlockSpec((rows, 1), lambda h: (0, 0)),
        row=pl.BlockSpec((8, rows), lambda h: (0, 0)),
    )


def heads_call(kernel, rows, ins, outs, scratch=(), name=None):
    table = specs(rows)
    shapes = {
        "pair": (rows, HEADS * FEAT),
        "head": (rows, HEADS * HEAD_V),
        "state": (HEADS, STATE, HEAD_V),
    }
    return pl.pallas_call(
        kernel,
        grid=(HEADS // STEP_HEADS,),
        in_specs=[table[kind] for kind in ins],
        out_specs=[table[kind] for kind, _ in outs],
        out_shape=[jax.ShapeDtypeStruct(shapes[kind], kept) for kind, kept in outs],
        scratch_shapes=list(scratch),
        compiler_params=pltpu.CompilerParams(
            dimension_semantics=("arbitrary",), vmem_limit_bytes=48 * 2**20
        ),
        cost_estimate=pl.CostEstimate(flops=2**20, bytes_accessed=2**16, transcendentals=0),
        name=name,
    )


f32, bf = jnp.float32, jnp.bfloat16


def mix_state(k, v, tables, last):
    rows = k.shape[0]
    return heads_call(state_kernel, rows, ["pair", "head", "pick", "column"],
        [("state", bf)], name="mix_state")(k, v, tables[0], last)[0]


def mix_local(q, k, v, seg_col, seg_row):
    rows = k.shape[0]
    return heads_call(local_kernel, rows, ["pair", "pair", "head", "column", "row"],
        [("head", f32), ("head", f32)], [pltpu.VMEM((rows, rows), bf)], name="mix_local")(q, k, v, seg_col, seg_row)


def mix_prefix(q, num, den, state, tables, reading):
    rows = q.shape[0]
    return heads_call(prefix_kernel, rows, ["pair", "head", "head", "state", "pick", "column"],
        [("head", bf), ("head", f32)], name="mix_prefix")(q, num, den, state, tables[0], reading)


def mix_state_grad(q, g, att, inverse, tables, reading):
    rows = q.shape[0]
    return heads_call(state_grad_kernel, rows, ["pair", "head", "head", "head", "pick", "column"],
        [("state", bf)], name="mix_state_grad")(q, g, att, inverse, tables[0], reading)[0]


def mix_local_grad(q, k, v, g, att, inverse, state, tables, reading, seg_col, seg_row):
    rows = q.shape[0]
    return heads_call(local_grad_kernel, rows,
        ["pair", "pair", "head", "head", "head", "head", "state", "pick", "back", "column", "column", "row"],
        [("pair", bf), ("pair", f32), ("head", f32)],
        [pltpu.VMEM((rows, rows), bf), pltpu.VMEM((rows, 128), f32)], name="mix_local_grad")(
        q, k, v, g, att, inverse, state, *tables, reading, seg_col, seg_row)


def mix_later_grad(k, v, gk, gv, state, tables, last):
    rows = k.shape[0]
    return heads_call(later_grad_kernel, rows,
        ["pair", "head", "pair", "head", "state", "pick", "back", "column"],
        [("pair", bf), ("head", bf)], [pltpu.VMEM((rows, 128), f32)], name="mix_later_grad")(
        k, v, gk, gv, state, *tables, last)


from jax.sharding import PartitionSpec as P

D = 2048
EPSILON = 1e-05
LIMIT = 58 * 2**20
TILE = 352


def cost(flops, moved):
    return pl.CostEstimate(flops=flops, bytes_accessed=moved, transcendentals=0)


def whole(*shape):
    return pl.BlockSpec(shape, lambda *_: (0,) * len(shape), pipeline_mode=pl.Buffered(1))


def tiling(parts, rows):
    if parts == 1:
        taken = TILE if rows % TILE == 0 else rows
        return 1, taken, rows // taken
    taken = max(1, TILE // rows)
    taken = taken if parts % taken == 0 else parts
    return taken, rows, parts // taken


def gate_kernel(x_ref, c_ref, *refs):
    count = len(refs) // 3
    half = x_ref.shape[0] // 2
    for n in range(count):
        both_ref, down_ref, out_ref = refs[2 * n], refs[2 * n + 1], refs[2 * count + n]
        parts, _, rows, _ = both_ref.shape
        gate_w, up_w = [both_ref[:, k].reshape(parts * rows, D) for k in range(2)]
        down_w = down_ref[:, 0].reshape(parts * rows, D)
        for at in (slice(0, half), slice(half, 2 * half)):
            x, c = x_ref[at, :], c_ref[at, :]
            gate = mul(gate_w, x, "nt")
            up = mul(up_w, x, "nt")
            grad = mul(down_w, c, "nt").astype(bf).astype(f32)
            sig = 1.0 / (1.0 + jnp.exp(-gate))
            act = gate * sig
            out_ref[0, :, at] = (grad * up * sig * (1.0 + gate * (1.0 - sig))).astype(bf)
            out_ref[1, :, at] = (grad * act).astype(bf)
            out_ref[2, :, at] = (act * up).astype(bf)


def ffn_gates(x, c, weights):
    rows, count = x.shape[0], len(weights)
    hidden = weights[0][1].shape[0] * weights[0][1].shape[2]
    ins, outs = [whole(rows, D)] * 2, []
    for pair in weights:
        for w in pair:
            taken, height, steps = tiling(w.shape[0], w.shape[2])
            at = (lambda i: (0, 0, i, 0)) if w.shape[0] == 1 else (lambda i: (i, 0, 0, 0))
            ins.append(pl.BlockSpec((taken, w.shape[1], height, D), at))
        outs.append(pl.BlockSpec((3, taken * height, rows), lambda i: (0, i, 0)))
    return pl.pallas_call(
        gate_kernel,
        grid=(steps,),
        in_specs=ins,
        out_specs=outs,
        out_shape=[jax.ShapeDtypeStruct((3, hidden, rows), bf)] * count,
        compiler_params=pltpu.CompilerParams(vmem_limit_bytes=LIMIT),
        cost_estimate=cost(
            6 * rows * D * hidden * count,
            2 * (2 * rows * D + 3 * count * hidden * (D + rows)),
        ),
        name="ffn_gates",
    )(x, c, *[w for pair in weights for w in pair])


def back_kernel(count, *refs):
    made, weights, out_ref, turned = (
        refs[:count], refs[count : 2 * count], refs[-count - 1], refs[-count:]
    )
    added = refs[2 * count : -count - 1]

    @pl.when(pl.program_id(0) == 0)
    def _():
        for block, kept in zip(made, turned):
            kinds, hidden, rows = block.shape
            kept[...] = block[...].reshape(kinds * hidden, rows).T

    total = None
    for kept, w_ref in zip(turned, weights):
        parts, kinds, rows, columns = w_ref.shape
        right = jnp.concatenate(
            [w_ref[:, k].reshape(parts * rows, columns) for k in range(kinds)], axis=0
        )
        part = mul(kept[...], right)
        total = part if total is None else total + part
    for more in added:
        total = total + more[...].astype(f32)
    out_ref[...] = total.astype(out_ref.dtype)


def ffn_back(made, weights, which, added=(), columns=512):
    count = len(weights)
    weights = [pair[which] for pair in weights]
    kinds = weights[0].shape[1]
    _, hidden, rows = made[0].shape
    out = pl.BlockSpec((rows, columns), lambda j: (0, j))
    ins = [
        pl.BlockSpec(
            (kinds, hidden, rows), lambda j: (2 * which // kinds, 0, 0), pipeline_mode=pl.Buffered(1)
        )
    ] * count
    for w in weights:
        ins.append(pl.BlockSpec((w.shape[0], kinds, w.shape[2], columns), lambda j: (0, 0, 0, j)))
    ins += [out] * len(added)
    return pl.pallas_call(
        functools.partial(back_kernel, count),
        grid=(D // columns,),
        in_specs=ins,
        out_specs=out,
        out_shape=jax.ShapeDtypeStruct((rows, D), bf),
        scratch_shapes=[pltpu.VMEM((rows, kinds * hidden), bf)] * count,
        compiler_params=pltpu.CompilerParams(vmem_limit_bytes=LIMIT),
        cost_estimate=cost(
            2 * rows * D * hidden * kinds * count,
            2 * (count * kinds * hidden * (D + rows) + rows * D),
        ),
        name="ffn_back",
    )(*made, *weights, *added)


def grad_kernel(blocks, *refs):
    made, xs, cs = refs[:blocks], refs[blocks : 2 * blocks], refs[2 * blocks : 3 * blocks]
    added, out_ref = refs[3 * blocks : -1], refs[-1]
    parts, _, rows, _ = out_ref.shape

    def write(rights):
        total = None
        for left, right in zip(made, rights):
            part = mul(left[0], right[...])
            total = part if total is None else total + part
        for more in added:
            total = total + more[...].reshape(parts * rows, D).astype(f32)
        out_ref[...] = total.astype(bf).reshape(parts, 1, rows, D)

    kind = pl.program_id(0)

    @pl.when(kind < 2)
    def _():
        write(xs)

    @pl.when(kind == 2)
    def _():
        write(cs)


def ffn_grad(made, xs, cs, parts, height, added=None):
    blocks = len(made)
    rows = xs[0].shape[0]
    hidden = made[0].shape[1]
    taken, rise, steps = tiling(parts, height)
    left = pl.BlockSpec((1, taken * rise, rows), lambda k, i: (k, i, 0))
    at = (lambda k, i: (0, k, i, 0)) if parts == 1 else (lambda k, i: (i, k, 0, 0))
    out = pl.BlockSpec((taken, 1, rise, D), at)
    more = [] if added is None else [added]
    return pl.pallas_call(
        functools.partial(grad_kernel, blocks),
        grid=(3, steps),
        in_specs=[left] * blocks + [whole(rows, D)] * (2 * blocks) + [out] * len(more),
        out_specs=out,
        out_shape=jax.ShapeDtypeStruct((parts, 3, height, D), bf),
        compiler_params=pltpu.CompilerParams(vmem_limit_bytes=LIMIT),
        cost_estimate=cost(
            6 * rows * D * hidden * blocks,
            2 * (2 * blocks * rows * D + 3 * hidden * (rows * blocks + D * (1 + len(more)))),
        ),
        name="ffn_grad",
    )(*made, *xs, *cs, *more)


def widen_kernel(sum_ref, *out_refs):
    for kind, out_ref in enumerate(out_refs):
        out_ref[...] = sum_ref[0, kind].astype(f32)


def widened(sums):
    parts, _, height, _ = sums.shape
    return pl.pallas_call(
        widen_kernel,
        grid=(parts,),
        in_specs=[pl.BlockSpec((1, 3, height, D), lambda i: (i, 0, 0, 0))],
        out_specs=[pl.BlockSpec((height, D), lambda i: (i, 0))] * 3,
        out_shape=[jax.ShapeDtypeStruct((parts * height, D), f32)] * 3,
        compiler_params=pltpu.CompilerParams(vmem_limit_bytes=LIMIT),
        cost_estimate=cost(0, 6 * parts * 3 * height * D),
        name="widened",
    )(sums)


def qkv_grad_kernel(n_ref, gq_ref, gk_ref, gv_ref, out_ref):
    turned = n_ref[...].T
    qk = gq_ref.shape[1]
    out_ref[:, :qk] = mul(turned, gq_ref[...]).astype(bf)
    out_ref[:, qk : 2 * qk] = mul(turned, gk_ref[...]).astype(bf)
    out_ref[:, 2 * qk :] = mul(turned, gv_ref[...]).astype(bf)


def qkv_grad(normed, gq, gk, gv):
    rows, qk = gq.shape
    columns = 2 * qk + D
    tile = 256
    return pl.pallas_call(
        qkv_grad_kernel,
        grid=(D // tile,),
        in_specs=[
            pl.BlockSpec((rows, tile), lambda i: (0, i)), whole(rows, qk), whole(rows, qk), whole(rows, D)
        ],
        out_specs=pl.BlockSpec((tile, columns), lambda i: (i, 0)),
        out_shape=jax.ShapeDtypeStruct((D, columns), bf),
        compiler_params=pltpu.CompilerParams(vmem_limit_bytes=LIMIT),
        cost_estimate=cost(2 * rows * D * columns, 2 * (rows * (D + columns) + D * columns)),
        name="qkv_grad",
    )(normed, gq, gk, gv)


def norm_forward(inputs):
    inverse = lax.rsqrt(jnp.mean(inputs * inputs, axis=-1, keepdims=True) + EPSILON)
    return (inputs * inverse, inverse)


def norm_backward(grad_normed, unit_rows, inverse, gain_vec):
    gain_grad = jnp.sum(grad_normed * unit_rows, axis=0)
    grad_unit = grad_normed * gain_vec
    return (
        inverse * (grad_unit - unit_rows * jnp.mean(grad_unit * unit_rows, axis=-1, keepdims=True)),
        gain_grad,
    )


def move(array, target, axis="mp"):
    size = lax.axis_size(axis)
    pairs = [(m, target(m)) for m in range(size)]
    return lax.ppermute(array, axis, [(m, t) for m, t in pairs if t is not None])


def then(value, *before):
    return lax.optimization_barrier((value, before))[0]


def beside(array, mover, *works):
    ends = [array.shape[0] * n // len(works) // 16 * 16 for n in range(len(works))] + [array.shape[0]]
    moved, made = [], []
    for n, work in enumerate(works):
        share = array[ends[n] : ends[n + 1]]
        if made:
            share = then(share, made[-1])
        result = work(share, made)
        arrived, result = lax.optimization_barrier((mover(share), result))
        moved.append(arrived)
        made.append(result)
    return jnp.concatenate(moved, axis=0), made


def to_mate(array):
    return move(array, lambda m: m ^ 1)


def to_half(array):
    size = lax.axis_size("mp")
    return move(array, lambda m: (m + size // 2) % size)


def to_peer(array, step):
    half = lax.axis_size("mp") // 2

    def target(m):
        low = m % half
        return m - low + (low + 2 * step) % half

    return move(array, target)


def to_chip(array, step):
    size = lax.axis_size("mp")
    return move(array, lambda m: m + 2 * step if 0 <= m + 2 * step < size else None)


def sums_before(own, sign, *beside, made=None):
    core = lax.axis_index("mp") % 2
    chips = lax.axis_size("mp") // 2
    wire = own.astype(bf)
    mate = to_mate(wire).astype(f32)
    half = own.shape[0] // 2
    both = wire.astype(f32) + mate
    running = lax.dynamic_slice_in_dim(both, core * half, half, 0)
    before = jnp.zeros_like(running)
    step, beside, made = 1, list(beside), [] if made is None else made
    while step < chips:
        came = to_chip(running.astype(bf), sign * step)
        if beside:
            came, result = lax.optimization_barrier((came, beside.pop(0)(running)))
            made.append(result)
        came = came.astype(f32)
        before = before + came
        running = running + came
        step *= 2
    before = before.astype(bf)
    other = to_mate(before)
    first = jnp.where(core == 0, before, other)
    second = jnp.where(core == 0, other, before)
    total = jnp.concatenate([first, second], axis=0).astype(f32)
    inner = core == (1 if sign > 0 else 0)
    return (total + jnp.where(inner, mate, 0.0)).astype(bf), made


def pick(array, index, dim=0):
    return lax.dynamic_index_in_dim(array, index, dim, keepdims=False)


def chip_halves(array):
    groups, size = lax.axis_size("dp"), lax.axis_size("mp")
    core = lax.axis_index("mp") % 2
    rows, columns = array.shape[0] // (groups * size), array.shape[1]
    blocks = array.reshape(groups, size // 2, 2, rows, columns)
    return pick(blocks, core, 2), pick(blocks, 1 - core, 2)


def add(first, *more, kept=bf):
    total = first.astype(f32)
    for array in more:
        total = total + array.astype(f32)
    return total.astype(kept)


def placed(shares, places):
    out = jnp.zeros((len(shares),) + shares[0].shape, shares[0].dtype)
    for share, at in zip(shares, places):
        out = lax.dynamic_update_index_in_dim(out, share, at, 0)
    return out


def chip_shares(array):
    steps = range(1, lax.axis_size("mp") // 2)
    return [move(array, lambda m: m ^ (2 * step)) for step in steps]


def by_chip(array, shares):
    chip = lax.axis_index("mp") // 2
    return placed([array] + shares, [chip ^ step for step in range(len(shares) + 1)])


def first_groups(array):
    return [move(array, lambda m: m ^ step, "dp") for step in (1, 2)]


def third_group(first, second):
    half = first.shape[0] // 2
    return [
        move(second[:half], lambda m: m ^ 1, "dp"),
        move(first[half:], lambda m: m ^ 2, "dp"),
    ]


def assembled(pieces, groups, chips, out=None):
    group, core = lax.axis_index("dp"), lax.axis_index("mp") % 2
    shape = pieces[0][2].shape[1:]
    if out is None:
        out = jnp.zeros((groups, chips, 2) + shape, bf)
    for step, at, own, other in pieces:
        both = jnp.where(core == 0, jnp.stack([own, other], 1), jnp.stack([other, own], 1))
        start = (group ^ step, at) + (0,) * (len(shape) + 1)
        out = lax.dynamic_update_slice(out, both[None], start)
    return out


def group_move(array, step):
    return move(pick(array, lax.axis_index("dp") ^ step), lambda m: m ^ step, "dp")


def chip_moves(array):
    chip = lax.axis_index("mp") // 2
    return [
        move(pick(array, chip ^ step), lambda m: m ^ (2 * step))
        for step in range(1, lax.axis_size("mp") // 2)
    ]


def sum_everywhere(array):
    for axis in ("mp", "dp"):
        step = 1
        while step < lax.axis_size(axis):
            array = array + move(array, lambda m: m ^ step, axis)
            step *= 2
    return array


def body(
    x_in,
    seq_lengths,
    norm1_gain,
    w_query,
    w_key,
    w_value,
    w_out,
    norm2_gain,
    w_gate,
    w_up,
    w_down,
    cotangent,
):
    rows = x_in.shape[0]
    groups = lax.axis_size("dp")
    size = lax.axis_size("mp")
    peers = size // 4
    hidden = w_gate.shape[1]
    piece = hidden // groups
    place = lax.axis_index("mp")
    group = lax.axis_index("dp")
    everywhere = ("dp", "mp")
    qk = w_query.shape[1]
    aligned = piece % 16 == 0

    own_rows = w_query.shape[0]
    gain_block = jnp.concatenate(
        [norm1_gain[:, None], norm2_gain[:, None], jnp.zeros((own_rows, 126), bf)], axis=1
    )
    packed = jnp.concatenate([w_query, w_key, w_value, gain_block], axis=1)
    in_chips, packed = lax.optimization_barrier((chip_shares(packed), packed))
    in_chips = by_chip(packed, in_chips)

    full_out = lax.all_gather(w_out, everywhere, axis=0, tiled=True)
    half_chips = size // 4
    mine_both = jnp.concatenate(then([w_gate.T, w_up.T], in_chips), axis=0)
    mine = (mine_both.reshape(1, 2, hidden, D), then(w_down, in_chips).reshape(1, 1, hidden, D))
    far_down = lax.dynamic_slice_in_dim(mine[1][0, 0], group * piece, piece, 0)
    far_both = lax.dynamic_slice_in_dim(mine[0][0], group * piece, piece, 1).reshape(2 * piece, D)
    cot_ends = [rows * n // 16 for n in (0, 3, 6, 10, 13, 16)]
    cot_shares = [cotangent[a:b] for a, b in zip(cot_ends, cot_ends[1:])]

    def peers_of(array):
        return [to_peer(array, step) for step in range(1, peers)]

    def beside_one(array, mover, work):
        return lax.optimization_barrier((mover(array), work(array)))

    both_cut, down_cut = 2 * piece * 8 // 11, piece * 7 // 11
    blank = jnp.zeros((groups, size // 2, 2) + packed.shape, bf)
    blank, in_near, in_mate, both_first = lax.optimization_barrier(
        (
            blank,
            first_groups(in_chips),
            to_mate(in_chips),
            to_half(then(far_both[:both_cut], in_chips)),
        )
    )
    full_in, in_third, in_mates, both_second = lax.optimization_barrier(
        (
            assembled([(0, 0, in_chips, in_mate)], groups, size // 2, blank),
            third_group(*in_near),
            [to_mate(share) for share in in_near],
            to_half(then(far_both[both_cut:], in_near)),
        )
    )
    in_mates = [*in_mates] + [to_mate(share) for share in in_third]
    far_both = jnp.concatenate([both_first, both_second], axis=0)
    far_both = lax.all_gather(far_both, "dp", axis=0, tiled=True).reshape(groups, 2, piece, D)
    down_first = to_half(then(far_down[:down_cut], in_third))
    mate_down = to_mate(then(mine[1], in_third))
    cot_third = peers_of(then(cot_shares[2], in_third))
    in_pieces = [
        (step, at, own, other)
        for (step, at, own), other in zip(
            (
                (1, 0, in_near[0]),
                (2, 0, in_near[1]),
                (3, 0, in_third[0]),
                (3, half_chips, in_third[1]),
            ),
            in_mates,
        )
    ]
    full_in = assembled(in_pieces, groups, size // 2, full_in).reshape(D, packed.shape[1])

    row_start = place * rows
    seq_ends = jnp.cumsum(seq_lengths[0], dtype=jnp.int32)
    positions = row_start + jnp.arange(rows, dtype=jnp.int32)
    segments = jnp.sum((positions[:, None] >= seq_ends[None, :]).astype(jnp.int32), axis=1)
    seg_before = jnp.sum((row_start - 1 >= seq_ends).astype(jnp.int32))
    reading = ((segments == seg_before) & (row_start > 0)).astype(f32)[:, None]
    last_doc = (segments == segments[-1]).astype(f32)[:, None]
    seg_col = segments[:, None]
    seg_row = jnp.broadcast_to(segments[None, :], (8, rows))
    tables = feature_tables()

    inputs = x_in.astype(f32)
    inverse_one = norm_forward(inputs)[1]
    early = (full_out, mine, down_first, mate_down, cot_third, inverse_one, reading, last_doc, seg_col, seg_row)
    full_in, early = lax.optimization_barrier((full_in, early))
    full_out, mine, down_first, mate_down, cot_third, inverse_one, reading, last_doc, seg_col, seg_row = early
    gain_one = full_in[:, 2 * qk + D].astype(f32)
    gain_two = full_in[:, 2 * qk + D + 1].astype(f32)
    full_qkv = full_in[:, : 2 * qk + D]
    unit_one = inputs * inverse_one
    normed_one = (unit_one * gain_one).astype(bf)
    (got, mate_gate, down_second), qkv = beside_one(
        then(cot_shares[3], full_in),
        lambda ready: (
            peers_of(ready),
            to_mate(then(w_gate.T, ready)).reshape(1, 1, hidden, D),
            to_half(then(far_down[down_cut:], ready)),
        ),
        lambda ready: mul(then(normed_one, ready), full_qkv).astype(bf),
    )
    cot_got = [cot_third, got]
    queries, keys, values = qkv[:, :qk], qkv[:, qk : 2 * qk], qkv[:, 2 * qk :]
    far_down = jnp.concatenate([down_first, down_second], axis=0)
    far_down = lax.all_gather(far_down, "dp", axis=0, tiled=True).reshape(groups, 1, piece, D)
    (got, mate_up), own_state = beside_one(
        then(cot_shares[4], qkv),
        lambda ready: (peers_of(ready), to_mate(then(w_up.T, ready)).reshape(1, 1, hidden, D)),
        lambda ready: mix_state(then(keys, ready), values, tables, last_doc),
    )
    cot_got.append(got)

    def local_work(ready):
        local = mix_local(then(queries, ready), keys, values, seg_col, seg_row)
        return local

    def pack_work(ready):
        gate, up = then((mate_gate, mate_up), ready)
        return jnp.concatenate([gate, up], axis=1)

    prefix, [(num, den), mate_both] = sums_before(own_state, 1, local_work, pack_work)
    cot_first, (attended, inverse_den) = beside_one(
        then(cot_shares[0], prefix),
        peers_of,
        lambda ready: mix_prefix(then(queries, ready), num, den, prefix, tables, reading),
    )
    mate = (mate_both, mate_down)
    near = [mine, mate]
    cot_second, hidden_in = beside_one(
        then(cot_shares[1], attended),
        peers_of,
        lambda ready: inputs + mul(then(attended, ready), full_out),
    )
    cot_got = [cot_first, cot_second] + cot_got
    unit_two, inverse_two = norm_forward(hidden_in)
    normed_two = (unit_two * gain_two).astype(bf)
    came = [to_peer(normed_two, step) for step in range(1, peers)]

    near_own = ffn_gates(normed_two, cotangent, near)
    far_mine = then((far_both, far_down), normed_two)
    if not aligned:
        far_mine = tuple(jnp.swapaxes(w, 0, 1).reshape(1, -1, hidden, D) for w in far_mine)
    far_mate = then(tuple(to_mate(w) for w in far_mine), near_own)
    far = [tuple(far_mine), far_mate]
    weights = near + far
    shape = (groups, piece) if aligned else (1, hidden)
    far_own = ffn_gates(normed_two, cotangent, far)
    made_own = list(near_own) + list(far_own)
    grad_own = ffn_back(made_own, weights, 0)
    normed = [normed_two] + then(came, grad_own)
    cot_got = then(cot_got, near_own)
    cots = [cotangent] + [jnp.concatenate(parts, axis=0) for parts in zip(*cot_got)]
    near_made = [near_own] + [ffn_gates(x, c, near) for x, c in zip(normed[1:], cots[1:])]
    far_made = [far_own] + [
        ffn_gates(x, c, then(far, near_made)) for x, c in zip(normed[1:], cots[1:])
    ]
    made = [list(a) + list(b) for a, b in zip(near_made, far_made)]

    def weight_grads(made, ready, added=None):
        return ffn_grad(then(made, ready), normed, cots, *shape, added)

    def over_groups(grad):
        if not aligned:
            grad = jnp.swapaxes(grad.reshape(3, groups, piece, D), 0, 1)
        return lax.psum_scatter(
            grad.reshape(groups * 3 * piece, D), "dp", scatter_dimension=0, tiled=True
        )

    def back(block, which, ready):
        return ffn_back(then(block, ready), weights, which)

    far_given = weight_grads([block[1] for block in far_made], far_made)
    far_sent = to_mate(far_given)
    grad_parts = [back(block, 0, far_given) for block in made[1:]]

    def owners(parts):
        return [to_peer(part, peers - step) for step, part in enumerate(parts, 1)]

    def stacked(parts):
        return jnp.concatenate([part[:, None] for part in parts], axis=1)

    def to_owners(parts):
        return stacked(owners([parts[:, n] for n in range(peers - 1)]))

    def near_work(ready, _):
        given = weight_grads([block[1] for block in near_made], ready)
        return given

    def far_work(ready, done):
        kept = weight_grads([block[0] for block in far_made], ready, far_sent)
        return kept, to_mate(then(done[0], ready))

    def last_work(ready, done):
        return weight_grads([block[0] for block in near_made], ready, done[1][1])

    grad_sent, (_, (far_kept, _), near_kept) = beside(
        stacked(grad_parts), to_owners, near_work, far_work, last_work
    )
    far_part = over_groups(far_kept)
    near_part = over_groups(near_kept)
    grad_normed_two = jnp.sum(grad_sent.astype(f32), axis=1) + grad_own.astype(f32)

    grad_two, gain_two_grad = norm_backward(grad_normed_two, unit_two, inverse_two, gain_two)
    grad_hidden_in = cotangent.astype(f32) + grad_two
    grad_branch = grad_hidden_in.astype(bf)
    grad_attended = mul(grad_branch, full_out, "nt").astype(bf)
    state_grad = mix_state_grad(queries, grad_attended, attended, inverse_den, tables, reading)

    def local_grads(ready):
        local = mix_local_grad(
            then(queries, ready), keys, values, grad_attended, attended, inverse_den, prefix, tables,
            reading, seg_col, seg_row,
        )
        return local, to_mate(then(out_halves[1], ready))

    out_halves = []

    def out_work(ready):
        halves = chip_halves(mul(then(attended, ready), grad_branch, "tn").astype(bf))
        out_halves.extend(halves)
        return halves

    later, [_, (local, out_came)] = sums_before(state_grad, -1, out_work, local_grads)
    grad_queries, part_keys, part_values = local
    out_kept = add(out_halves[0], out_came)
    out_kept, far_part = then((out_kept, far_part), later)
    ends = [far_part.shape[0] * n // 33 for n in (0, 3, 9, 16, 22, 33)]
    far_shares = [far_part[a:b] for a, b in zip(ends, ends[1:])]
    out_first, out_second, out_diag = [pick(out_kept, group ^ step) for step in range(1, groups)]
    low, high = slice(None, half_chips), slice(half_chips, None)

    def by_first(block):
        return move(block, lambda m: m ^ 1, "dp")

    def by_second(block):
        return move(block, lambda m: m ^ 2, "dp")

    (far_first, for_second, for_first), (grad_keys, grad_values) = beside_one(
        then(far_shares[0], out_kept),
        lambda ready: (
            to_half(ready), by_first(then(out_diag[low], ready)), by_second(then(out_diag[high], ready))
        ),
        lambda ready: mix_later_grad(
            then(keys, ready), values, part_keys, part_values, later, tables, last_doc
        ),
    )
    out_second = [add(out_second[low], for_second), out_second[high]]
    out_first = [out_first[low], add(out_first[high], for_first)]
    (out_low, far_slot), in_grad = beside_one(
        then((out_first[0], out_second[0]), grad_keys),
        lambda ready: (
            [by_first(ready[0]), by_second(ready[1])], to_half(then(far_shares[1], ready))
        ),
        lambda ready: qkv_grad(then(normed_one, ready), grad_queries, grad_keys, grad_values),
    )
    in_keep, in_give = chip_halves(in_grad)
    out_parts = [back(block, 1, in_grad) for block in made[1:]]
    out_parts, in_came, out_high, far_second = lax.optimization_barrier(
        (
            out_parts,
            to_mate(in_give),
            [by_first(then(out_first[1], in_grad)), by_second(then(out_second[1], in_grad))],
            to_half(then(far_shares[2], in_grad)),
        )
    )
    in_diag = add(pick(in_keep, group ^ 3), pick(in_came, group ^ 3))
    in_first, in_second = [
        add(pick(in_keep, group ^ step), pick(in_came, group ^ step)) for step in (1, 2)
    ]
    grad_queries, grad_keys, grad_values = then(
        (grad_queries, grad_keys, grad_values), (in_diag, in_first, in_second)
    )
    grad_normed_one = (
        mul(grad_queries, full_qkv[:, :qk], "nt")
        + mul(grad_keys, full_qkv[:, qk : 2 * qk], "nt")
        + mul(grad_values, full_qkv[:, 2 * qk :], "nt")
    )
    out_split = jnp.split(stacked(out_parts), [rows * 3 // 8], axis=0)
    out_early, for_second, for_first, far_third, grad_normed_one, in_first, in_second = (
        lax.optimization_barrier(
            (
                to_owners(then(out_split[0], in_diag)),
                by_first(in_diag[low]),
                by_second(in_diag[high]),
                to_half(then(far_shares[3], in_diag)),
                grad_normed_one,
                in_first,
                in_second,
            )
        )
    )
    in_first = jnp.concatenate([in_first[low], add(in_first[high], for_first)], axis=0)
    in_second = jnp.concatenate([add(in_second[low], for_second), in_second[high]], axis=0)
    in_moved = [by_first(in_first), by_second(in_second)]
    far_last = to_half(then(far_shares[4], in_first))
    grad_normed_one = then(grad_normed_one, (in_first, in_second))
    grad_one, gain_one_grad = norm_backward(grad_normed_one, unit_one, inverse_one, gain_one)
    input_grad = (grad_hidden_in + grad_one).astype(bf)
    input_grad, gain_one_grad, in_moved, far_last = lax.optimization_barrier(
        (input_grad, gain_one_grad, in_moved, far_last)
    )
    out_own = back(made[0], 1, in_moved)
    far_sum = jnp.concatenate([far_first, far_slot, far_second, far_third, far_last], axis=0)
    ffn_sum = lax.all_gather(add(near_part, far_sum), "dp", axis=0, tiled=True)
    ffn_sum = ffn_sum.reshape(groups, 3, piece, D)
    chip = place // 2

    def over_chips(blocks, kept):
        shares = [
            add(*[pick(block, chip ^ step) for block in blocks]) for step in range(1, size // 2)
        ]
        moved = [move(share, lambda m: m ^ (2 * step)) for step, share in enumerate(shares, 1)]
        return add(*[pick(block, chip) for block in blocks], *moved, kept=kept)

    in_sum = over_chips([pick(in_keep, group), pick(in_came, group), *in_moved], f32)
    out_blocks = [jnp.concatenate(pair, axis=0) for pair in zip(out_low, out_high)]
    out_blocks = then([pick(out_kept, group), *out_blocks], in_moved)
    out_sum = over_chips(out_blocks, f32)
    if not aligned:
        ffn_sum = jnp.swapaxes(ffn_sum, 0, 1).reshape(1, 3, hidden, D)
    gate_grad, up_grad, down_grad = widened(ffn_sum)
    gain_sums = sum_everywhere(jnp.stack([gain_one_grad, gain_two_grad]))
    gain_sums = lax.dynamic_slice_in_dim(
        gain_sums, (group * size + place) * own_rows, own_rows, 1
    )
    out_last = to_owners(then(out_split[1], in_sum, gain_sums))
    out_sent = jnp.concatenate([out_early, out_last], axis=0)
    output = (hidden_in + jnp.sum(out_sent.astype(f32), axis=1) + out_own.astype(f32)).astype(bf)
    return (
        output,
        input_grad,
        gain_sums[0],
        in_sum[:, :qk],
        in_sum[:, qk : 2 * qk],
        in_sum[:, 2 * qk :],
        out_sum,
        gain_sums[1],
        gate_grad.T,
        up_grad.T,
        down_grad,
    )


def solution(mesh):
    rows, vector = P(("dp", "mp"), None), P(("dp", "mp"))
    columns, down = P(None, "mp"), P("mp", None)
    return jax.shard_map(
        body,
        mesh=mesh,
        in_specs=(rows, P("dp", None), vector, rows, rows, rows, rows, vector, columns, columns, down, rows),
        out_specs=(rows, rows, vector, rows, rows, rows, rows, vector, columns, columns, down),
        check_vma=False,
    )
```

```python
import functools
import numpy as np
import jax
import jax.numpy as jnp
from jax import lax
from jax.experimental import pallas as pl
from jax.experimental.pallas import tpu as pltpu

HEADS = 16
FEAT = 16
HEAD_V = 128
WIDE = 256
STATE = 160
SQUARES = FEAT * (FEAT + 1) // 2
LINEAR = SQUARES + FEAT
HALF_HEADS = 128 // FEAT
STEP_HEADS = 8


def feature_tables():
    pairs = [(a, b) for a in range(FEAT) for b in range(a, FEAT)]
    pick = np.zeros((3, WIDE, WIDE), np.float32)
    for row in range(128):
        for entry, (a, b) in enumerate(pairs):
            if row % FEAT == a:
                pick[0, row, entry] = 1.0
                pick[1, row, entry] = 0.5 if a == b else 1.0
            if row % FEAT == b:
                pick[2, row, entry] = 1.0
        pick[0:2, row, SQUARES + row % FEAT] = 1.0
    pick[0:2, 128, LINEAR] = 1.0
    pick[2, 128, SQUARES : LINEAR + 1] = 1.0
    back = np.stack([np.concatenate([pick[n, :128], pick[2, :128]], axis=1) for n in (0, 1)])
    return jnp.asarray(pick, jnp.bfloat16), jnp.asarray(back, jnp.bfloat16)


def mul(left, right, kind="nn"):
    dims = {"nn": ((1,), (0,)), "nt": ((1,), (1,)), "tn": ((0,), (0,))}[kind]
    return lax.dot_general(left, right, (dims, ((), ())), preferred_element_type=jnp.float32)


def head_lanes(head, rows):
    lane = lax.broadcasted_iota(jnp.int32, (rows, 128), 1)
    return lane // FEAT == lax.rem(head, HALF_HEADS)


def own_lanes(block, head):
    scaled = block * jnp.asarray(FEAT**-0.25, jnp.bfloat16)
    return jnp.where(head_lanes(head, block.shape[0]), scaled, jnp.zeros_like(scaled))


def first_lanes(*columns):
    lane = lax.broadcasted_iota(jnp.int32, (columns[0].shape[0], 128), 1)
    out = jnp.zeros(lane.shape, jnp.float32)
    for n, column in enumerate(columns):
        out = jnp.where(lane == n, column, out)
    return out.astype(jnp.bfloat16)


def factors(own, pick_ref, which, kept):
    ones = first_lanes(jnp.ones_like(kept))
    plain = jnp.concatenate([own, ones], axis=1)
    masked = jnp.concatenate(
        [own * kept.astype(jnp.bfloat16), ones * kept.astype(jnp.bfloat16)], axis=1
    )
    first = mul(masked, pick_ref[which]).astype(jnp.bfloat16)
    second = mul(plain, pick_ref[2]).astype(jnp.bfloat16)
    return first, second


def pack_state(state, norm_rows):
    row = lax.broadcasted_iota(jnp.int32, (STATE, HEAD_V), 0)
    out = jnp.where(row == LINEAR + 1, norm_rows[0:1, :HEAD_V], state[:STATE])
    return jnp.where(row == LINEAR + 2, norm_rows[0:1, HEAD_V:], out)


def widen(packed):
    padded = jnp.concatenate([packed, jnp.zeros((WIDE - STATE, HEAD_V), packed.dtype)], axis=0)
    norm = jnp.concatenate(
        [packed[LINEAR + 1 : LINEAR + 2, :], packed[LINEAR + 2 : LINEAR + 3, :]], axis=1
    )
    return padded, norm


def step_heads():
    first = pl.program_id(0) * STEP_HEADS
    return [
        (first + n, n, slice(n * HEAD_V, (n + 1) * HEAD_V)) for n in range(STEP_HEADS)
    ]


def state_kernel(k_ref, v_ref, pick_ref, last_ref, out_ref):
    keys, last = k_ref[...], last_ref[...]
    ones = jnp.ones((16, keys.shape[0]), jnp.bfloat16)
    for head, n, lanes in step_heads():
        first, second = factors(own_lanes(keys, head), pick_ref, 0, last)
        phi = first * second
        state = mul(phi, v_ref[:, lanes], "tn")
        out_ref[n] = pack_state(state, mul(ones, phi)).astype(out_ref.dtype)


def causal_mask(seg_col_ref, seg_row_ref, mask_ref):
    rows = mask_ref.shape[0]
    i = lax.broadcasted_iota(jnp.int32, (rows, rows), 0)
    j = lax.broadcasted_iota(jnp.int32, (rows, rows), 1)
    keep = (seg_col_ref[...] == seg_row_ref[0:1, :]) & (j <= i)
    mask_ref[...] = keep.astype(jnp.float32).astype(jnp.bfloat16)


def triangle(rows):
    half = rows // 2
    return ((slice(0, half), slice(0, half)), (slice(half, rows), slice(0, rows)))


def local_kernel(q_ref, k_ref, v_ref, seg_col_ref, seg_row_ref, num_ref, den_ref, mask_ref):
    @pl.when(pl.program_id(0) == 0)
    def _():
        causal_mask(seg_col_ref, seg_row_ref, mask_ref)

    queries = q_ref[...]
    scaled = k_ref[...] * jnp.asarray(FEAT**-0.25, jnp.bfloat16)
    for head, _, lanes in step_heads():
        own_q = own_lanes(queries, head)
        value = v_ref[:, lanes]
        wide = jnp.concatenate([value, jnp.ones_like(value)], axis=1)
        for at, upto in triangle(own_q.shape[0]):
            up = 1.0 + mul(own_q[at], scaled[upto], "nt")
            kappa = (0.5 * up * up + 0.5).astype(jnp.bfloat16) * mask_ref[at, upto]
            both = mul(kappa, wide[upto])
            num_ref[at, lanes] = both[:, :HEAD_V]
            den_ref[at, lanes] = both[:, HEAD_V:]


def prefix_kernel(
    q_ref, num_ref, den_ref, state_ref, pick_ref, reading_ref, out_ref, inverse_ref
):
    queries, reading = q_ref[...], reading_ref[...]
    for head, n, lanes in step_heads():
        first, second = factors(own_lanes(queries, head), pick_ref, 1, reading)
        phi = first * second
        state, norm = widen(state_ref[n])
        num = num_ref[:, lanes] + mul(phi, state)
        norm = mul(phi, jnp.broadcast_to(norm, (HEAD_V, WIDE)), "nt")
        inverse = 1.0 / (den_ref[:, lanes] + norm)
        out_ref[:, lanes] = (num * inverse).astype(jnp.bfloat16)
        inverse_ref[:, lanes] = inverse


def scaled_grad(g_ref, att_ref, inverse_ref, lanes):
    gn = (g_ref[:, lanes].astype(jnp.float32) * inverse_ref[:, lanes]).astype(jnp.bfloat16)
    mixed = att_ref[:, lanes].astype(jnp.float32)
    gd = -jnp.sum(gn.astype(jnp.float32) * mixed, axis=1, keepdims=True)
    return gn, gd


def state_grad_kernel(q_ref, g_ref, att_ref, inverse_ref, pick_ref, reading_ref, out_ref):
    queries, reading = q_ref[...], reading_ref[...]
    for head, n, lanes in step_heads():
        gn, gd = scaled_grad(g_ref, att_ref, inverse_ref, lanes)
        first, second = factors(own_lanes(queries, head), pick_ref, 1, reading)
        phi = first * second
        state = mul(phi, gn, "tn")
        wide = jnp.broadcast_to(gd, gn.shape).astype(jnp.bfloat16)
        out_ref[n] = pack_state(state, mul(wide, phi, "tn")).astype(out_ref.dtype)


def chain(grad_phi, first, second, back_ref, which, head):
    both = jnp.concatenate([grad_phi * second, grad_phi * first], axis=1)
    grad = mul(both, back_ref[which], "nt")
    return jnp.where(head_lanes(head, grad_phi.shape[0]), grad, 0.0)


def local_grad_kernel(
    q_ref, k_ref, v_ref, g_ref, att_ref, inverse_ref, state_ref, pick_ref, back_ref,
    reading_ref, seg_col_ref, seg_row_ref, gq_ref, gk_ref, gv_ref, mask_ref, acc_ref,
):
    start = pl.program_id(0) * STEP_HEADS

    @pl.when(start == 0)
    def _():
        causal_mask(seg_col_ref, seg_row_ref, mask_ref)

    @pl.when(lax.rem(start, HALF_HEADS) == 0)
    def _():
        acc_ref[...] = jnp.zeros_like(acc_ref)
        gk_ref[...] = jnp.zeros_like(gk_ref)

    queries, keys, reading = q_ref[...], k_ref[...], reading_ref[...]
    half = queries.shape[0] // 2
    query_sums = jnp.zeros_like(acc_ref)
    key_sums = jnp.zeros_like(gk_ref)
    for head, n, lanes in step_heads():
        gn, gd = scaled_grad(g_ref, att_ref, inverse_ref, lanes)
        high = gd.astype(jnp.bfloat16).astype(jnp.float32)
        gn_wide = jnp.concatenate([gn, first_lanes(high, gd - high)], axis=1)
        ones = jnp.ones_like(gd)
        v_wide = jnp.concatenate([v_ref[:, lanes], first_lanes(ones, ones)], axis=1)
        own_q = own_lanes(queries, head)
        own_k = own_lanes(keys, head)
        parts, query_parts, key_parts = [], [], []
        for at, upto in triangle(own_q.shape[0]):
            keep = mask_ref[at, upto]
            up = 1.0 + mul(own_q[at], own_k[upto], "nt")
            kappa = (0.5 * up * up + 0.5).astype(jnp.bfloat16) * keep
            grad_t = mul(gn_wide[at], v_wide[upto], "nt").astype(jnp.bfloat16)
            grad_t = grad_t * up.astype(jnp.bfloat16) * keep
            query_parts.append(mul(grad_t, own_k[upto]))
            key_parts.append(mul(grad_t, own_q[at], "tn"))
            parts.append(mul(kappa, gn[at], "tn"))
        gv_ref[:half, lanes] = parts[0] + parts[1][:half]
        gv_ref[half:, lanes] = parts[1][half:]
        key_sums += key_parts[1] + jnp.concatenate(
            [key_parts[0], jnp.zeros_like(key_parts[0])], axis=0
        )
        first, second = factors(own_q, pick_ref, 1, reading)
        state, norm = widen(state_ref[n])
        grad_phi = mul(gn, state, "nt") + gd * norm.astype(jnp.float32)
        grad_phi = (grad_phi * reading).astype(jnp.bfloat16)
        query_sums += jnp.concatenate(query_parts, axis=0)
        query_sums += chain(grad_phi, first, second, back_ref, 1, head)
    acc_ref[...] += query_sums
    gk_ref[...] += key_sums

    @pl.when(lax.rem(start + STEP_HEADS, HALF_HEADS) == 0)
    def _():
        gq_ref[...] = (acc_ref[...] * FEAT**-0.25).astype(jnp.bfloat16)


def later_grad_kernel(
    k_ref, v_ref, gk_in_ref, gv_in_ref, state_ref, pick_ref, back_ref, last_ref,
    gk_ref, gv_ref, acc_ref,
):
    start = pl.program_id(0) * STEP_HEADS

    @pl.when(lax.rem(start, HALF_HEADS) == 0)
    def _():
        acc_ref[...] = gk_in_ref[...]

    keys, last = k_ref[...], last_ref[...]
    total = jnp.zeros_like(acc_ref)
    for head, n, lanes in step_heads():
        first, second = factors(own_lanes(keys, head), pick_ref, 0, last)
        state, norm = widen(state_ref[n])
        values = gv_in_ref[:, lanes] + mul(first * second, state)
        gv_ref[:, lanes] = values.astype(jnp.bfloat16)
        grad_phi = mul(v_ref[:, lanes], state, "nt") + norm.astype(jnp.float32)
        grad_phi = (grad_phi * last).astype(jnp.bfloat16)
        total = total + chain(grad_phi, first, second, back_ref, 0, head)
    acc_ref[...] += total

    @pl.when(lax.rem(start + STEP_HEADS, HALF_HEADS) == 0)
    def _():
        gk_ref[...] = (acc_ref[...] * FEAT**-0.25).astype(jnp.bfloat16)


def specs(rows):
    return dict(
        pair=pl.BlockSpec((rows, 128), lambda h: (0, h * STEP_HEADS // HALF_HEADS)),
        head=pl.BlockSpec((rows, STEP_HEADS * HEAD_V), lambda h: (0, h)),
        state=pl.BlockSpec((STEP_HEADS, STATE, HEAD_V), lambda h: (h, 0, 0)),
        pick=pl.BlockSpec((3, WIDE, WIDE), lambda h: (0, 0, 0)),
        back=pl.BlockSpec((2, 128, 2 * WIDE), lambda h: (0, 0, 0)),
        column=pl.BlockSpec((rows, 1), lambda h: (0, 0)),
        row=pl.BlockSpec((8, rows), lambda h: (0, 0)),
    )


def heads_call(kernel, rows, ins, outs, scratch=(), name=None):
    table = specs(rows)
    shapes = {
        "pair": (rows, HEADS * FEAT),
        "head": (rows, HEADS * HEAD_V),
        "state": (HEADS, STATE, HEAD_V),
    }
    return pl.pallas_call(
        kernel,
        grid=(HEADS // STEP_HEADS,),
        in_specs=[table[kind] for kind in ins],
        out_specs=[table[kind] for kind, _ in outs],
        out_shape=[jax.ShapeDtypeStruct(shapes[kind], kept) for kind, kept in outs],
        scratch_shapes=list(scratch),
        compiler_params=pltpu.CompilerParams(
            dimension_semantics=("arbitrary",), vmem_limit_bytes=48 * 2**20
        ),
        cost_estimate=pl.CostEstimate(flops=2**20, bytes_accessed=2**16, transcendentals=0),
        name=name,
    )


f32, bf = jnp.float32, jnp.bfloat16


def mix_state(k, v, tables, last):
    rows = k.shape[0]
    return heads_call(state_kernel, rows, ["pair", "head", "pick", "column"],
        [("state", bf)], name="mix_state")(k, v, tables[0], last)[0]


def mix_local(q, k, v, seg_col, seg_row):
    rows = k.shape[0]
    return heads_call(local_kernel, rows, ["pair", "pair", "head", "column", "row"],
        [("head", f32), ("head", f32)], [pltpu.VMEM((rows, rows), bf)], name="mix_local")(q, k, v, seg_col, seg_row)


def mix_prefix(q, num, den, state, tables, reading):
    rows = q.shape[0]
    return heads_call(prefix_kernel, rows, ["pair", "head", "head", "state", "pick", "column"],
        [("head", bf), ("head", f32)], name="mix_prefix")(q, num, den, state, tables[0], reading)


def mix_state_grad(q, g, att, inverse, tables, reading):
    rows = q.shape[0]
    return heads_call(state_grad_kernel, rows, ["pair", "head", "head", "head", "pick", "column"],
        [("state", bf)], name="mix_state_grad")(q, g, att, inverse, tables[0], reading)[0]


def mix_local_grad(q, k, v, g, att, inverse, state, tables, reading, seg_col, seg_row):
    rows = q.shape[0]
    return heads_call(local_grad_kernel, rows,
        ["pair", "pair", "head", "head", "head", "head", "state", "pick", "back", "column", "column", "row"],
        [("pair", bf), ("pair", f32), ("head", f32)],
        [pltpu.VMEM((rows, rows), bf), pltpu.VMEM((rows, 128), f32)], name="mix_local_grad")(
        q, k, v, g, att, inverse, state, *tables, reading, seg_col, seg_row)


def mix_later_grad(k, v, gk, gv, state, tables, last):
    rows = k.shape[0]
    return heads_call(later_grad_kernel, rows,
        ["pair", "head", "pair", "head", "state", "pick", "back", "column"],
        [("pair", bf), ("head", bf)], [pltpu.VMEM((rows, 128), f32)], name="mix_later_grad")(
        k, v, gk, gv, state, *tables, last)


from jax.sharding import PartitionSpec as P

D = 2048
EPSILON = 1e-05
LIMIT = 58 * 2**20
TILE = 352


def cost(flops, moved):
    return pl.CostEstimate(flops=flops, bytes_accessed=moved, transcendentals=0)


def whole(*shape):
    return pl.BlockSpec(shape, lambda *_: (0,) * len(shape), pipeline_mode=pl.Buffered(1))


def tiling(parts, rows):
    if parts == 1:
        taken = TILE if rows % TILE == 0 else rows
        return 1, taken, rows // taken
    taken = max(1, TILE // rows)
    taken = taken if parts % taken == 0 else parts
    return taken, rows, parts // taken


def gate_kernel(x_ref, c_ref, *refs):
    count = len(refs) // 3
    half = x_ref.shape[0] // 2
    for n in range(count):
        both_ref, down_ref, out_ref = refs[2 * n], refs[2 * n + 1], refs[2 * count + n]
        parts, _, rows, _ = both_ref.shape
        gate_w, up_w = [both_ref[:, k].reshape(parts * rows, D) for k in range(2)]
        down_w = down_ref[:, 0].reshape(parts * rows, D)
        for at in (slice(0, half), slice(half, 2 * half)):
            x, c = x_ref[at, :], c_ref[at, :]
            gate = mul(gate_w, x, "nt")
            up = mul(up_w, x, "nt")
            grad = mul(down_w, c, "nt").astype(bf).astype(f32)
            sig = 1.0 / (1.0 + jnp.exp(-gate))
            act = gate * sig
            out_ref[0, :, at] = (grad * up * sig * (1.0 + gate * (1.0 - sig))).astype(bf)
            out_ref[1, :, at] = (grad * act).astype(bf)
            out_ref[2, :, at] = (act * up).astype(bf)


def ffn_gates(x, c, weights):
    rows, count = x.shape[0], len(weights)
    hidden = weights[0][1].shape[0] * weights[0][1].shape[2]
    ins, outs = [whole(rows, D)] * 2, []
    for pair in weights:
        for w in pair:
            taken, height, steps = tiling(w.shape[0], w.shape[2])
            at = (lambda i: (0, 0, i, 0)) if w.shape[0] == 1 else (lambda i: (i, 0, 0, 0))
            ins.append(pl.BlockSpec((taken, w.shape[1], height, D), at))
        outs.append(pl.BlockSpec((3, taken * height, rows), lambda i: (0, i, 0)))
    return pl.pallas_call(
        gate_kernel,
        grid=(steps,),
        in_specs=ins,
        out_specs=outs,
        out_shape=[jax.ShapeDtypeStruct((3, hidden, rows), bf)] * count,
        compiler_params=pltpu.CompilerParams(vmem_limit_bytes=LIMIT),
        cost_estimate=cost(
            6 * rows * D * hidden * count,
            2 * (2 * rows * D + 3 * count * hidden * (D + rows)),
        ),
        name="ffn_gates",
    )(x, c, *[w for pair in weights for w in pair])


def back_kernel(count, *refs):
    made, weights, out_ref, turned = (
        refs[:count], refs[count : 2 * count], refs[-count - 1], refs[-count:]
    )
    added = refs[2 * count : -count - 1]

    @pl.when(pl.program_id(0) == 0)
    def _():
        for block, kept in zip(made, turned):
            kinds, hidden, rows = block.shape
            kept[...] = block[...].reshape(kinds * hidden, rows).T

    total = None
    for kept, w_ref in zip(turned, weights):
        parts, kinds, rows, columns = w_ref.shape
        right = jnp.concatenate(
            [w_ref[:, k].reshape(parts * rows, columns) for k in range(kinds)], axis=0
        )
        part = mul(kept[...], right)
        total = part if total is None else total + part
    for more in added:
        total = total + more[...].astype(f32)
    out_ref[...] = total.astype(out_ref.dtype)


def ffn_back(made, weights, which, added=(), columns=512):
    count = len(weights)
    weights = [pair[which] for pair in weights]
    kinds = weights[0].shape[1]
    _, hidden, rows = made[0].shape
    out = pl.BlockSpec((rows, columns), lambda j: (0, j))
    ins = [
        pl.BlockSpec(
            (kinds, hidden, rows), lambda j: (2 * which // kinds, 0, 0), pipeline_mode=pl.Buffered(1)
        )
    ] * count
    for w in weights:
        ins.append(pl.BlockSpec((w.shape[0], kinds, w.shape[2], columns), lambda j: (0, 0, 0, j)))
    ins += [out] * len(added)
    return pl.pallas_call(
        functools.partial(back_kernel, count),
        grid=(D // columns,),
        in_specs=ins,
        out_specs=out,
        out_shape=jax.ShapeDtypeStruct((rows, D), bf),
        scratch_shapes=[pltpu.VMEM((rows, kinds * hidden), bf)] * count,
        compiler_params=pltpu.CompilerParams(vmem_limit_bytes=LIMIT),
        cost_estimate=cost(
            2 * rows * D * hidden * kinds * count,
            2 * (count * kinds * hidden * (D + rows) + rows * D),
        ),
        name="ffn_back",
    )(*made, *weights, *added)


def grad_kernel(blocks, *refs):
    made, xs, cs = refs[:blocks], refs[blocks : 2 * blocks], refs[2 * blocks : 3 * blocks]
    added, out_ref = refs[3 * blocks : -1], refs[-1]
    parts, _, rows, _ = out_ref.shape

    def write(rights):
        total = None
        for left, right in zip(made, rights):
            part = mul(left[0], right[...])
            total = part if total is None else total + part
        for more in added:
            total = total + more[...].reshape(parts * rows, D).astype(f32)
        out_ref[...] = total.astype(bf).reshape(parts, 1, rows, D)

    kind = pl.program_id(0)

    @pl.when(kind < 2)
    def _():
        write(xs)

    @pl.when(kind == 2)
    def _():
        write(cs)


def ffn_grad(made, xs, cs, parts, height, added=None):
    blocks = len(made)
    rows = xs[0].shape[0]
    hidden = made[0].shape[1]
    taken, rise, steps = tiling(parts, height)
    left = pl.BlockSpec((1, taken * rise, rows), lambda k, i: (k, i, 0))
    at = (lambda k, i: (0, k, i, 0)) if parts == 1 else (lambda k, i: (i, k, 0, 0))
    out = pl.BlockSpec((taken, 1, rise, D), at)
    more = [] if added is None else [added]
    return pl.pallas_call(
        functools.partial(grad_kernel, blocks),
        grid=(3, steps),
        in_specs=[left] * blocks + [whole(rows, D)] * (2 * blocks) + [out] * len(more),
        out_specs=out,
        out_shape=jax.ShapeDtypeStruct((parts, 3, height, D), bf),
        compiler_params=pltpu.CompilerParams(vmem_limit_bytes=LIMIT),
        cost_estimate=cost(
            6 * rows * D * hidden * blocks,
            2 * (2 * blocks * rows * D + 3 * hidden * (rows * blocks + D * (1 + len(more)))),
        ),
        name="ffn_grad",
    )(*made, *xs, *cs, *more)


def widen_kernel(sum_ref, *out_refs):
    for kind, out_ref in enumerate(out_refs):
        out_ref[...] = sum_ref[0, kind].astype(f32)


def widened(sums):
    parts, _, height, _ = sums.shape
    return pl.pallas_call(
        widen_kernel,
        grid=(parts,),
        in_specs=[pl.BlockSpec((1, 3, height, D), lambda i: (i, 0, 0, 0))],
        out_specs=[pl.BlockSpec((height, D), lambda i: (i, 0))] * 3,
        out_shape=[jax.ShapeDtypeStruct((parts * height, D), f32)] * 3,
        compiler_params=pltpu.CompilerParams(vmem_limit_bytes=LIMIT),
        cost_estimate=cost(0, 6 * parts * 3 * height * D),
        name="widened",
    )(sums)


def qkv_grad_kernel(n_ref, gq_ref, gk_ref, gv_ref, out_ref):
    turned = n_ref[...].T
    qk = gq_ref.shape[1]
    out_ref[:, :qk] = mul(turned, gq_ref[...]).astype(bf)
    out_ref[:, qk : 2 * qk] = mul(turned, gk_ref[...]).astype(bf)
    out_ref[:, 2 * qk :] = mul(turned, gv_ref[...]).astype(bf)


def qkv_grad(normed, gq, gk, gv):
    rows, qk = gq.shape
    columns = 2 * qk + D
    tile = 256
    return pl.pallas_call(
        qkv_grad_kernel,
        grid=(D // tile,),
        in_specs=[
            pl.BlockSpec((rows, tile), lambda i: (0, i)), whole(rows, qk), whole(rows, qk), whole(rows, D)
        ],
        out_specs=pl.BlockSpec((tile, columns), lambda i: (i, 0)),
        out_shape=jax.ShapeDtypeStruct((D, columns), bf),
        compiler_params=pltpu.CompilerParams(vmem_limit_bytes=LIMIT),
        cost_estimate=cost(2 * rows * D * columns, 2 * (rows * (D + columns) + D * columns)),
        name="qkv_grad",
    )(normed, gq, gk, gv)


def norm_forward(inputs):
    inverse = lax.rsqrt(jnp.mean(inputs * inputs, axis=-1, keepdims=True) + EPSILON)
    return (inputs * inverse, inverse)


def norm_backward(grad_normed, unit_rows, inverse, gain_vec):
    gain_grad = jnp.sum(grad_normed * unit_rows, axis=0)
    grad_unit = grad_normed * gain_vec
    return (
        inverse * (grad_unit - unit_rows * jnp.mean(grad_unit * unit_rows, axis=-1, keepdims=True)),
        gain_grad,
    )


def move(array, target, axis="mp"):
    size = lax.axis_size(axis)
    pairs = [(m, target(m)) for m in range(size)]
    return lax.ppermute(array, axis, [(m, t) for m, t in pairs if t is not None])


def then(value, *before):
    return lax.optimization_barrier((value, before))[0]


def beside(array, mover, *works):
    ends = [array.shape[0] * n // len(works) // 16 * 16 for n in range(len(works))] + [array.shape[0]]
    moved, made = [], []
    for n, work in enumerate(works):
        share = array[ends[n] : ends[n + 1]]
        if made:
            share = then(share, made[-1])
        result = work(share, made)
        arrived, result = lax.optimization_barrier((mover(share), result))
        moved.append(arrived)
        made.append(result)
    return jnp.concatenate(moved, axis=0), made


def to_mate(array):
    return move(array, lambda m: m ^ 1)


def to_half(array):
    size = lax.axis_size("mp")
    return move(array, lambda m: (m + size // 2) % size)


def to_peer(array, step):
    half = lax.axis_size("mp") // 2

    def target(m):
        low = m % half
        return m - low + (low + 2 * step) % half

    return move(array, target)


def to_chip(array, step):
    size = lax.axis_size("mp")
    return move(array, lambda m: m + 2 * step if 0 <= m + 2 * step < size else None)


def sums_before(own, sign, *beside, made=None):
    core = lax.axis_index("mp") % 2
    chips = lax.axis_size("mp") // 2
    wire = own.astype(bf)
    mate = to_mate(wire).astype(f32)
    half = own.shape[0] // 2
    both = wire.astype(f32) + mate
    running = lax.dynamic_slice_in_dim(both, core * half, half, 0)
    before = jnp.zeros_like(running)
    step, beside, made = 1, list(beside), [] if made is None else made
    while step < chips:
        came = to_chip(running.astype(bf), sign * step)
        if beside:
            came, result = lax.optimization_barrier((came, beside.pop(0)(running)))
            made.append(result)
        came = came.astype(f32)
        before = before + came
        running = running + came
        step *= 2
    before = before.astype(bf)
    other = to_mate(before)
    first = jnp.where(core == 0, before, other)
    second = jnp.where(core == 0, other, before)
    total = jnp.concatenate([first, second], axis=0).astype(f32)
    inner = core == (1 if sign > 0 else 0)
    return (total + jnp.where(inner, mate, 0.0)).astype(bf), made


def pick(array, index, dim=0):
    return lax.dynamic_index_in_dim(array, index, dim, keepdims=False)


def chip_halves(array):
    groups, size = lax.axis_size("dp"), lax.axis_size("mp")
    core = lax.axis_index("mp") % 2
    rows, columns = array.shape[0] // (groups * size), array.shape[1]
    blocks = array.reshape(groups, size // 2, 2, rows, columns)
    return pick(blocks, core, 2), pick(blocks, 1 - core, 2)


def add(first, *more, kept=bf):
    total = first.astype(f32)
    for array in more:
        total = total + array.astype(f32)
    return total.astype(kept)


def placed(shares, places):
    out = jnp.zeros((len(shares),) + shares[0].shape, shares[0].dtype)
    for share, at in zip(shares, places):
        out = lax.dynamic_update_index_in_dim(out, share, at, 0)
    return out


def chip_shares(array):
    steps = range(1, lax.axis_size("mp") // 2)
    return [move(array, lambda m: m ^ (2 * step)) for step in steps]


def by_chip(array, shares):
    chip = lax.axis_index("mp") // 2
    return placed([array] + shares, [chip ^ step for step in range(len(shares) + 1)])


def first_groups(array):
    return [move(array, lambda m: m ^ step, "dp") for step in (1, 2)]


def third_group(first, second):
    half = first.shape[0] // 2
    return [
        move(second[:half], lambda m: m ^ 1, "dp"),
        move(first[half:], lambda m: m ^ 2, "dp"),
    ]


def assembled(pieces, groups, chips, out=None):
    group, core = lax.axis_index("dp"), lax.axis_index("mp") % 2
    shape = pieces[0][2].shape[1:]
    if out is None:
        out = jnp.zeros((groups, chips, 2) + shape, bf)
    for step, at, own, other in pieces:
        both = jnp.where(core == 0, jnp.stack([own, other], 1), jnp.stack([other, own], 1))
        start = (group ^ step, at) + (0,) * (len(shape) + 1)
        out = lax.dynamic_update_slice(out, both[None], start)
    return out


def group_move(array, step):
    return move(pick(array, lax.axis_index("dp") ^ step), lambda m: m ^ step, "dp")


def chip_moves(array):
    chip = lax.axis_index("mp") // 2
    return [
        move(pick(array, chip ^ step), lambda m: m ^ (2 * step))
        for step in range(1, lax.axis_size("mp") // 2)
    ]


def sum_everywhere(array):
    for axis in ("mp", "dp"):
        step = 1
        while step < lax.axis_size(axis):
            array = array + move(array, lambda m: m ^ step, axis)
            step *= 2
    return array


def body(
    x_in,
    seq_lengths,
    norm1_gain,
    w_query,
    w_key,
    w_value,
    w_out,
    norm2_gain,
    w_gate,
    w_up,
    w_down,
    cotangent,
):
    rows = x_in.shape[0]
    groups = lax.axis_size("dp")
    size = lax.axis_size("mp")
    peers = size // 4
    hidden = w_gate.shape[1]
    piece = hidden // groups
    place = lax.axis_index("mp")
    group = lax.axis_index("dp")
    everywhere = ("dp", "mp")
    qk = w_query.shape[1]
    aligned = piece % 16 == 0

    own_rows = w_query.shape[0]
    gain_block = jnp.concatenate(
        [norm1_gain[:, None], norm2_gain[:, None], jnp.zeros((own_rows, 126), bf)], axis=1
    )
    packed = jnp.concatenate([w_query, w_key, w_value, gain_block], axis=1)
    in_chips, packed = lax.optimization_barrier((chip_shares(packed), packed))
    in_chips = by_chip(packed, in_chips)

    full_out = lax.all_gather(w_out, everywhere, axis=0, tiled=True)
    half_chips = size // 4
    mine_both = jnp.concatenate(then([w_gate.T, w_up.T], in_chips), axis=0)
    mine = (mine_both.reshape(1, 2, hidden, D), then(w_down, in_chips).reshape(1, 1, hidden, D))
    far_down = lax.dynamic_slice_in_dim(mine[1][0, 0], group * piece, piece, 0)
    far_both = lax.dynamic_slice_in_dim(mine[0][0], group * piece, piece, 1).reshape(2 * piece, D)
    cot_ends = [rows * n // 16 for n in (0, 3, 6, 10, 13, 16)]
    cot_shares = [cotangent[a:b] for a, b in zip(cot_ends, cot_ends[1:])]

    def peers_of(array):
        return [to_peer(array, step) for step in range(1, peers)]

    def beside_one(array, mover, work):
        return lax.optimization_barrier((mover(array), work(array)))

    both_cut, down_cut = 2 * piece * 8 // 11, piece * 7 // 11
    blank = jnp.zeros((groups, size // 2, 2) + packed.shape, bf)
    blank, in_near, in_mate, both_first = lax.optimization_barrier(
        (
            blank,
            first_groups(in_chips),
            to_mate(in_chips),
            to_half(then(far_both[:both_cut], in_chips)),
        )
    )
    full_in, in_third, in_mates, both_second = lax.optimization_barrier(
        (
            assembled([(0, 0, in_chips, in_mate)], groups, size // 2, blank),
            third_group(*in_near),
            [to_mate(share) for share in in_near],
            to_half(then(far_both[both_cut:], in_near)),
        )
    )
    in_mates = [*in_mates] + [to_mate(share) for share in in_third]
    far_both = jnp.concatenate([both_first, both_second], axis=0)
    far_both = lax.all_gather(far_both, "dp", axis=0, tiled=True).reshape(groups, 2, piece, D)
    down_first = to_half(then(far_down[:down_cut], in_third))
    mate_down = to_mate(then(mine[1], in_third))
    cot_third = peers_of(then(cot_shares[2], in_third))
    in_pieces = [
        (step, at, own, other)
        for (step, at, own), other in zip(
            (
                (1, 0, in_near[0]),
                (2, 0, in_near[1]),
                (3, 0, in_third[0]),
                (3, half_chips, in_third[1]),
            ),
            in_mates,
        )
    ]
    full_in = assembled(in_pieces, groups, size // 2, full_in).reshape(D, packed.shape[1])

    row_start = place * rows
    seq_ends = jnp.cumsum(seq_lengths[0], dtype=jnp.int32)
    positions = row_start + jnp.arange(rows, dtype=jnp.int32)
    segments = jnp.sum((positions[:, None] >= seq_ends[None, :]).astype(jnp.int32), axis=1)
    seg_before = jnp.sum((row_start - 1 >= seq_ends).astype(jnp.int32))
    reading = ((segments == seg_before) & (row_start > 0)).astype(f32)[:, None]
    last_doc = (segments == segments[-1]).astype(f32)[:, None]
    seg_col = segments[:, None]
    seg_row = jnp.broadcast_to(segments[None, :], (8, rows))
    tables = feature_tables()

    inputs = x_in.astype(f32)
    inverse_one = norm_forward(inputs)[1]
    early = (full_out, mine, down_first, mate_down, cot_third, inverse_one, reading, last_doc, seg_col, seg_row)
    full_in, early = lax.optimization_barrier((full_in, early))
    full_out, mine, down_first, mate_down, cot_third, inverse_one, reading, last_doc, seg_col, seg_row = early
    gain_one = full_in[:, 2 * qk + D].astype(f32)
    gain_two = full_in[:, 2 * qk + D + 1].astype(f32)
    full_qkv = full_in[:, : 2 * qk + D]
    unit_one = inputs * inverse_one
    normed_one = (unit_one * gain_one).astype(bf)
    (got, mate_gate, down_second), qkv = beside_one(
        then(cot_shares[3], full_in),
        lambda ready: (
            peers_of(ready),
            to_mate(then(w_gate.T, ready)).reshape(1, 1, hidden, D),
            to_half(then(far_down[down_cut:], ready)),
        ),
        lambda ready: mul(then(normed_one, ready), full_qkv).astype(bf),
    )
    cot_got = [cot_third, got]
    queries, keys, values = qkv[:, :qk], qkv[:, qk : 2 * qk], qkv[:, 2 * qk :]
    far_down = jnp.concatenate([down_first, down_second], axis=0)
    far_down = lax.all_gather(far_down, "dp", axis=0, tiled=True).reshape(groups, 1, piece, D)
    (got, mate_up), own_state = beside_one(
        then(cot_shares[4], qkv),
        lambda ready: (peers_of(ready), to_mate(then(w_up.T, ready)).reshape(1, 1, hidden, D)),
        lambda ready: mix_state(then(keys, ready), values, tables, last_doc),
    )
    cot_got.append(got)

    def local_work(ready):
        local = mix_local(then(queries, ready), keys, values, seg_col, seg_row)
        return local

    def pack_work(ready):
        gate, up = then((mate_gate, mate_up), ready)
        return jnp.concatenate([gate, up], axis=1)

    prefix, [(num, den), mate_both] = sums_before(own_state, 1, local_work, pack_work)
    cot_first, (attended, inverse_den) = beside_one(
        then(cot_shares[0], prefix),
        peers_of,
        lambda ready: mix_prefix(then(queries, ready), num, den, prefix, tables, reading),
    )
    mate = (mate_both, mate_down)
    near = [mine, mate]
    cot_second, hidden_in = beside_one(
        then(cot_shares[1], attended),
        peers_of,
        lambda ready: inputs + mul(then(attended, ready), full_out),
    )
    cot_got = [cot_first, cot_second] + cot_got
    unit_two, inverse_two = norm_forward(hidden_in)
    normed_two = (unit_two * gain_two).astype(bf)
    came = [to_peer(normed_two, step) for step in range(1, peers)]

    near_own = ffn_gates(normed_two, cotangent, near)
    far_mine = then((far_both, far_down), normed_two)
    if not aligned:
        far_mine = tuple(jnp.swapaxes(w, 0, 1).reshape(1, -1, hidden, D) for w in far_mine)
    far_mate = then(tuple(to_mate(w) for w in far_mine), near_own)
    far = [tuple(far_mine), far_mate]
    weights = near + far
    shape = (groups, piece) if aligned else (1, hidden)
    far_own = ffn_gates(normed_two, cotangent, far)
    made_own = list(near_own) + list(far_own)
    grad_own = ffn_back(made_own, weights, 0)
    normed = [normed_two] + then(came, grad_own)
    cot_got = then(cot_got, near_own)
    cots = [cotangent] + [jnp.concatenate(parts, axis=0) for parts in zip(*cot_got)]
    near_made = [near_own] + [ffn_gates(x, c, near) for x, c in zip(normed[1:], cots[1:])]
    far_made = [far_own] + [
        ffn_gates(x, c, then(far, near_made)) for x, c in zip(normed[1:], cots[1:])
    ]
    made = [list(a) + list(b) for a, b in zip(near_made, far_made)]

    def weight_grads(made, ready, added=None):
        return ffn_grad(then(made, ready), normed, cots, *shape, added)

    def over_groups(grad):
        if not aligned:
            grad = jnp.swapaxes(grad.reshape(3, groups, piece, D), 0, 1)
        return lax.psum_scatter(
            grad.reshape(groups * 3 * piece, D), "dp", scatter_dimension=0, tiled=True
        )

    def back(block, which, ready):
        return ffn_back(then(block, ready), weights, which)

    far_given = weight_grads([block[1] for block in far_made], far_made)
    far_sent = to_mate(far_given)
    grad_parts = [back(block, 0, far_given) for block in made[1:]]

    def owners(parts):
        return [to_peer(part, peers - step) for step, part in enumerate(parts, 1)]

    def stacked(parts):
        return jnp.concatenate([part[:, None] for part in parts], axis=1)

    def to_owners(parts):
        return stacked(owners([parts[:, n] for n in range(peers - 1)]))

    def near_work(ready, _):
        given = weight_grads([block[1] for block in near_made], ready)
        return given

    def far_work(ready, done):
        kept = weight_grads([block[0] for block in far_made], ready, far_sent)
        return kept, to_mate(then(done[0], ready))

    def last_work(ready, done):
        return weight_grads([block[0] for block in near_made], ready, done[1][1])

    grad_sent, (_, (far_kept, _), near_kept) = beside(
        stacked(grad_parts), to_owners, near_work, far_work, last_work
    )
    far_part = over_groups(far_kept)
    near_part = over_groups(near_kept)
    grad_normed_two = jnp.sum(grad_sent.astype(f32), axis=1) + grad_own.astype(f32)

    grad_two, gain_two_grad = norm_backward(grad_normed_two, unit_two, inverse_two, gain_two)
    grad_hidden_in = cotangent.astype(f32) + grad_two
    grad_branch = grad_hidden_in.astype(bf)
    grad_attended = mul(grad_branch, full_out, "nt").astype(bf)
    state_grad = mix_state_grad(queries, grad_attended, attended, inverse_den, tables, reading)

    def local_grads(ready):
        local = mix_local_grad(
            then(queries, ready), keys, values, grad_attended, attended, inverse_den, prefix, tables,
            reading, seg_col, seg_row,
        )
        return local, to_mate(then(out_halves[1], ready))

    out_halves = []

    def out_work(ready):
        halves = chip_halves(mul(then(attended, ready), grad_branch, "tn").astype(bf))
        out_halves.extend(halves)
        return halves

    later, [_, (local, out_came)] = sums_before(state_grad, -1, out_work, local_grads)
    grad_queries, part_keys, part_values = local
    out_kept = add(out_halves[0], out_came)
    out_kept, far_part = then((out_kept, far_part), later)
    ends = [far_part.shape[0] * n // 33 for n in (0, 6, 13, 17, 23, 33)]
    far_shares = [far_part[a:b] for a, b in zip(ends, ends[1:])]
    out_first, out_second, out_diag = [pick(out_kept, group ^ step) for step in range(1, groups)]
    low, high = slice(None, half_chips), slice(half_chips, None)

    def by_first(block):
        return move(block, lambda m: m ^ 1, "dp")

    def by_second(block):
        return move(block, lambda m: m ^ 2, "dp")

    (far_first, for_second, for_first), (grad_keys, grad_values) = beside_one(
        then(far_shares[0], out_kept),
        lambda ready: (
            to_half(ready), by_first(then(out_diag[low], ready)), by_second(then(out_diag[high], ready))
        ),
        lambda ready: mix_later_grad(
            then(keys, ready), values, part_keys, part_values, later, tables, last_doc
        ),
    )
    out_second = [add(out_second[low], for_second), out_second[high]]
    out_first = [out_first[low], add(out_first[high], for_first)]
    (out_low, far_slot), in_grad = beside_one(
        then((out_first[0], out_second[0]), grad_keys),
        lambda ready: (
            [by_first(ready[0]), by_second(ready[1])], to_half(then(far_shares[1], ready))
        ),
        lambda ready: qkv_grad(then(normed_one, ready), grad_queries, grad_keys, grad_values),
    )
    in_keep, in_give = chip_halves(in_grad)
    out_parts = [back(block, 1, in_grad) for block in made[1:]]
    out_parts, in_came, out_high, far_second = lax.optimization_barrier(
        (
            out_parts,
            to_mate(in_give),
            [by_first(then(out_first[1], in_grad)), by_second(then(out_second[1], in_grad))],
            to_half(then(far_shares[2], in_grad)),
        )
    )
    in_diag = add(pick(in_keep, group ^ 3), pick(in_came, group ^ 3))
    in_first, in_second = [
        add(pick(in_keep, group ^ step), pick(in_came, group ^ step)) for step in (1, 2)
    ]
    grad_queries, grad_keys, grad_values = then(
        (grad_queries, grad_keys, grad_values), (in_diag, in_first, in_second)
    )
    grad_normed_one = (
        mul(grad_queries, full_qkv[:, :qk], "nt")
        + mul(grad_keys, full_qkv[:, qk : 2 * qk], "nt")
        + mul(grad_values, full_qkv[:, 2 * qk :], "nt")
    )
    out_split = jnp.split(
        stacked(out_parts), [rows * 3 // 16, rows * 13 // 32], axis=0
    )
    out_early, for_second, for_first, far_third, grad_normed_one, in_first, in_second = (
        lax.optimization_barrier(
            (
                to_owners(then(out_split[0], in_diag)),
                by_first(in_diag[low]),
                by_second(in_diag[high]),
                to_half(then(far_shares[3], in_diag)),
                grad_normed_one,
                in_first,
                in_second,
            )
        )
    )
    in_first = jnp.concatenate([in_first[low], add(in_first[high], for_first)], axis=0)
    in_second = jnp.concatenate([add(in_second[low], for_second), in_second[high]], axis=0)
    in_moved = [by_first(in_first), by_second(in_second)]
    far_last = to_half(then(far_shares[4], in_first))
    grad_normed_one = then(grad_normed_one, (in_first, in_second))
    grad_one, gain_one_grad = norm_backward(grad_normed_one, unit_one, inverse_one, gain_one)
    input_grad = (grad_hidden_in + grad_one).astype(bf)
    out_middle = to_owners(then(out_split[1], (in_first, in_second)))
    out_middle, input_grad, gain_one_grad, in_moved, far_last = lax.optimization_barrier(
        (out_middle, input_grad, gain_one_grad, in_moved, far_last)
    )
    out_own = back(made[0], 1, in_moved)
    far_sum = jnp.concatenate([far_first, far_slot, far_second, far_third, far_last], axis=0)
    ffn_sum = lax.all_gather(add(near_part, far_sum), "dp", axis=0, tiled=True)
    ffn_sum = ffn_sum.reshape(groups, 3, piece, D)
    chip = place // 2

    def over_chips(blocks, kept):
        shares = [
            add(*[pick(block, chip ^ step) for block in blocks]) for step in range(1, size // 2)
        ]
        moved = [move(share, lambda m: m ^ (2 * step)) for step, share in enumerate(shares, 1)]
        return add(*[pick(block, chip) for block in blocks], *moved, kept=kept)

    in_sum = over_chips([pick(in_keep, group), pick(in_came, group), *in_moved], f32)
    out_blocks = [jnp.concatenate(pair, axis=0) for pair in zip(out_low, out_high)]
    out_blocks = then([pick(out_kept, group), *out_blocks], in_moved)
    out_sum = over_chips(out_blocks, f32)
    if not aligned:
        ffn_sum = jnp.swapaxes(ffn_sum, 0, 1).reshape(1, 3, hidden, D)
    gate_grad, up_grad, down_grad = widened(ffn_sum)
    gain_sums = sum_everywhere(jnp.stack([gain_one_grad, gain_two_grad]))
    gain_sums = lax.dynamic_slice_in_dim(
        gain_sums, (group * size + place) * own_rows, own_rows, 1
    )
    out_last = to_owners(then(out_split[2], in_sum, gain_sums))
    out_sent = jnp.concatenate([out_early, out_middle, out_last], axis=0)
    output = (hidden_in + jnp.sum(out_sent.astype(f32), axis=1) + out_own.astype(f32)).astype(bf)
    return (
        output,
        input_grad,
        gain_sums[0],
        in_sum[:, :qk],
        in_sum[:, qk : 2 * qk],
        in_sum[:, 2 * qk :],
        out_sum,
        gain_sums[1],
        gate_grad.T,
        up_grad.T,
        down_grad,
    )


def solution(mesh):
    rows, vector = P(("dp", "mp"), None), P(("dp", "mp"))
    columns, down = P(None, "mp"), P("mp", None)
    return jax.shard_map(
        body,
        mesh=mesh,
        in_specs=(rows, P("dp", None), vector, rows, rows, rows, rows, vector, columns, columns, down, rows),
        out_specs=(rows, rows, vector, rows, rows, rows, rows, vector, columns, columns, down),
        check_vma=False,
    )
```
